32 devices in a mesh: tm: 8 (over z, y), col: 4 (over x, core).
Axes of the slice: x: 2, y: 2, z: 4, core: 2. Of those that a mesh axis runs over, the one named last changes fastest.
Arguments:
- frames: bfloat16 [24, 2, 96, 384], P('tm', None, 'col'), may hold values from -6 to 6
- up_kernel: bfloat16 [10368, 256], P(None, 'tm'), may hold values from -0.109375 to 0.109375
- mix_kernel: bfloat16 [6912, 256], P(None, 'tm'), may hold values from -0.078125 to 0.078125
- cotangent: bfloat16 [48, 2, 96, 256], P('tm', None, 'col'), may hold values from -6 to 6
Outputs:
- decoded: bfloat16 [48, 2, 96, 256], P('tm', None, 'col')
- frames_grad: bfloat16 [24, 2, 96, 384], P('tm', None, 'col')
The draws below stay inside these ranges and needn't reach their ends.
All inputs are finite; a program needn't handle non-finite values.
Results may differ from the reference program's by a relative error of at most 0.005.
Values may be sent and summed in bfloat16 or wider, within the bound.
A program may use at most 64 MiB of HBM per device.

```python
import jax
import jax.numpy as jnp
from jax import lax

CI = 384
C = 256
H = 2
FRAMES_IN = 24
COLUMNS = 96


def block_levels(stream_key, shape, cuts, low, top_value):
    level = 1.0
    for dim, blocks in cuts:
        steps = jax.random.uniform(jax.random.fold_in(jax.random.fold_in(stream_key, 6), dim), (blocks,), jnp.float32, low / len(cuts), top_value / len(cuts))
        level = level * jnp.repeat(jnp.exp(steps), shape[dim] // blocks).reshape((-1,) + (1,) * (len(shape) - 1 - dim))
    return level


def gaussian(key, shape, scale, limit, split=(), held_as=jnp.bfloat16):
    entries = scale * jax.random.normal(key, shape, jnp.float32)
    if split:
        entries = entries * block_levels(key, shape, split, -0.22, 0.18)
    return jnp.clip(entries, -limit, limit).astype(held_as)


def setup_inputs(seed: int = 0) -> dict:
    key_of = jax.random.split(jax.random.key(seed), 5)
    return {
        "frames": gaussian(key_of[0], (FRAMES_IN, H, COLUMNS, CI), 1.0, 6.0, ((0, 8), (2, 4))),
        "up_kernel": gaussian(key_of[1], (27 * CI, C), (9 * CI) ** -0.5, 0.109375, ((1, 8),)),
        "mix_kernel": gaussian(key_of[2], (27 * C, C), (27 * C) ** -0.5, 0.078125, ((1, 8),)),
        "cotangent": gaussian(key_of[3], (2 * FRAMES_IN, H, COLUMNS, C), 1.0, 6.0, ((0, 8), (2, 4))),
    }


def tap_product(window, matrix):
    return jnp.einsum("thwc,cd->thwd", window, matrix, precision=lax.Precision.HIGHEST)


def reference(frames, up_kernel, mix_kernel, cotangent):
    frame_count = frames.shape[0]
    height = frames.shape[1]
    width = frames.shape[2]
    count = 2 * frame_count
    up_taps = up_kernel.astype(jnp.float32).reshape(3, 3, 3, CI, C)
    mix_taps = mix_kernel.astype(jnp.float32).reshape(3, 3, 3, C, C)
    padded = jnp.pad(frames.astype(jnp.float32), ((0, 0), (1, 1), (1, 1), (0, 0)))
    parts = []
    for tap_t in range(3):
        total = jnp.zeros((frame_count, height, width, C), jnp.float32)
        for tap_h in range(3):
            for tap_w in range(3):
                total = total + tap_product(padded[:, tap_h:tap_h + height, tap_w:tap_w + width], up_taps[tap_t, tap_h, tap_w])
        parts.append(total)
    even = parts[0] + jnp.pad(parts[2], ((1, 0), (0, 0), (0, 0), (0, 0)))[:-1]
    before = jnp.stack((even, parts[1]), axis=1).reshape(count, height, width, C)
    hidden = jax.nn.silu(before).astype(jnp.bfloat16)
    hidden_pad = jnp.pad(hidden.astype(jnp.float32), ((2, 0), (1, 1), (1, 1), (0, 0)))
    cot_pad = jnp.pad(cotangent.astype(jnp.float32), ((0, 2), (1, 1), (1, 1), (0, 0)))
    output = jnp.zeros((count, height, width, C), jnp.float32)
    hidden_grad = jnp.zeros((count, height, width, C), jnp.float32)
    for tap_t in range(3):
        for tap_h in range(3):
            for tap_w in range(3):
                matrix = mix_taps[tap_t, tap_h, tap_w]
                output = output + tap_product(hidden_pad[tap_t:tap_t + count, tap_h:tap_h + height, tap_w:tap_w + width], matrix)
                hidden_grad = hidden_grad + tap_product(cot_pad[2 - tap_t:2 - tap_t + count, 2 - tap_h:2 - tap_h + height, 2 - tap_w:2 - tap_w + width], matrix.T)
    decoded = output.astype(jnp.bfloat16)
    sigma = jax.nn.sigmoid(before)
    before_grad = (hidden_grad * sigma * (1.0 + before * (1.0 - sigma))).astype(jnp.bfloat16)
    pairs = before_grad.astype(jnp.float32).reshape(frame_count, 2, height, width, C)
    evens = pairs[:, 0]
    odds = pairs[:, 1]
    later_evens = jnp.pad(evens, ((0, 1), (0, 0), (0, 0), (0, 0)))[1:]
    sources = (evens, odds, later_evens)
    grad_total = jnp.zeros((frame_count, height, width, CI), jnp.float32)
    for tap_t in range(3):
        source_pad = jnp.pad(sources[tap_t], ((0, 0), (1, 1), (1, 1), (0, 0)))
        for tap_h in range(3):
            for tap_w in range(3):
                grad_total = grad_total + tap_product(source_pad[:, 2 - tap_h:2 - tap_h + height, 2 - tap_w:2 - tap_w + width], up_taps[tap_t, tap_h, tap_w].T)
    return decoded, grad_total.astype(jnp.bfloat16)
```

```python
import functools

import jax
import jax.numpy as jnp
from jax import lax
from jax.experimental import pallas as pl
from jax.experimental.pallas import tpu as pltpu
from jax.sharding import PartitionSpec as P


def with_halo(block, sides, width):
    for axis, dim in sides:
        count = lax.axis_size(axis)
        forward = [(i, i + 1) for i in range(count - 1)]
        backward = [(target, source) for source, target in forward]
        low = lax.ppermute(
            lax.slice_in_dim(block, block.shape[dim] - width, None, axis=dim), axis, forward
        )
        high = lax.ppermute(lax.slice_in_dim(block, 0, width, axis=dim), axis, backward)
        block = jnp.concatenate([low, block, high], axis=dim)
    return block


def from_behind(array, axis, by):
    devices = lax.axis_size(axis)
    pairs = [(i, i + by) for i in range(devices) if 0 <= i + by < devices]
    return lax.ppermute(array, axis, pairs)


def widen(field):
    return with_halo(field, (("col", 2),), 1)


def from_previous(field):
    return from_behind(field, "tm", 1)


def from_next(field):
    return from_behind(field, "tm", -1)


def forward_pass(kernel, produce):
    return produce(lax.all_gather(kernel, "tm", axis=1, tiled=True), jnp.int32(0))


def backward_pass(kernel, combine, initial):
    return combine(initial, lax.all_gather(kernel, "tm", axis=1, tiled=True), jnp.int32(0))


def pad_rows(field):
    return jnp.pad(field, ((0, 0), (1, 1), (0, 0), (0, 0)))


def window(padded, first, count, row_low, col_low, height, width):
    part = padded[first : first + count, row_low : row_low + height, col_low : col_low + width]
    return part.reshape(-1, part.shape[-1])


def transposed(rows, matrix):
    return lax.dot_general(
        rows, matrix, (((1,), (1,)), ((), ())), preferred_element_type=jnp.float32
    )


def shards(frames, up_kernel, mix_kernel, cotangent):
    frame_count, height, width, in_channels = frames.shape
    out_channels = mix_kernel.shape[0] // 27
    count = 2 * frame_count
    block = count * height * width
    widened = widen(frames)
    earlier = from_previous(widened[-1:])
    extended = pad_rows(jnp.concatenate((earlier, widened), axis=0))
    rows_in = extended.shape[0] - 1

    def up_columns(piece, start):
        taps = piece.reshape(3, 3, 3, in_channels, piece.shape[1])
        even = jnp.zeros((rows_in * height * width, piece.shape[1]), jnp.float32)
        odd = even
        for tap_h in range(3):
            for tap_w in range(3):
                current = window(extended, 1, rows_in, tap_h, tap_w, height, width)
                prior = window(extended, 0, rows_in, tap_h, tap_w, height, width)
                even = even + jnp.dot(
                    current, taps[0, tap_h, tap_w], preferred_element_type=jnp.float32
                )
                even = even + jnp.dot(
                    prior, taps[2, tap_h, tap_w], preferred_element_type=jnp.float32
                )
                odd = odd + jnp.dot(
                    current, taps[1, tap_h, tap_w], preferred_element_type=jnp.float32
                )
        stacked = jnp.stack(
            (even.reshape(rows_in, height * width, -1), odd.reshape(rows_in, height * width, -1)),
            axis=1,
        )
        return stacked.reshape(-1, piece.shape[1])

    before_all = forward_pass(up_kernel, up_columns).reshape(
        2 * rows_in, height, width, out_channels
    )
    hidden = jax.nn.silu(before_all).astype(jnp.bfloat16)
    earlier_hidden = from_previous(hidden[-2:])
    hidden_pad = pad_rows(widen(jnp.concatenate((earlier_hidden, hidden), axis=0)))
    cot_pad = pad_rows(widen(jnp.concatenate((cotangent, from_next(cotangent[:2])), axis=0)))

    def mix_forward(piece, start):
        taps = piece.reshape(3, 3, 3, out_channels, piece.shape[1])
        total = jnp.zeros((block, piece.shape[1]), jnp.float32)
        for tap_t in range(3):
            for tap_h in range(3):
                for tap_w in range(3):
                    total = total + jnp.dot(
                        window(hidden_pad, tap_t, count, tap_h, tap_w, height, width),
                        taps[tap_t, tap_h, tap_w],
                        preferred_element_type=jnp.float32,
                    )
        return total

    def mix_backward(piece):
        taps = piece.reshape(3, 3, 3, out_channels, piece.shape[1])
        total = jnp.zeros((block, out_channels), jnp.float32)
        for tap_t in range(3):
            for tap_h in range(3):
                for tap_w in range(3):
                    total = total + transposed(
                        window(cot_pad, 2 - tap_t, count, 2 - tap_h, 2 - tap_w, height, width),
                        taps[tap_t, tap_h, tap_w],
                    )
        return total

    empty = jnp.zeros((block, out_channels), jnp.float32)
    decoded_flat = forward_pass(mix_kernel, mix_forward)

    def accumulate(total, piece, start):
        return mix_backward(piece)

    hidden_grad = backward_pass(mix_kernel, accumulate, empty)
    flat_before = before_all.reshape(block, out_channels)
    sigma = jax.nn.sigmoid(flat_before)
    before_grad = (hidden_grad * sigma * (1.0 + flat_before * (1.0 - sigma))).astype(jnp.bfloat16)
    before_grad = before_grad.reshape(count, height, width, out_channels)
    grad_pad = pad_rows(widen(jnp.concatenate((before_grad, from_next(before_grad[:1])), axis=0)))
    evens = grad_pad[0::2]
    odds = grad_pad[1::2]

    def up_backward(total, piece, start):
        taps = piece.reshape(3, 3, 3, in_channels, piece.shape[1])
        for tap_h in range(3):
            for tap_w in range(3):
                total = total + transposed(
                    window(evens, 0, frame_count, 2 - tap_h, 2 - tap_w, height, width),
                    taps[0, tap_h, tap_w],
                )
                total = total + transposed(
                    window(odds, 0, frame_count, 2 - tap_h, 2 - tap_w, height, width),
                    taps[1, tap_h, tap_w],
                )
                total = total + transposed(
                    window(evens, 1, frame_count, 2 - tap_h, 2 - tap_w, height, width),
                    taps[2, tap_h, tap_w],
                )
        return total

    grad_start = jnp.zeros((frame_count * height * width, in_channels), jnp.float32)
    grad_total = backward_pass(up_kernel, up_backward, grad_start)
    decoded = decoded_flat.astype(jnp.bfloat16).reshape(count, height, width, out_channels)
    frames_grad = grad_total.astype(jnp.bfloat16).reshape(frame_count, height, width, in_channels)
    return (decoded, frames_grad)


MESH_ID = pl.DeviceIdType.MESH
BF16 = jnp.bfloat16
F32 = jnp.float32


def shifted(rows, by):
    if by == 0:
        return rows
    count = rows.shape[0]
    place = lax.broadcasted_iota(jnp.int32, rows.shape, 0)
    if by < 0:
        return jnp.where(place == 0, 0.0, pltpu.roll(rows, 1, 0))
    return jnp.where(place == count - 1, 0.0, pltpu.roll(rows, count - 1, 0))


def pairs(parts):
    if len(parts) % 2:
        parts = parts + [jnp.zeros_like(parts[0])]
    return [
        jnp.concatenate((parts[i], parts[i + 1]), axis=1).astype(BF16)
        for i in range(0, len(parts), 2)
    ]


def ring_tm(place, n):
    half = place // (n // 2)
    level = place + half * (n - 1 - 2 * place)
    return 2 * level + half


def fused_kernel(
    n, up_ref, mix_ref, frames_ref, cot_ref, decoded_ref, grad_ref,
    up_all, mix_all, frames_all, cot_all, up_taps, inputs, raw, before, hidden, patches,
    cots, spread, grads, part_d, part_g, got_d, got_g, sum_d, sum_g, last_d, last_g,
    ring_send, ring_recv, halo_send, halo_recv, col_send, col_recv, out_send, out_recv,
):
    me, q = lax.axis_index("tm"), lax.axis_index("col")
    sibling = q + 1 - 2 * (q % 2)
    across = (q + 2) % 4
    diagonal = (sibling + 2) % 4
    level, side = me // 2, me % 2
    place = level + side * (n - 1 - 2 * level)
    right, left = ring_tm((place + 1) % n, n), ring_tm((place + n - 1) % n, n)
    after, ahead = (me + 1) % n, (me + n - 1) % n
    count, in_channels = frames_ref.shape[0], frames_ref.shape[3]
    times, channels = cot_ref.shape[0], cot_ref.shape[3]
    cols = frames_ref.shape[2]
    width = 4 * cols
    small = channels // 4
    rows = mix_ref.shape[0]
    span = 9 * small + small

    def remote(src, dst, send, recv, tm, col):
        return pltpu.make_async_remote_copy(
            src_ref=src, dst_ref=dst, send_sem=send, recv_sem=recv,
            device_id=(tm, col), device_id_type=MESH_ID,
        )

    barrier = pltpu.get_barrier_semaphore()
    for tm, col in ((left, q), (right, q), (after, q), (ahead, q), (me, sibling), (me, across)):
        pl.semaphore_signal(barrier, inc=1, device_id=(tm, col), device_id_type=MESH_ID)

    source = lax.broadcasted_iota(jnp.int32, (channels, 2 * small), 0)
    lane = lax.broadcasted_iota(jnp.int32, (channels, 2 * small), 1)
    lane_low = lane % small
    wanted = rows * (lane_low // 8) + 8 * q + lane_low % 8
    first = jnp.where((source == wanted) & (lane < small), 1.0, 0.0).astype(BF16)
    second = jnp.where((source == wanted) & (lane >= small), 1.0, 0.0).astype(BF16)
    mine = pl.ds(pl.multiple_of(me * rows, rows), rows)
    for tap_h in range(3):
        order = [(kt * 3 + tap_h) * 3 + kw for kw in range(3) for kt in range(3)]
        for i in range(0, 10, 2):
            picked = jnp.dot(
                mix_ref[:, order[i] * channels : (order[i] + 1) * channels], first,
                preferred_element_type=F32,
            )
            if i < 8:
                picked = picked + jnp.dot(
                    mix_ref[:, order[i + 1] * channels : (order[i + 1] + 1) * channels], second,
                    preferred_element_type=F32,
                )
            start = tap_h * span + i * small
            mix_all[mine, start : start + 2 * small] = picked.astype(BF16)
    up_all[me] = up_ref[...]
    frames_all[q, 2 : 2 + count] = frames_ref[...]
    cot_all[q, 0:times] = cot_ref[...]
    pl.semaphore_wait(barrier, 6)

    def ring(direction, kind, step):
        owner = ring_tm((place + (n - step if direction == 0 else step)) % n, n)
        target = right if direction == 0 else left
        ref = up_all.at[owner] if kind == 0 else mix_all.at[
            pl.ds(pl.multiple_of(owner * rows, rows), rows)
        ]
        return remote(
            ref, ref, ring_send.at[direction, kind, step], ring_recv.at[direction, kind, step],
            target, q,
        )

    def steps_of(direction, kind):
        return n // 2 if direction == kind else n // 2 - 1

    copies = {}

    def ring_start(kind, step):
        for direction in range(2):
            if step < steps_of(direction, kind):
                copies[direction, kind, step] = ring(direction, kind, step)
                copies[direction, kind, step].start()

    def ring_got(kind, step):
        for direction in range(2):
            if step < steps_of(direction, kind):
                copies[direction, kind, step].wait_recv()

    ring_start(0, 0)
    halos = [
        remote(frames_ref.at[count - 2 : count], frames_all.at[q, 0:2],
               halo_send.at[0], halo_recv.at[0], after, q),
        remote(frames_ref.at[0:1], frames_all.at[q, count + 2 : count + 3],
               halo_send.at[1], halo_recv.at[1], ahead, q),
        remote(cot_ref.at[0:3], cot_all.at[q, times : times + 3],
               halo_send.at[2], halo_recv.at[2], ahead, q),
    ]
    for copy in halos:
        copy.start()
    ring_start(1, 0)
    for copy in halos:
        copy.wait_recv()

    @pl.when(me == 0)
    def _():
        frames_all[q, 0:2] = jnp.zeros((2,) + frames_ref.shape[1:], BF16)

    @pl.when(me == n - 1)
    def _():
        frames_all[q, count + 2 : count + 3] = jnp.zeros((1,) + frames_ref.shape[1:], BF16)
        cot_all[q, times : times + 3] = jnp.zeros((3,) + cot_ref.shape[1:], BF16)

    crossing = [
        remote(ref.at[q], ref.at[q], col_send.at[i], col_recv.at[i], me, across)
        for i, ref in enumerate((frames_all, cot_all))
    ]
    beside = [
        remote(ref.at[q], ref.at[q], col_send.at[2 + i], col_recv.at[2 + i], me, sibling)
        for i, ref in enumerate((frames_all, cot_all))
    ]
    for copy in crossing + beside:
        copy.start()
    ring_got(0, 0)
    ring_start(0, 1)
    ring_got(1, 0)
    ring_start(1, 1)
    for copy in crossing:
        copy.wait_recv()
    passed = [
        remote(ref.at[across], ref.at[across], col_send.at[4 + i], col_recv.at[4 + i], me, sibling)
        for i, ref in enumerate((frames_all, cot_all))
    ]
    for copy in passed:
        copy.start()
    ring_got(0, 1)
    ring_start(0, 2)
    ring_got(1, 1)
    ring_start(1, 2)
    for copy in beside + passed:
        copy.wait_recv()

    @pl.loop(0, count + 3)
    def _(t):
        for r in range(2):
            line = jnp.concatenate([frames_all[c, t, r].astype(F32) for c in range(4)], axis=0)
            at = pl.ds(pl.multiple_of(t * width, width), width)
            for kw in range(3):
                inputs[r, at, kw * in_channels : (kw + 1) * in_channels] = shifted(
                    line, kw - 1
                ).astype(BF16)

    @pl.loop(0, times + 3)
    def _(t):
        for r in range(2):
            line = jnp.concatenate([cot_all[c, t, r].astype(F32) for c in range(4)], axis=0)
            cots[r, pl.ds(pl.multiple_of(t * width, width), width)] = line.astype(BF16)

    ring_got(0, 2)
    ring_start(0, 3)
    ring_got(1, 2)
    ring_start(1, 3)
    ring_got(0, 3)

    taken = 9 * in_channels
    for kt in range(3):
        for start in range(0, taken, in_channels):
            part = up_all[:, kt * 8 : kt * 8 + 8, start : start + in_channels].astype(F32)
            up_taps[kt * small : (kt + 1) * small, start : start + in_channels] = part.reshape(
                small, in_channels
            ).astype(BF16)
    up_taps[3 * small : 4 * small] = jnp.zeros((small, taken), BF16)

    wide = 3 * in_channels
    for r in range(2):
        total = None
        for r_in in range(2):
            kh = r_in - r + 1
            term = lax.dot_general(
                inputs[r_in], up_taps[:, kh * wide : (kh + 1) * wide],
                (((1,), (1,)), ((), ())), preferred_element_type=F32,
            )
            total = term if total is None else total + term
        raw[r] = total

    def frame(t):
        return slice(t * width, (t + 1) * width)

    for r in range(2):
        for t in range(times + 3):
            if t % 2 == 0:
                value = raw[r, frame(t // 2 + 1), 0:small] + raw[
                    r, frame(t // 2), 2 * small : 3 * small
                ]
            else:
                value = raw[r, frame((t + 1) // 2), small : 2 * small]
            before[r, frame(t)] = value
            active = value / (1.0 + jnp.exp(-value))
            hidden[r, frame(t)] = active.astype(BF16).astype(F32)

    for r in range(2):
        @pl.loop(0, times)
        def _(t):
            parts = []
            lines = [
                hidden[r, pl.ds(pl.multiple_of((t + kt) * width, width), width)] for kt in range(3)
            ]
            for kw in range(3):
                parts += [shifted(line, kw - 1) for line in lines]
            at = pl.ds(pl.multiple_of(t * width, width), width)
            for i, pair in enumerate(pairs(parts)):
                patches[r, at, i * 2 * small : (i + 1) * 2 * small] = pair

    ring_got(1, 3)

    for r in range(2):
        total = None
        for r_in in range(2):
            kh = r_in - r + 1
            term = lax.dot_general(
                patches[r_in], mix_all[:, kh * span : (kh + 1) * span],
                (((1,), (1,)), ((), ())), preferred_element_type=F32,
            )
            total = term if total is None else total + term
        for t in range(times):
            for c in range(4):
                low = t * width + c * cols
                part_d[c, t, r] = total[low : low + cols].astype(BF16)

    def exchange(i, part, got):
        return [
            remote(part.at[target], got.at[j], out_send.at[i + j], out_recv.at[i + j], me, sibling)
            for j, target in enumerate((sibling, diagonal))
        ]

    def add_and_cross(i, part, got, summed, last, first_copies):
        for copy in first_copies:
            copy.wait_recv()
        summed[...] = (part[across].astype(F32) + got[1].astype(F32)).astype(BF16)
        copy = remote(summed, last, out_send.at[i + 2], out_recv.at[i + 2], me, across)
        copy.start()
        return copy

    def finish(part, got, last, copy, out):
        copy.wait_recv()
        out[...] = (part[q].astype(F32) + got[0].astype(F32) + last[...].astype(F32)).astype(BF16)

    out_d = exchange(0, part_d, got_d)
    for copy in out_d:
        copy.start()

    for r in range(2):
        total = None
        for r_in in range(2):
            kh = r - r_in + 1
            term = jnp.dot(
                cots[r_in], mix_all[:, kh * span : (kh + 1) * span], preferred_element_type=F32
            )
            total = term if total is None else total + term
        spread[r] = total

    cross_d = add_and_cross(0, part_d, got_d, sum_d, last_d, out_d)

    for r in range(2):
        lines = []
        for t in range(times + 1):
            gradient = None
            for kw in range(3):
                part = None
                for kt in range(3):
                    low = (kw * 3 + kt) * small
                    piece = spread[r, frame(t + 2 - kt), low : low + small]
                    part = piece if part is None else part + piece
                part = shifted(part, 1 - kw)
                gradient = part if gradient is None else gradient + part
            value = before[r, frame(t + 2)]
            sigma = 1.0 / (1.0 + jnp.exp(-value))
            gradient = gradient * sigma * (1.0 + value * (1.0 - sigma))
            hidden[r, frame(t)] = gradient.astype(BF16).astype(F32)

    for r in range(2):
        for i in range(count):
            lines = [hidden[r, frame(2 * i + kt)] for kt in range(3)]
            for kw in range(3):
                for j, pair in enumerate(pairs([shifted(line, 1 - kw) for line in lines])):
                    grads[r, kw, frame(i), j * 2 * small : (j + 1) * 2 * small] = pair

    for r in range(2):
        total = None
        for r_in in range(2):
            kh = r - r_in + 1
            for kw in range(3):
                start = (kh * 3 + kw) * in_channels
                term = jnp.dot(
                    grads[r_in, kw], up_taps[:, start : start + in_channels],
                    preferred_element_type=F32,
                )
                total = term if total is None else total + term
        for i in range(count):
            for c in range(4):
                low = i * width + c * cols
                part_g[c, i, r] = total[low : low + cols].astype(BF16)

    out_g = exchange(3, part_g, got_g)
    for copy in out_g:
        copy.start()
    finish(part_d, got_d, last_d, cross_d, decoded_ref)
    cross_g = add_and_cross(3, part_g, got_g, sum_g, last_g, out_g)
    finish(part_g, got_g, last_g, cross_g, grad_ref)
    for copy in list(copies.values()) + halos + crossing + beside + passed:
        copy.wait_send()
    for copy in out_d + out_g + [cross_d, cross_g]:
        copy.wait_send()


def fused(frames, up_kernel, mix_kernel, cotangent):
    n = lax.axis_size("tm")
    count, height, cols, in_channels = frames.shape
    times, channels = cotangent.shape[0], cotangent.shape[3]
    width, small = 4 * cols, channels // 4
    share = up_kernel.shape[1] // 4
    q = lax.axis_index("col")
    up_rows = lax.dynamic_slice_in_dim(up_kernel.T, q * share, share, 0)
    up_rows = up_rows.reshape(share, 3, 9 * in_channels).transpose(1, 0, 2)
    up_rows = up_rows.reshape(3 * share, 9 * in_channels)
    mix_rows = mix_kernel.T
    whole = pl.BlockSpec(memory_space=pltpu.VMEM)
    d_block, g_block = (times, height, cols, channels), (count, height, cols, in_channels)
    dma = pltpu.SemaphoreType.DMA
    return pl.pallas_call(
        functools.partial(fused_kernel, n),
        out_shape=(
            jax.ShapeDtypeStruct(d_block, BF16),
            jax.ShapeDtypeStruct(g_block, BF16),
        ),
        in_specs=[whole] * 4,
        out_specs=(whole, whole),
        scratch_shapes=[
            pltpu.VMEM((n,) + up_rows.shape, BF16),
            pltpu.VMEM((channels, 30 * small), BF16),
            pltpu.VMEM((4, count + 3, height, cols, in_channels), BF16),
            pltpu.VMEM((4, times + 3, height, cols, channels), BF16),
            pltpu.VMEM((4 * small, 9 * in_channels), BF16),
            pltpu.VMEM((2, (count + 3) * width, 3 * in_channels), BF16),
            pltpu.VMEM((2, (count + 3) * width, 4 * small), F32),
            pltpu.VMEM((2, (times + 3) * width, small), F32),
            pltpu.VMEM((2, (times + 3) * width, small), F32),
            pltpu.VMEM((2, times * width, 10 * small), BF16),
            pltpu.VMEM((2, (times + 3) * width, channels), BF16),
            pltpu.VMEM((2, (times + 3) * width, 10 * small), F32),
            pltpu.VMEM((2, 3, count * width, 4 * small), BF16),
            pltpu.VMEM((4,) + d_block, BF16),
            pltpu.VMEM((4,) + g_block, BF16),
            pltpu.VMEM((2,) + d_block, BF16),
            pltpu.VMEM((2,) + g_block, BF16),
            pltpu.VMEM(d_block, BF16),
            pltpu.VMEM(g_block, BF16),
            pltpu.VMEM(d_block, BF16),
            pltpu.VMEM(g_block, BF16),
            dma((2, 2, n // 2)),
            dma((2, 2, n // 2)),
            dma((3,)),
            dma((3,)),
            dma((6,)),
            dma((6,)),
            dma((6,)),
            dma((6,)),
        ],
        compiler_params=pltpu.CompilerParams(
            collective_id=0, has_side_effects=True, vmem_limit_bytes=56 * 1024 * 1024
        ),
    )(up_rows, mix_rows, frames, cotangent)


def solution(mesh):
    placed = (P("tm", None, "col", None), P(None, "tm"), P(None, "tm"), P("tm", None, "col", None))
    small = mesh.shape["tm"] == 8 and mesh.shape["col"] == 4
    return jax.shard_map(
        fused if small else shards,
        mesh=mesh,
        in_specs=placed,
        out_specs=(P("tm", None, "col", None), P("tm", None, "col", None)),
        check_vma=False,
    )
```

```python
import functools

import jax
import jax.numpy as jnp
from jax import lax
from jax.experimental import pallas as pl
from jax.experimental.pallas import tpu as pltpu
from jax.sharding import PartitionSpec as P


def with_halo(block, sides, width):
    for axis, dim in sides:
        count = lax.axis_size(axis)
        forward = [(i, i + 1) for i in range(count - 1)]
        backward = [(target, source) for source, target in forward]
        low = lax.ppermute(
            lax.slice_in_dim(block, block.shape[dim] - width, None, axis=dim), axis, forward
        )
        high = lax.ppermute(lax.slice_in_dim(block, 0, width, axis=dim), axis, backward)
        block = jnp.concatenate([low, block, high], axis=dim)
    return block


def from_behind(array, axis, by):
    devices = lax.axis_size(axis)
    pairs = [(i, i + by) for i in range(devices) if 0 <= i + by < devices]
    return lax.ppermute(array, axis, pairs)


def widen(field):
    return with_halo(field, (("col", 2),), 1)


def from_previous(field):
    return from_behind(field, "tm", 1)


def from_next(field):
    return from_behind(field, "tm", -1)


def forward_pass(kernel, produce):
    return produce(lax.all_gather(kernel, "tm", axis=1, tiled=True), jnp.int32(0))


def backward_pass(kernel, combine, initial):
    return combine(initial, lax.all_gather(kernel, "tm", axis=1, tiled=True), jnp.int32(0))


def pad_rows(field):
    return jnp.pad(field, ((0, 0), (1, 1), (0, 0), (0, 0)))


def window(padded, first, count, row_low, col_low, height, width):
    part = padded[first : first + count, row_low : row_low + height, col_low : col_low + width]
    return part.reshape(-1, part.shape[-1])


def transposed(rows, matrix):
    return lax.dot_general(
        rows, matrix, (((1,), (1,)), ((), ())), preferred_element_type=jnp.float32
    )


def shards(frames, up_kernel, mix_kernel, cotangent):
    frame_count, height, width, in_channels = frames.shape
    out_channels = mix_kernel.shape[0] // 27
    count = 2 * frame_count
    block = count * height * width
    widened = widen(frames)
    earlier = from_previous(widened[-1:])
    extended = pad_rows(jnp.concatenate((earlier, widened), axis=0))
    rows_in = extended.shape[0] - 1

    def up_columns(piece, start):
        taps = piece.reshape(3, 3, 3, in_channels, piece.shape[1])
        even = jnp.zeros((rows_in * height * width, piece.shape[1]), jnp.float32)
        odd = even
        for tap_h in range(3):
            for tap_w in range(3):
                current = window(extended, 1, rows_in, tap_h, tap_w, height, width)
                prior = window(extended, 0, rows_in, tap_h, tap_w, height, width)
                even = even + jnp.dot(
                    current, taps[0, tap_h, tap_w], preferred_element_type=jnp.float32
                )
                even = even + jnp.dot(
                    prior, taps[2, tap_h, tap_w], preferred_element_type=jnp.float32
                )
                odd = odd + jnp.dot(
                    current, taps[1, tap_h, tap_w], preferred_element_type=jnp.float32
                )
        stacked = jnp.stack(
            (even.reshape(rows_in, height * width, -1), odd.reshape(rows_in, height * width, -1)),
            axis=1,
        )
        return stacked.reshape(-1, piece.shape[1])

    before_all = forward_pass(up_kernel, up_columns).reshape(
        2 * rows_in, height, width, out_channels
    )
    hidden = jax.nn.silu(before_all).astype(jnp.bfloat16)
    earlier_hidden = from_previous(hidden[-2:])
    hidden_pad = pad_rows(widen(jnp.concatenate((earlier_hidden, hidden), axis=0)))
    cot_pad = pad_rows(widen(jnp.concatenate((cotangent, from_next(cotangent[:2])), axis=0)))

    def mix_forward(piece, start):
        taps = piece.reshape(3, 3, 3, out_channels, piece.shape[1])
        total = jnp.zeros((block, piece.shape[1]), jnp.float32)
        for tap_t in range(3):
            for tap_h in range(3):
                for tap_w in range(3):
                    total = total + jnp.dot(
                        window(hidden_pad, tap_t, count, tap_h, tap_w, height, width),
                        taps[tap_t, tap_h, tap_w],
                        preferred_element_type=jnp.float32,
                    )
        return total

    def mix_backward(piece):
        taps = piece.reshape(3, 3, 3, out_channels, piece.shape[1])
        total = jnp.zeros((block, out_channels), jnp.float32)
        for tap_t in range(3):
            for tap_h in range(3):
                for tap_w in range(3):
                    total = total + transposed(
                        window(cot_pad, 2 - tap_t, count, 2 - tap_h, 2 - tap_w, height, width),
                        taps[tap_t, tap_h, tap_w],
                    )
        return total

    empty = jnp.zeros((block, out_channels), jnp.float32)
    decoded_flat = forward_pass(mix_kernel, mix_forward)

    def accumulate(total, piece, start):
        return mix_backward(piece)

    hidden_grad = backward_pass(mix_kernel, accumulate, empty)
    flat_before = before_all.reshape(block, out_channels)
    sigma = jax.nn.sigmoid(flat_before)
    before_grad = (hidden_grad * sigma * (1.0 + flat_before * (1.0 - sigma))).astype(jnp.bfloat16)
    before_grad = before_grad.reshape(count, height, width, out_channels)
    grad_pad = pad_rows(widen(jnp.concatenate((before_grad, from_next(before_grad[:1])), axis=0)))
    evens = grad_pad[0::2]
    odds = grad_pad[1::2]

    def up_backward(total, piece, start):
        taps = piece.reshape(3, 3, 3, in_channels, piece.shape[1])
        for tap_h in range(3):
            for tap_w in range(3):
                total = total + transposed(
                    window(evens, 0, frame_count, 2 - tap_h, 2 - tap_w, height, width),
                    taps[0, tap_h, tap_w],
                )
                total = total + transposed(
                    window(odds, 0, frame_count, 2 - tap_h, 2 - tap_w, height, width),
                    taps[1, tap_h, tap_w],
                )
                total = total + transposed(
                    window(evens, 1, frame_count, 2 - tap_h, 2 - tap_w, height, width),
                    taps[2, tap_h, tap_w],
                )
        return total

    grad_start = jnp.zeros((frame_count * height * width, in_channels), jnp.float32)
    grad_total = backward_pass(up_kernel, up_backward, grad_start)
    decoded = decoded_flat.astype(jnp.bfloat16).reshape(count, height, width, out_channels)
    frames_grad = grad_total.astype(jnp.bfloat16).reshape(frame_count, height, width, in_channels)
    return (decoded, frames_grad)


MESH_ID = pl.DeviceIdType.MESH
BF16 = jnp.bfloat16
F32 = jnp.float32
HEIGHTS = (1, 0, 2)


def shifted(rows, by):
    if by == 0:
        return rows
    count = rows.shape[0]
    place = lax.broadcasted_iota(jnp.int32, rows.shape, 0)
    if by < 0:
        return jnp.where(place == 0, 0.0, pltpu.roll(rows, 1, 0))
    return jnp.where(place == count - 1, 0.0, pltpu.roll(rows, count - 1, 0))


def pairs(parts):
    if len(parts) % 2:
        parts = parts + [jnp.zeros_like(parts[0])]
    return [
        jnp.concatenate((parts[i], parts[i + 1]), axis=1).astype(BF16)
        for i in range(0, len(parts), 2)
    ]


def ring_tm(place, n):
    half = place // (n // 2)
    level = place + half * (n - 1 - 2 * place)
    return 2 * level + half


def fused_kernel(
    n, up_ref, mix_ref, frames_ref, cot_ref, decoded_ref, grad_ref,
    up_all, mix_all, frames_all, cot_all, up_taps, inputs, raw, before, hidden, patches, decoding,
    cots, spread, grads, part_d, part_g, got_d, got_g, sum_d, sum_g, last_d, last_g,
    ring_send, ring_recv, halo_send, halo_recv, col_send, col_recv, out_send, out_recv,
):
    me, q = lax.axis_index("tm"), lax.axis_index("col")
    sibling = q + 1 - 2 * (q % 2)
    across = (q + 2) % 4
    diagonal = (sibling + 2) % 4
    level, side = me // 2, me % 2
    place = level + side * (n - 1 - 2 * level)
    right, left = ring_tm((place + 1) % n, n), ring_tm((place + n - 1) % n, n)
    after, ahead = (me + 1) % n, (me + n - 1) % n
    count, in_channels = frames_ref.shape[0], frames_ref.shape[3]
    times, channels = cot_ref.shape[0], cot_ref.shape[3]
    cols = frames_ref.shape[2]
    width = 4 * cols
    small = channels // 4
    rows = mix_ref.shape[0]

    def remote(src, dst, send, recv, tm, col):
        return pltpu.make_async_remote_copy(
            src_ref=src, dst_ref=dst, send_sem=send, recv_sem=recv,
            device_id=(tm, col), device_id_type=MESH_ID,
        )

    barrier = pltpu.get_barrier_semaphore()
    for tm, col in ((left, q), (right, q), (after, q), (ahead, q), (me, sibling), (me, across)):
        pl.semaphore_signal(barrier, inc=1, device_id=(tm, col), device_id_type=MESH_ID)

    taken = 3 * in_channels
    row = lax.broadcasted_iota(jnp.int32, (24, rows), 0)
    column = lax.broadcasted_iota(jnp.int32, (24, rows), 1)
    picks = [
        jnp.where((row // 8 == kt) & (column == 8 * q + row % 8), 1.0, 0.0).astype(BF16)
        for kt in range(3)
    ]
    for tap_h in HEIGHTS:
        picked = None
        for kt in range(3):
            start = (kt * 3 + tap_h) * taken
            term = jnp.dot(
                picks[kt], up_ref[:, start : start + taken], preferred_element_type=F32
            )
            picked = term if picked is None else picked + term
        up_all[tap_h, me] = picked.astype(BF16)
    pl.semaphore_wait(barrier, 6)

    def ring(direction, kind, tap_h, step):
        owner = ring_tm((place + (n - step if direction == 0 else step)) % n, n)
        target = right if direction == 0 else left
        ref = up_all.at[tap_h, owner] if kind == 0 else mix_all.at[
            tap_h, pl.ds(pl.multiple_of(owner * rows, rows), rows)
        ]
        index = (direction, kind, tap_h, step)
        return remote(ref, ref, ring_send.at[index], ring_recv.at[index], target, q)

    def steps_of(direction, kind):
        return n // 2 if direction == kind else n // 2 - 1

    copies = {}

    def ring_start(kind, tap_h, step):
        for direction in range(2):
            if step < steps_of(direction, kind):
                copy = ring(direction, kind, tap_h, step)
                copies[direction, kind, tap_h, step] = copy
                copy.start()

    def ring_got(kind, tap_h, step):
        for direction in range(2):
            if step < steps_of(direction, kind):
                copies[direction, kind, tap_h, step].wait_recv()

    def ring_pass(kind, step):
        for tap_h in HEIGHTS:
            ring_got(kind, tap_h, step)
            ring_start(kind, tap_h, step + 1)

    for tap_h in HEIGHTS:
        ring_start(0, tap_h, 0)
    halos = [
        remote(frames_ref.at[count - 2 : count], frames_all.at[q, 0:2],
               halo_send.at[0], halo_recv.at[0], after, q),
        remote(frames_ref.at[0:1], frames_all.at[q, count + 2 : count + 3],
               halo_send.at[1], halo_recv.at[1], ahead, q),
        remote(cot_ref.at[0:3], cot_all.at[q, times : times + 3],
               halo_send.at[2], halo_recv.at[2], ahead, q),
    ]
    for copy in halos:
        copy.start()
    frames_all[q, 2 : 2 + count] = frames_ref[...]
    cot_all[q, 0:times] = cot_ref[...]

    source = lax.broadcasted_iota(jnp.int32, (channels, 2 * small), 0)
    lane = lax.broadcasted_iota(jnp.int32, (channels, 2 * small), 1)
    lane_low = lane % small
    wanted = rows * (lane_low // 8) + 8 * q + lane_low % 8
    first = jnp.where((source == wanted) & (lane < small), 1.0, 0.0).astype(BF16)
    second = jnp.where((source == wanted) & (lane >= small), 1.0, 0.0).astype(BF16)
    mine = pl.ds(pl.multiple_of(me * rows, rows), rows)
    for tap_h in HEIGHTS:
        order = [(kt * 3 + tap_h) * 3 + kw for kw in range(3) for kt in range(3)]
        for i in range(0, 10, 2):
            picked = jnp.dot(
                mix_ref[:, order[i] * channels : (order[i] + 1) * channels], first,
                preferred_element_type=F32,
            )
            if i < 8:
                picked = picked + jnp.dot(
                    mix_ref[:, order[i + 1] * channels : (order[i + 1] + 1) * channels], second,
                    preferred_element_type=F32,
                )
            mix_all[tap_h, mine, i * small : (i + 2) * small] = picked.astype(BF16)
    ring_pass(0, 0)
    for tap_h in HEIGHTS:
        ring_start(1, tap_h, 0)
    for copy in halos:
        copy.wait_recv()

    @pl.when(me == 0)
    def _():
        frames_all[q, 0:2] = jnp.zeros((2,) + frames_ref.shape[1:], BF16)

    @pl.when(me == n - 1)
    def _():
        frames_all[q, count + 2 : count + 3] = jnp.zeros((1,) + frames_ref.shape[1:], BF16)
        cot_all[q, times : times + 3] = jnp.zeros((3,) + cot_ref.shape[1:], BF16)

    crossing = [
        remote(ref.at[q], ref.at[q], col_send.at[i], col_recv.at[i], me, across)
        for i, ref in enumerate((frames_all, cot_all))
    ]
    beside = [
        remote(ref.at[q], ref.at[q], col_send.at[2 + i], col_recv.at[2 + i], me, sibling)
        for i, ref in enumerate((frames_all, cot_all))
    ]
    for copy in crossing + beside:
        copy.start()
    ring_pass(0, 1)
    for copy in crossing:
        copy.wait_recv()
    passed = [
        remote(ref.at[across], ref.at[across], col_send.at[4 + i], col_recv.at[4 + i], me, sibling)
        for i, ref in enumerate((frames_all, cot_all))
    ]
    for copy in passed:
        copy.start()
    ring_pass(1, 0)
    ring_pass(0, 2)
    for copy in beside + passed:
        copy.wait_recv()

    @pl.loop(0, count + 3)
    def _(t):
        for r in range(2):
            line = jnp.concatenate([frames_all[c, t, r].astype(F32) for c in range(4)], axis=0)
            at = pl.ds(pl.multiple_of(t * width, width), width)
            for kw in range(3):
                inputs[r, at, kw * in_channels : (kw + 1) * in_channels] = shifted(
                    line, kw - 1
                ).astype(BF16)

    @pl.loop(0, times + 3)
    def _(t):
        for r in range(2):
            line = jnp.concatenate([cot_all[c, t, r].astype(F32) for c in range(4)], axis=0)
            cots[r, pl.ds(pl.multiple_of(t * width, width), width)] = line.astype(BF16)

    ring_pass(1, 1)

    for step, kh in enumerate(HEIGHTS):
        ring_got(0, kh, 3)
        for kt in range(3):
            part = up_all[kh, :, kt * 8 : kt * 8 + 8, :].astype(F32)
            up_taps[kh, kt * small : (kt + 1) * small] = part.reshape(small, taken).astype(BF16)
        up_taps[kh, 3 * small : 4 * small] = jnp.zeros((small, taken), BF16)
        for r in range(2):
            r_in = r + kh - 1
            if 0 <= r_in < 2:
                term = lax.dot_general(
                    inputs[r_in], up_taps[kh], (((1,), (1,)), ((), ())),
                    preferred_element_type=F32,
                )
                raw[r] = term if step == 0 else raw[r] + term
        if step == 0:
            ring_pass(1, 2)

    def frame(t):
        return slice(t * width, (t + 1) * width)

    for r in range(2):
        for t in range(times + 3):
            if t % 2 == 0:
                value = raw[r, frame(t // 2 + 1), 0:small] + raw[
                    r, frame(t // 2), 2 * small : 3 * small
                ]
            else:
                value = raw[r, frame((t + 1) // 2), small : 2 * small]
            before[r, frame(t)] = value
            active = value / (1.0 + jnp.exp(-value))
            hidden[r, frame(t)] = active.astype(BF16).astype(F32)

    for r in range(2):
        @pl.loop(0, times)
        def _(t):
            parts = []
            lines = [
                hidden[r, pl.ds(pl.multiple_of((t + kt) * width, width), width)] for kt in range(3)
            ]
            for kw in range(3):
                parts += [shifted(line, kw - 1) for line in lines]
            at = pl.ds(pl.multiple_of(t * width, width), width)
            for i, pair in enumerate(pairs(parts)):
                patches[r, at, i * 2 * small : (i + 1) * 2 * small] = pair

    def exchange(i, part, got):
        return [
            remote(part.at[target], got.at[j], out_send.at[i + j], out_recv.at[i + j], me, sibling)
            for j, target in enumerate((sibling, diagonal))
        ]

    out_d = exchange(0, part_d, got_d)
    for step, kh in enumerate(HEIGHTS):
        ring_got(1, kh, 3)
        for r in range(2):
            r_in = r + kh - 1
            if 0 <= r_in < 2:
                term = lax.dot_general(
                    patches[r_in], mix_all[kh], (((1,), (1,)), ((), ())),
                    preferred_element_type=F32,
                )
                decoding[r] = term if step == 0 else decoding[r] + term
        if step == 2:
            for r in range(2):
                for t in range(times):
                    for c in range(4):
                        low = t * width + c * cols
                        part_d[c, t, r] = decoding[r, low : low + cols].astype(BF16)
            for copy in out_d:
                copy.start()
        for r in range(2):
            r_in = r - kh + 1
            if 0 <= r_in < 2:
                term = jnp.dot(cots[r_in], mix_all[kh], preferred_element_type=F32)
                spread[r] = term if step == 0 else spread[r] + term

    def add_and_cross(i, part, got, summed, last, first_copies):
        for copy in first_copies:
            copy.wait_recv()
        summed[...] = (part[across].astype(F32) + got[1].astype(F32)).astype(BF16)
        copy = remote(summed, last, out_send.at[i + 2], out_recv.at[i + 2], me, across)
        copy.start()
        return copy

    def finish(part, got, last, copy, out):
        copy.wait_recv()
        out[...] = (part[q].astype(F32) + got[0].astype(F32) + last[...].astype(F32)).astype(BF16)

    cross_d = add_and_cross(0, part_d, got_d, sum_d, last_d, out_d)

    for r in range(2):
        lines = []
        for t in range(times + 1):
            gradient = None
            for kw in range(3):
                part = None
                for kt in range(3):
                    low = (kw * 3 + kt) * small
                    piece = spread[r, frame(t + 2 - kt), low : low + small]
                    part = piece if part is None else part + piece
                part = shifted(part, 1 - kw)
                gradient = part if gradient is None else gradient + part
            value = before[r, frame(t + 2)]
            sigma = 1.0 / (1.0 + jnp.exp(-value))
            gradient = gradient * sigma * (1.0 + value * (1.0 - sigma))
            hidden[r, frame(t)] = gradient.astype(BF16).astype(F32)

    for r in range(2):
        for i in range(count):
            lines = [hidden[r, frame(2 * i + kt)] for kt in range(3)]
            for kw in range(3):
                for j, pair in enumerate(pairs([shifted(line, 1 - kw) for line in lines])):
                    grads[r, kw, frame(i), j * 2 * small : (j + 1) * 2 * small] = pair

    for r in range(2):
        total = None
        for r_in in range(2):
            kh = r - r_in + 1
            for kw in range(3):
                start = kw * in_channels
                term = jnp.dot(
                    grads[r_in, kw], up_taps[kh, :, start : start + in_channels],
                    preferred_element_type=F32,
                )
                total = term if total is None else total + term
        for i in range(count):
            for c in range(4):
                low = i * width + c * cols
                part_g[c, i, r] = total[low : low + cols].astype(BF16)

    out_g = exchange(3, part_g, got_g)
    for copy in out_g:
        copy.start()
    finish(part_d, got_d, last_d, cross_d, decoded_ref)
    cross_g = add_and_cross(3, part_g, got_g, sum_g, last_g, out_g)
    finish(part_g, got_g, last_g, cross_g, grad_ref)
    for copy in list(copies.values()) + halos + crossing + beside + passed:
        copy.wait_send()
    for copy in out_d + out_g + [cross_d, cross_g]:
        copy.wait_send()


def fused(frames, up_kernel, mix_kernel, cotangent):
    n = lax.axis_size("tm")
    count, height, cols, in_channels = frames.shape
    times, channels = cotangent.shape[0], cotangent.shape[3]
    width, small = 4 * cols, channels // 4
    up_rows, mix_rows = up_kernel.T, mix_kernel.T
    whole = pl.BlockSpec(memory_space=pltpu.VMEM)
    d_block, g_block = (times, height, cols, channels), (count, height, cols, in_channels)
    dma = pltpu.SemaphoreType.DMA
    return pl.pallas_call(
        functools.partial(fused_kernel, n),
        out_shape=(
            jax.ShapeDtypeStruct(d_block, BF16),
            jax.ShapeDtypeStruct(g_block, BF16),
        ),
        in_specs=[whole] * 4,
        out_specs=(whole, whole),
        scratch_shapes=[
            pltpu.VMEM((3, n, 24, 3 * in_channels), BF16),
            pltpu.VMEM((3, channels, 10 * small), BF16),
            pltpu.VMEM((4, count + 3, height, cols, in_channels), BF16),
            pltpu.VMEM((4, times + 3, height, cols, channels), BF16),
            pltpu.VMEM((3, 4 * small, 3 * in_channels), BF16),
            pltpu.VMEM((2, (count + 3) * width, 3 * in_channels), BF16),
            pltpu.VMEM((2, (count + 3) * width, 4 * small), F32),
            pltpu.VMEM((2, (times + 3) * width, small), F32),
            pltpu.VMEM((2, (times + 3) * width, small), F32),
            pltpu.VMEM((2, times * width, 10 * small), BF16),
            pltpu.VMEM((2, times * width, channels), F32),
            pltpu.VMEM((2, (times + 3) * width, channels), BF16),
            pltpu.VMEM((2, (times + 3) * width, 10 * small), F32),
            pltpu.VMEM((2, 3, count * width, 4 * small), BF16),
            pltpu.VMEM((4,) + d_block, BF16),
            pltpu.VMEM((4,) + g_block, BF16),
            pltpu.VMEM((2,) + d_block, BF16),
            pltpu.VMEM((2,) + g_block, BF16),
            pltpu.VMEM(d_block, BF16),
            pltpu.VMEM(g_block, BF16),
            pltpu.VMEM(d_block, BF16),
            pltpu.VMEM(g_block, BF16),
            dma((2, 2, 3, n // 2)),
            dma((2, 2, 3, n // 2)),
            dma((3,)),
            dma((3,)),
            dma((6,)),
            dma((6,)),
            dma((6,)),
            dma((6,)),
        ],
        compiler_params=pltpu.CompilerParams(
            collective_id=0, has_side_effects=True, vmem_limit_bytes=56 * 1024 * 1024
        ),
    )(up_rows, mix_rows, frames, cotangent)


def solution(mesh):
    placed = (P("tm", None, "col", None), P(None, "tm"), P(None, "tm"), P("tm", None, "col", None))
    small = mesh.shape["tm"] == 8 and mesh.shape["col"] == 4
    return jax.shard_map(
        fused if small else shards,
        mesh=mesh,
        in_specs=placed,
        out_specs=(P("tm", None, "col", None), P("tm", None, "col", None)),
        check_vma=False,
    )
```

```python
import functools

import jax
import jax.numpy as jnp
from jax import lax
from jax.experimental import pallas as pl
from jax.experimental.pallas import tpu as pltpu
from jax.sharding import PartitionSpec as P


def with_halo(block, sides, width):
    for axis, dim in sides:
        count = lax.axis_size(axis)
        forward = [(i, i + 1) for i in range(count - 1)]
        backward = [(target, source) for source, target in forward]
        low = lax.ppermute(
            lax.slice_in_dim(block, block.shape[dim] - width, None, axis=dim), axis, forward
        )
        high = lax.ppermute(lax.slice_in_dim(block, 0, width, axis=dim), axis, backward)
        block = jnp.concatenate([low, block, high], axis=dim)
    return block


def from_behind(array, axis, by):
    devices = lax.axis_size(axis)
    pairs = [(i, i + by) for i in range(devices) if 0 <= i + by < devices]
    return lax.ppermute(array, axis, pairs)


def widen(field):
    return with_halo(field, (("col", 2),), 1)


def from_previous(field):
    return from_behind(field, "tm", 1)


def from_next(field):
    return from_behind(field, "tm", -1)


def forward_pass(kernel, produce):
    return produce(lax.all_gather(kernel, "tm", axis=1, tiled=True), jnp.int32(0))


def backward_pass(kernel, combine, initial):
    return combine(initial, lax.all_gather(kernel, "tm", axis=1, tiled=True), jnp.int32(0))


def pad_rows(field):
    return jnp.pad(field, ((0, 0), (1, 1), (0, 0), (0, 0)))


def window(padded, first, count, row_low, col_low, height, width):
    part = padded[first : first + count, row_low : row_low + height, col_low : col_low + width]
    return part.reshape(-1, part.shape[-1])


def transposed(rows, matrix):
    return lax.dot_general(
        rows, matrix, (((1,), (1,)), ((), ())), preferred_element_type=jnp.float32
    )


def shards(frames, up_kernel, mix_kernel, cotangent):
    frame_count, height, width, in_channels = frames.shape
    out_channels = mix_kernel.shape[0] // 27
    count = 2 * frame_count
    block = count * height * width
    widened = widen(frames)
    earlier = from_previous(widened[-1:])
    extended = pad_rows(jnp.concatenate((earlier, widened), axis=0))
    rows_in = extended.shape[0] - 1

    def up_columns(piece, start):
        taps = piece.reshape(3, 3, 3, in_channels, piece.shape[1])
        even = jnp.zeros((rows_in * height * width, piece.shape[1]), jnp.float32)
        odd = even
        for tap_h in range(3):
            for tap_w in range(3):
                current = window(extended, 1, rows_in, tap_h, tap_w, height, width)
                prior = window(extended, 0, rows_in, tap_h, tap_w, height, width)
                even = even + jnp.dot(
                    current, taps[0, tap_h, tap_w], preferred_element_type=jnp.float32
                )
                even = even + jnp.dot(
                    prior, taps[2, tap_h, tap_w], preferred_element_type=jnp.float32
                )
                odd = odd + jnp.dot(
                    current, taps[1, tap_h, tap_w], preferred_element_type=jnp.float32
                )
        stacked = jnp.stack(
            (even.reshape(rows_in, height * width, -1), odd.reshape(rows_in, height * width, -1)),
            axis=1,
        )
        return stacked.reshape(-1, piece.shape[1])

    before_all = forward_pass(up_kernel, up_columns).reshape(
        2 * rows_in, height, width, out_channels
    )
    hidden = jax.nn.silu(before_all).astype(jnp.bfloat16)
    earlier_hidden = from_previous(hidden[-2:])
    hidden_pad = pad_rows(widen(jnp.concatenate((earlier_hidden, hidden), axis=0)))
    cot_pad = pad_rows(widen(jnp.concatenate((cotangent, from_next(cotangent[:2])), axis=0)))

    def mix_forward(piece, start):
        taps = piece.reshape(3, 3, 3, out_channels, piece.shape[1])
        total = jnp.zeros((block, piece.shape[1]), jnp.float32)
        for tap_t in range(3):
            for tap_h in range(3):
                for tap_w in range(3):
                    total = total + jnp.dot(
                        window(hidden_pad, tap_t, count, tap_h, tap_w, height, width),
                        taps[tap_t, tap_h, tap_w],
                        preferred_element_type=jnp.float32,
                    )
        return total

    def mix_backward(piece):
        taps = piece.reshape(3, 3, 3, out_channels, piece.shape[1])
        total = jnp.zeros((block, out_channels), jnp.float32)
        for tap_t in range(3):
            for tap_h in range(3):
                for tap_w in range(3):
                    total = total + transposed(
                        window(cot_pad, 2 - tap_t, count, 2 - tap_h, 2 - tap_w, height, width),
                        taps[tap_t, tap_h, tap_w],
                    )
        return total

    empty = jnp.zeros((block, out_channels), jnp.float32)
    decoded_flat = forward_pass(mix_kernel, mix_forward)

    def accumulate(total, piece, start):
        return mix_backward(piece)

    hidden_grad = backward_pass(mix_kernel, accumulate, empty)
    flat_before = before_all.reshape(block, out_channels)
    sigma = jax.nn.sigmoid(flat_before)
    before_grad = (hidden_grad * sigma * (1.0 + flat_before * (1.0 - sigma))).astype(jnp.bfloat16)
    before_grad = before_grad.reshape(count, height, width, out_channels)
    grad_pad = pad_rows(widen(jnp.concatenate((before_grad, from_next(before_grad[:1])), axis=0)))
    evens = grad_pad[0::2]
    odds = grad_pad[1::2]

    def up_backward(total, piece, start):
        taps = piece.reshape(3, 3, 3, in_channels, piece.shape[1])
        for tap_h in range(3):
            for tap_w in range(3):
                total = total + transposed(
                    window(evens, 0, frame_count, 2 - tap_h, 2 - tap_w, height, width),
                    taps[0, tap_h, tap_w],
                )
                total = total + transposed(
                    window(odds, 0, frame_count, 2 - tap_h, 2 - tap_w, height, width),
                    taps[1, tap_h, tap_w],
                )
                total = total + transposed(
                    window(evens, 1, frame_count, 2 - tap_h, 2 - tap_w, height, width),
                    taps[2, tap_h, tap_w],
                )
        return total

    grad_start = jnp.zeros((frame_count * height * width, in_channels), jnp.float32)
    grad_total = backward_pass(up_kernel, up_backward, grad_start)
    decoded = decoded_flat.astype(jnp.bfloat16).reshape(count, height, width, out_channels)
    frames_grad = grad_total.astype(jnp.bfloat16).reshape(frame_count, height, width, in_channels)
    return (decoded, frames_grad)


MESH_ID = pl.DeviceIdType.MESH
BF16 = jnp.bfloat16
F32 = jnp.float32
HEIGHTS = (1, 0, 2)


def shifted(rows, by):
    if by == 0:
        return rows
    count = rows.shape[0]
    place = lax.broadcasted_iota(jnp.int32, rows.shape, 0)
    if by < 0:
        return jnp.where(place == 0, 0.0, pltpu.roll(rows, 1, 0))
    return jnp.where(place == count - 1, 0.0, pltpu.roll(rows, count - 1, 0))


def pairs(parts):
    if len(parts) % 2:
        parts = parts + [jnp.zeros_like(parts[0])]
    return [
        jnp.concatenate((parts[i], parts[i + 1]), axis=1).astype(BF16)
        for i in range(0, len(parts), 2)
    ]


def ring_tm(place, n):
    half = place // (n // 2)
    level = place + half * (n - 1 - 2 * place)
    return 2 * level + half


def fused_kernel(
    n, up_ref, mix_ref, frames_ref, cot_ref, decoded_ref, grad_ref,
    up_all, mix_all, frames_all, cot_all, up_taps, inputs, raw, before, hidden, patches, decoding,
    cots, spread, grads, part_d, part_g, got_d, got_g, sum_d, sum_g, last_d, last_g,
    ring_send, ring_recv, halo_send, halo_recv, col_send, col_recv, out_send, out_recv,
):
    me, q = lax.axis_index("tm"), lax.axis_index("col")
    sibling = q + 1 - 2 * (q % 2)
    across = (q + 2) % 4
    diagonal = (sibling + 2) % 4
    level, side = me // 2, me % 2
    place = level + side * (n - 1 - 2 * level)
    right, left = ring_tm((place + 1) % n, n), ring_tm((place + n - 1) % n, n)
    after, ahead = (me + 1) % n, (me + n - 1) % n
    count, in_channels = frames_ref.shape[0], frames_ref.shape[3]
    times, channels = cot_ref.shape[0], cot_ref.shape[3]
    cols = frames_ref.shape[2]
    width = 4 * cols
    small = channels // 4
    rows = mix_ref.shape[0]

    def remote(src, dst, send, recv, tm, col):
        return pltpu.make_async_remote_copy(
            src_ref=src, dst_ref=dst, send_sem=send, recv_sem=recv,
            device_id=(tm, col), device_id_type=MESH_ID,
        )

    barrier = pltpu.get_barrier_semaphore()
    for tm, col in ((left, q), (right, q), (after, q), (ahead, q), (me, sibling), (me, across)):
        pl.semaphore_signal(barrier, inc=1, device_id=(tm, col), device_id_type=MESH_ID)

    taken = 3 * in_channels
    row = lax.broadcasted_iota(jnp.int32, (24, rows), 0)
    column = lax.broadcasted_iota(jnp.int32, (24, rows), 1)
    picks = [
        jnp.where((row // 8 == kt) & (column == 8 * q + row % 8), 1.0, 0.0).astype(BF16)
        for kt in range(3)
    ]
    for tap_h in HEIGHTS:
        picked = None
        for kt in range(3):
            start = (kt * 3 + tap_h) * taken
            term = jnp.dot(
                picks[kt], up_ref[:, start : start + taken], preferred_element_type=F32
            )
            picked = term if picked is None else picked + term
        up_all[tap_h, me] = picked.astype(BF16)
    pl.semaphore_wait(barrier, 6)

    def ring(direction, kind, tap_h, step):
        owner = ring_tm((place + (n - step if direction == 0 else step)) % n, n)
        target = right if direction == 0 else left
        ref = up_all.at[tap_h, owner] if kind == 0 else mix_all.at[
            tap_h, pl.ds(pl.multiple_of(owner * rows, rows), rows)
        ]
        index = (direction, kind, tap_h, step)
        return remote(ref, ref, ring_send.at[index], ring_recv.at[index], target, q)

    def steps_of(direction, kind):
        return n // 2 if direction == kind else n // 2 - 1

    copies = {}

    def ring_start(kind, tap_h, step):
        for direction in range(2):
            if step < steps_of(direction, kind):
                copy = ring(direction, kind, tap_h, step)
                copies[direction, kind, tap_h, step] = copy
                copy.start()

    def ring_got(kind, tap_h, step):
        for direction in range(2):
            if step < steps_of(direction, kind):
                copies[direction, kind, tap_h, step].wait_recv()

    def ring_pass(kind, step):
        for tap_h in HEIGHTS:
            ring_got(kind, tap_h, step)
            ring_start(kind, tap_h, step + 1)

    own = [
        remote(src, dst, col_send.at[i], col_recv.at[i], me, col)
        for i, (src, dst, col) in enumerate((
            (frames_ref, frames_all.at[q, 2 : 2 + count], across),
            (cot_ref, cot_all.at[q, 0:times], across),
            (frames_ref, frames_all.at[q, 2 : 2 + count], sibling),
            (cot_ref, cot_all.at[q, 0:times], sibling),
        ))
    ]
    halos = [
        remote(frames_ref.at[count - 2 : count], frames_all.at[q, 0:2],
               halo_send.at[0], halo_recv.at[0], after, q),
        remote(frames_ref.at[0:1], frames_all.at[q, count + 2 : count + 3],
               halo_send.at[1], halo_recv.at[1], ahead, q),
        remote(cot_ref.at[0:3], cot_all.at[q, times : times + 3],
               halo_send.at[2], halo_recv.at[2], ahead, q),
    ]
    for copy in halos:
        copy.start()
    for tap_h in HEIGHTS:
        ring_start(0, tap_h, 0)
    for copy in own:
        copy.start()
    frames_all[q, 2 : 2 + count] = frames_ref[...]
    cot_all[q, 0:times] = cot_ref[...]

    source = lax.broadcasted_iota(jnp.int32, (channels, 2 * small), 0)
    lane = lax.broadcasted_iota(jnp.int32, (channels, 2 * small), 1)
    lane_low = lane % small
    wanted = rows * (lane_low // 8) + 8 * q + lane_low % 8
    first = jnp.where((source == wanted) & (lane < small), 1.0, 0.0).astype(BF16)
    second = jnp.where((source == wanted) & (lane >= small), 1.0, 0.0).astype(BF16)
    mine = pl.ds(pl.multiple_of(me * rows, rows), rows)
    for tap_h in HEIGHTS:
        order = [(kt * 3 + tap_h) * 3 + kw for kw in range(3) for kt in range(3)]
        for i in range(0, 10, 2):
            picked = jnp.dot(
                mix_ref[:, order[i] * channels : (order[i] + 1) * channels], first,
                preferred_element_type=F32,
            )
            if i < 8:
                picked = picked + jnp.dot(
                    mix_ref[:, order[i + 1] * channels : (order[i + 1] + 1) * channels], second,
                    preferred_element_type=F32,
                )
            mix_all[tap_h, mine, i * small : (i + 2) * small] = picked.astype(BF16)
    ring_pass(0, 0)
    for tap_h in HEIGHTS:
        ring_start(1, tap_h, 0)
    for copy in halos:
        copy.wait_recv()

    @pl.when(me == 0)
    def _():
        frames_all[q, 0:2] = jnp.zeros((2,) + frames_ref.shape[1:], BF16)

    @pl.when(me == n - 1)
    def _():
        frames_all[q, count + 2 : count + 3] = jnp.zeros((1,) + frames_ref.shape[1:], BF16)
        cot_all[q, times : times + 3] = jnp.zeros((3,) + cot_ref.shape[1:], BF16)

    edges = (
        frames_all.at[q, 0:2], frames_all.at[q, count + 2 : count + 3],
        cot_all.at[q, times : times + 3],
    )
    crossing = [
        remote(ref, ref, col_send.at[4 + i], col_recv.at[4 + i], me, across)
        for i, ref in enumerate(edges)
    ]
    beside = [
        remote(ref, ref, col_send.at[7 + i], col_recv.at[7 + i], me, sibling)
        for i, ref in enumerate(edges)
    ]
    for copy in crossing + beside:
        copy.start()
    ring_pass(0, 1)
    ring_pass(1, 0)
    ring_pass(0, 2)
    for copy in own[:2] + crossing:
        copy.wait_recv()
    passed = [
        remote(ref.at[across], ref.at[across], col_send.at[10 + i], col_recv.at[10 + i], me, sibling)
        for i, ref in enumerate((frames_all, cot_all))
    ]
    for copy in passed:
        copy.start()
    ring_pass(1, 1)
    for copy in own[2:] + beside + passed:
        copy.wait_recv()

    @pl.loop(0, count + 3)
    def _(t):
        for r in range(2):
            line = jnp.concatenate([frames_all[c, t, r].astype(F32) for c in range(4)], axis=0)
            at = pl.ds(pl.multiple_of(t * width, width), width)
            for kw in range(3):
                inputs[r, at, kw * in_channels : (kw + 1) * in_channels] = shifted(
                    line, kw - 1
                ).astype(BF16)

    @pl.loop(0, times + 3)
    def _(t):
        for r in range(2):
            line = jnp.concatenate([cot_all[c, t, r].astype(F32) for c in range(4)], axis=0)
            cots[r, pl.ds(pl.multiple_of(t * width, width), width)] = line.astype(BF16)

    for step, kh in enumerate(HEIGHTS):
        ring_got(0, kh, 3)
        for kt in range(3):
            part = up_all[kh, :, kt * 8 : kt * 8 + 8, :].astype(F32)
            up_taps[kh, kt * small : (kt + 1) * small] = part.reshape(small, taken).astype(BF16)
        up_taps[kh, 3 * small : 4 * small] = jnp.zeros((small, taken), BF16)
        for r in range(2):
            r_in = r + kh - 1
            if 0 <= r_in < 2:
                term = lax.dot_general(
                    inputs[r_in], up_taps[kh], (((1,), (1,)), ((), ())),
                    preferred_element_type=F32,
                )
                raw[r] = term if step == 0 else raw[r] + term
        if step == 0:
            ring_pass(1, 2)

    def frame(t):
        return slice(t * width, (t + 1) * width)

    for r in range(2):
        for t in range(times + 3):
            if t % 2 == 0:
                value = raw[r, frame(t // 2 + 1), 0:small] + raw[
                    r, frame(t // 2), 2 * small : 3 * small
                ]
            else:
                value = raw[r, frame((t + 1) // 2), small : 2 * small]
            before[r, frame(t)] = value
            active = value / (1.0 + jnp.exp(-value))
            hidden[r, frame(t)] = active.astype(BF16).astype(F32)

    for r in range(2):
        @pl.loop(0, times)
        def _(t):
            parts = []
            lines = [
                hidden[r, pl.ds(pl.multiple_of((t + kt) * width, width), width)] for kt in range(3)
            ]
            for kw in range(3):
                parts += [shifted(line, kw - 1) for line in lines]
            at = pl.ds(pl.multiple_of(t * width, width), width)
            for i, pair in enumerate(pairs(parts)):
                patches[r, at, i * 2 * small : (i + 1) * 2 * small] = pair

    def exchange(i, part, got):
        return [
            remote(part.at[target], got.at[j], out_send.at[i + j], out_recv.at[i + j], me, sibling)
            for j, target in enumerate((sibling, diagonal))
        ]

    out_d = exchange(0, part_d, got_d)
    for step, kh in enumerate(HEIGHTS):
        ring_got(1, kh, 3)
        for r in range(2):
            r_in = r + kh - 1
            if 0 <= r_in < 2:
                term = lax.dot_general(
                    patches[r_in], mix_all[kh], (((1,), (1,)), ((), ())),
                    preferred_element_type=F32,
                )
                decoding[r] = term if step == 0 else decoding[r] + term
        if step == 2:
            for r in range(2):
                for t in range(times):
                    for c in range(4):
                        low = t * width + c * cols
                        part_d[c, t, r] = decoding[r, low : low + cols].astype(BF16)
            for copy in out_d:
                copy.start()
        for r in range(2):
            r_in = r - kh + 1
            if 0 <= r_in < 2:
                term = jnp.dot(cots[r_in], mix_all[kh], preferred_element_type=F32)
                spread[r] = term if step == 0 else spread[r] + term

    def add_and_cross(i, part, got, summed, last, first_copies):
        for copy in first_copies:
            copy.wait_recv()
        summed[...] = (part[across].astype(F32) + got[1].astype(F32)).astype(BF16)
        copy = remote(summed, last, out_send.at[i + 2], out_recv.at[i + 2], me, across)
        copy.start()
        return copy

    def finish(part, got, last, copy, out):
        copy.wait_recv()
        out[...] = (part[q].astype(F32) + got[0].astype(F32) + last[...].astype(F32)).astype(BF16)

    cross_d = add_and_cross(0, part_d, got_d, sum_d, last_d, out_d)

    for r in range(2):
        lines = []
        for t in range(times + 1):
            gradient = None
            for kw in range(3):
                part = None
                for kt in range(3):
                    low = (kw * 3 + kt) * small
                    piece = spread[r, frame(t + 2 - kt), low : low + small]
                    part = piece if part is None else part + piece
                part = shifted(part, 1 - kw)
                gradient = part if gradient is None else gradient + part
            value = before[r, frame(t + 2)]
            sigma = 1.0 / (1.0 + jnp.exp(-value))
            gradient = gradient * sigma * (1.0 + value * (1.0 - sigma))
            hidden[r, frame(t)] = gradient.astype(BF16).astype(F32)

    for r in range(2):
        for i in range(count):
            lines = [hidden[r, frame(2 * i + kt)] for kt in range(3)]
            for kw in range(3):
                for j, pair in enumerate(pairs([shifted(line, 1 - kw) for line in lines])):
                    grads[r, kw, frame(i), j * 2 * small : (j + 1) * 2 * small] = pair

    out_g = []
    for r in range(2):
        total = None
        for r_in in range(2):
            kh = r - r_in + 1
            for kw in range(3):
                start = kw * in_channels
                term = jnp.dot(
                    grads[r_in, kw], up_taps[kh, :, start : start + in_channels],
                    preferred_element_type=F32,
                )
                total = term if total is None else total + term
        for i in range(count):
            for c in range(4):
                low = i * width + c * cols
                part_g[r, c, i] = total[low : low + cols].astype(BF16)
        out_g.append(exchange(3 + 3 * r, part_g.at[r], got_g.at[r]))
        for copy in out_g[r]:
            copy.start()
    finish(part_d, got_d, last_d, cross_d, decoded_ref)
    cross_g = [
        add_and_cross(
            3 + 3 * r, part_g.at[r], got_g.at[r], sum_g.at[r], last_g.at[r], out_g[r]
        )
        for r in range(2)
    ]
    for r in range(2):
        finish(part_g.at[r], got_g.at[r], last_g.at[r], cross_g[r], grad_ref.at[:, r])
    for copy in list(copies.values()) + halos + own + crossing + beside + passed:
        copy.wait_send()
    for copy in out_d + out_g[0] + out_g[1] + [cross_d] + cross_g:
        copy.wait_send()


def fused(frames, up_kernel, mix_kernel, cotangent):
    n = lax.axis_size("tm")
    count, height, cols, in_channels = frames.shape
    times, channels = cotangent.shape[0], cotangent.shape[3]
    width, small = 4 * cols, channels // 4
    up_rows, mix_rows = up_kernel.T, mix_kernel.T
    whole = pl.BlockSpec(memory_space=pltpu.VMEM)
    d_block, g_block = (times, height, cols, channels), (count, height, cols, in_channels)
    g_half = (count, cols, in_channels)
    dma = pltpu.SemaphoreType.DMA
    return pl.pallas_call(
        functools.partial(fused_kernel, n),
        out_shape=(
            jax.ShapeDtypeStruct(d_block, BF16),
            jax.ShapeDtypeStruct(g_block, BF16),
        ),
        in_specs=[whole] * 4,
        out_specs=(whole, whole),
        scratch_shapes=[
            pltpu.VMEM((3, n, 24, 3 * in_channels), BF16),
            pltpu.VMEM((3, channels, 10 * small), BF16),
            pltpu.VMEM((4, count + 3, height, cols, in_channels), BF16),
            pltpu.VMEM((4, times + 3, height, cols, channels), BF16),
            pltpu.VMEM((3, 4 * small, 3 * in_channels), BF16),
            pltpu.VMEM((2, (count + 3) * width, 3 * in_channels), BF16),
            pltpu.VMEM((2, (count + 3) * width, 4 * small), F32),
            pltpu.VMEM((2, (times + 3) * width, small), F32),
            pltpu.VMEM((2, (times + 3) * width, small), F32),
            pltpu.VMEM((2, times * width, 10 * small), BF16),
            pltpu.VMEM((2, times * width, channels), F32),
            pltpu.VMEM((2, (times + 3) * width, channels), BF16),
            pltpu.VMEM((2, (times + 3) * width, 10 * small), F32),
            pltpu.VMEM((2, 3, count * width, 4 * small), BF16),
            pltpu.VMEM((4,) + d_block, BF16),
            pltpu.VMEM((2, 4) + g_half, BF16),
            pltpu.VMEM((2,) + d_block, BF16),
            pltpu.VMEM((2, 2) + g_half, BF16),
            pltpu.VMEM(d_block, BF16),
            pltpu.VMEM((2,) + g_half, BF16),
            pltpu.VMEM(d_block, BF16),
            pltpu.VMEM((2,) + g_half, BF16),
            dma((2, 2, 3, n // 2)),
            dma((2, 2, 3, n // 2)),
            dma((3,)),
            dma((3,)),
            dma((12,)),
            dma((12,)),
            dma((9,)),
            dma((9,)),
        ],
        compiler_params=pltpu.CompilerParams(
            collective_id=0, has_side_effects=True, vmem_limit_bytes=56 * 1024 * 1024
        ),
    )(up_rows, mix_rows, frames, cotangent)


def solution(mesh):
    placed = (P("tm", None, "col", None), P(None, "tm"), P(None, "tm"), P("tm", None, "col", None))
    small = mesh.shape["tm"] == 8 and mesh.shape["col"] == 4
    return jax.shard_map(
        fused if small else shards,
        mesh=mesh,
        in_specs=placed,
        out_specs=(P("tm", None, "col", None), P("tm", None, "col", None)),
        check_vma=False,
    )
```

```python
import functools

import jax
import jax.numpy as jnp
from jax import lax
from jax.experimental import pallas as pl
from jax.experimental.pallas import tpu as pltpu
from jax.sharding import PartitionSpec as P


def with_halo(block, sides, width):
    for axis, dim in sides:
        count = lax.axis_size(axis)
        forward = [(i, i + 1) for i in range(count - 1)]
        backward = [(target, source) for source, target in forward]
        low = lax.ppermute(
            lax.slice_in_dim(block, block.shape[dim] - width, None, axis=dim), axis, forward
        )
        high = lax.ppermute(lax.slice_in_dim(block, 0, width, axis=dim), axis, backward)
        block = jnp.concatenate([low, block, high], axis=dim)
    return block


def from_behind(array, axis, by):
    devices = lax.axis_size(axis)
    pairs = [(i, i + by) for i in range(devices) if 0 <= i + by < devices]
    return lax.ppermute(array, axis, pairs)


def widen(field):
    return with_halo(field, (("col", 2),), 1)


def from_previous(field):
    return from_behind(field, "tm", 1)


def from_next(field):
    return from_behind(field, "tm", -1)


def forward_pass(kernel, produce):
    return produce(lax.all_gather(kernel, "tm", axis=1, tiled=True), jnp.int32(0))


def backward_pass(kernel, combine, initial):
    return combine(initial, lax.all_gather(kernel, "tm", axis=1, tiled=True), jnp.int32(0))


def pad_rows(field):
    return jnp.pad(field, ((0, 0), (1, 1), (0, 0), (0, 0)))


def window(padded, first, count, row_low, col_low, height, width):
    part = padded[first : first + count, row_low : row_low + height, col_low : col_low + width]
    return part.reshape(-1, part.shape[-1])


def transposed(rows, matrix):
    return lax.dot_general(
        rows, matrix, (((1,), (1,)), ((), ())), preferred_element_type=jnp.float32
    )


def shards(frames, up_kernel, mix_kernel, cotangent):
    frame_count, height, width, in_channels = frames.shape
    out_channels = mix_kernel.shape[0] // 27
    count = 2 * frame_count
    block = count * height * width
    widened = widen(frames)
    earlier = from_previous(widened[-1:])
    extended = pad_rows(jnp.concatenate((earlier, widened), axis=0))
    rows_in = extended.shape[0] - 1

    def up_columns(piece, start):
        taps = piece.reshape(3, 3, 3, in_channels, piece.shape[1])
        even = jnp.zeros((rows_in * height * width, piece.shape[1]), jnp.float32)
        odd = even
        for tap_h in range(3):
            for tap_w in range(3):
                current = window(extended, 1, rows_in, tap_h, tap_w, height, width)
                prior = window(extended, 0, rows_in, tap_h, tap_w, height, width)
                even = even + jnp.dot(
                    current, taps[0, tap_h, tap_w], preferred_element_type=jnp.float32
                )
                even = even + jnp.dot(
                    prior, taps[2, tap_h, tap_w], preferred_element_type=jnp.float32
                )
                odd = odd + jnp.dot(
                    current, taps[1, tap_h, tap_w], preferred_element_type=jnp.float32
                )
        stacked = jnp.stack(
            (even.reshape(rows_in, height * width, -1), odd.reshape(rows_in, height * width, -1)),
            axis=1,
        )
        return stacked.reshape(-1, piece.shape[1])

    before_all = forward_pass(up_kernel, up_columns).reshape(
        2 * rows_in, height, width, out_channels
    )
    hidden = jax.nn.silu(before_all).astype(jnp.bfloat16)
    earlier_hidden = from_previous(hidden[-2:])
    hidden_pad = pad_rows(widen(jnp.concatenate((earlier_hidden, hidden), axis=0)))
    cot_pad = pad_rows(widen(jnp.concatenate((cotangent, from_next(cotangent[:2])), axis=0)))

    def mix_forward(piece, start):
        taps = piece.reshape(3, 3, 3, out_channels, piece.shape[1])
        total = jnp.zeros((block, piece.shape[1]), jnp.float32)
        for tap_t in range(3):
            for tap_h in range(3):
                for tap_w in range(3):
                    total = total + jnp.dot(
                        window(hidden_pad, tap_t, count, tap_h, tap_w, height, width),
                        taps[tap_t, tap_h, tap_w],
                        preferred_element_type=jnp.float32,
                    )
        return total

    def mix_backward(piece):
        taps = piece.reshape(3, 3, 3, out_channels, piece.shape[1])
        total = jnp.zeros((block, out_channels), jnp.float32)
        for tap_t in range(3):
            for tap_h in range(3):
                for tap_w in range(3):
                    total = total + transposed(
                        window(cot_pad, 2 - tap_t, count, 2 - tap_h, 2 - tap_w, height, width),
                        taps[tap_t, tap_h, tap_w],
                    )
        return total

    empty = jnp.zeros((block, out_channels), jnp.float32)
    decoded_flat = forward_pass(mix_kernel, mix_forward)

    def accumulate(total, piece, start):
        return mix_backward(piece)

    hidden_grad = backward_pass(mix_kernel, accumulate, empty)
    flat_before = before_all.reshape(block, out_channels)
    sigma = jax.nn.sigmoid(flat_before)
    before_grad = (hidden_grad * sigma * (1.0 + flat_before * (1.0 - sigma))).astype(jnp.bfloat16)
    before_grad = before_grad.reshape(count, height, width, out_channels)
    grad_pad = pad_rows(widen(jnp.concatenate((before_grad, from_next(before_grad[:1])), axis=0)))
    evens = grad_pad[0::2]
    odds = grad_pad[1::2]

    def up_backward(total, piece, start):
        taps = piece.reshape(3, 3, 3, in_channels, piece.shape[1])
        for tap_h in range(3):
            for tap_w in range(3):
                total = total + transposed(
                    window(evens, 0, frame_count, 2 - tap_h, 2 - tap_w, height, width),
                    taps[0, tap_h, tap_w],
                )
                total = total + transposed(
                    window(odds, 0, frame_count, 2 - tap_h, 2 - tap_w, height, width),
                    taps[1, tap_h, tap_w],
                )
                total = total + transposed(
                    window(evens, 1, frame_count, 2 - tap_h, 2 - tap_w, height, width),
                    taps[2, tap_h, tap_w],
                )
        return total

    grad_start = jnp.zeros((frame_count * height * width, in_channels), jnp.float32)
    grad_total = backward_pass(up_kernel, up_backward, grad_start)
    decoded = decoded_flat.astype(jnp.bfloat16).reshape(count, height, width, out_channels)
    frames_grad = grad_total.astype(jnp.bfloat16).reshape(frame_count, height, width, in_channels)
    return (decoded, frames_grad)


MESH_ID = pl.DeviceIdType.MESH
BF16 = jnp.bfloat16
F32 = jnp.float32
TAPS_W = (1, 0, 2)


def shifted(rows, by):
    if by == 0:
        return rows
    count = rows.shape[0]
    place = lax.broadcasted_iota(jnp.int32, rows.shape, 0)
    if by < 0:
        return jnp.where(place == 0, 0.0, pltpu.roll(rows, 1, 0))
    return jnp.where(place == count - 1, 0.0, pltpu.roll(rows, count - 1, 0))


def ring_tm(place, n):
    half = place // (n // 2)
    level = place + half * (n - 1 - 2 * place)
    return 2 * level + half


def fused_kernel(
    n, up_ref, mix_ref, frames_ref, cot_ref, decoded_ref, grad_ref,
    up_all, mix_all, frames_all, cot_all, up_taps, inputs, mix_taps, raw, before, patches, decoding,
    cots, spread, gradient, grads, part_d, part_g, got_d, got_g, sum_d, sum_g, last_d, last_g,
    ring_send, ring_recv, halo_send, halo_recv, col_send, col_recv, out_send, out_recv,
):
    me, q = lax.axis_index("tm"), lax.axis_index("col")
    sibling = q + 1 - 2 * (q % 2)
    across = (q + 2) % 4
    diagonal = (sibling + 2) % 4
    level, side = me // 2, me % 2
    place = level + side * (n - 1 - 2 * level)
    right, left = ring_tm((place + 1) % n, n), ring_tm((place + n - 1) % n, n)
    after, ahead = (me + 1) % n, (me + n - 1) % n
    count, in_channels = frames_ref.shape[0], frames_ref.shape[3]
    times, channels = cot_ref.shape[0], cot_ref.shape[3]
    cols = frames_ref.shape[2]
    width = 4 * cols
    small = channels // 4
    rows = mix_ref.shape[0]

    def remote(src, dst, send, recv, tm, col):
        return pltpu.make_async_remote_copy(
            src_ref=src, dst_ref=dst, send_sem=send, recv_sem=recv,
            device_id=(tm, col), device_id_type=MESH_ID,
        )

    barrier = pltpu.get_barrier_semaphore()
    for tm, col in ((left, q), (right, q), (after, q), (ahead, q), (me, sibling), (me, across)):
        pl.semaphore_signal(barrier, inc=1, device_id=(tm, col), device_id_type=MESH_ID)

    row = lax.broadcasted_iota(jnp.int32, (24, rows), 0)
    column = lax.broadcasted_iota(jnp.int32, (24, rows), 1)
    picked = None
    for kt in range(3):
        pick = jnp.where((row // 8 == kt) & (column == 8 * q + row % 8), 1.0, 0.0).astype(BF16)
        term = jnp.dot(
            pick, up_ref[:, kt * 9 * in_channels : (kt + 1) * 9 * in_channels],
            preferred_element_type=F32,
        )
        picked = term if picked is None else picked + term
    for kw in range(3):
        for kh in range(3):
            low = (kh * 3 + kw) * in_channels
            up_all[kw, me, :, kh * in_channels : (kh + 1) * in_channels] = picked[
                :, low : low + in_channels
            ].astype(BF16)
    pl.semaphore_wait(barrier, 6)

    def ring(direction, kind, tap_w, step):
        owner = ring_tm((place + (n - step if direction == 0 else step)) % n, n)
        target = right if direction == 0 else left
        ref = up_all.at[tap_w, owner] if kind == 0 else mix_all.at[
            tap_w, pl.ds(pl.multiple_of(owner * rows, rows), rows)
        ]
        index = (direction, kind, tap_w, step)
        return remote(ref, ref, ring_send.at[index], ring_recv.at[index], target, q)

    def steps_of(direction, kind):
        return n // 2 if direction == kind else n // 2 - 1

    copies = {}

    def ring_start(kind, tap_w, step):
        for direction in range(2):
            if step < steps_of(direction, kind):
                copy = ring(direction, kind, tap_w, step)
                copies[direction, kind, tap_w, step] = copy
                copy.start()

    def ring_got(kind, tap_w, step):
        for direction in range(2):
            if step < steps_of(direction, kind):
                copies[direction, kind, tap_w, step].wait_recv()

    def ring_pass(kind, step):
        for tap_w in TAPS_W:
            ring_got(kind, tap_w, step)
            ring_start(kind, tap_w, step + 1)

    own = [
        remote(src, dst, col_send.at[i], col_recv.at[i], me, col)
        for i, (src, dst, col) in enumerate((
            (frames_ref, frames_all.at[q, 2 : 2 + count], across),
            (cot_ref, cot_all.at[q, 0:times], across),
            (frames_ref, frames_all.at[q, 2 : 2 + count], sibling),
            (cot_ref, cot_all.at[q, 0:times], sibling),
        ))
    ]
    halos = [
        remote(frames_ref.at[count - 2 : count], frames_all.at[q, 0:2],
               halo_send.at[0], halo_recv.at[0], after, q),
        remote(frames_ref.at[0:1], frames_all.at[q, count + 2 : count + 3],
               halo_send.at[1], halo_recv.at[1], ahead, q),
        remote(cot_ref.at[0:3], cot_all.at[q, times : times + 3],
               halo_send.at[2], halo_recv.at[2], ahead, q),
    ]

    @pl.when(me < n - 1)
    def _():
        halos[0].start()

    @pl.when(me > 0)
    def _():
        halos[1].start()
        halos[2].start()

    for tap_w in TAPS_W:
        ring_start(0, tap_w, 0)
    for copy in own:
        copy.start()
    frames_all[q, 2 : 2 + count] = frames_ref[...]
    cot_all[q, 0:times] = cot_ref[...]

    source = lax.broadcasted_iota(jnp.int32, (channels, 2 * small), 0)
    lane = lax.broadcasted_iota(jnp.int32, (channels, 2 * small), 1)
    lane_low = lane % small
    wanted = rows * (lane_low // 8) + 8 * q + lane_low % 8
    first = jnp.where((source == wanted) & (lane < small), 1.0, 0.0).astype(BF16)
    second = jnp.where((source == wanted) & (lane >= small), 1.0, 0.0).astype(BF16)
    mine = pl.ds(pl.multiple_of(me * rows, rows), rows)
    def taken(order, pick):
        lines = [
            mix_ref[:, ((kt * 3 + kh) * 3 + kw) * channels : ((kt * 3 + kh) * 3 + kw + 1) * channels]
            for kt, kh, kw in order
        ]
        return jnp.dot(jnp.concatenate(lines, axis=0), pick, preferred_element_type=F32)

    for kw in TAPS_W:
        low = taken([(0, 0, kw), (1, 0, kw), (2, 0, kw), (1, 2, kw)], first)
        high = taken([(0, 1, kw), (1, 1, kw), (2, 1, kw), (0, 2, kw), (2, 2, kw)], second)
        for i in range(5):
            part = high[i * rows : (i + 1) * rows]
            if i < 4:
                part = part + low[i * rows : (i + 1) * rows]
            mix_all[kw, mine, i * 2 * small : (i + 1) * 2 * small] = part.astype(BF16)
    ring_pass(0, 0)
    for tap_w in TAPS_W:
        ring_start(1, tap_w, 0)

    @pl.when(me > 0)
    def _():
        halos[0].wait_recv()

    @pl.when(me == 0)
    def _():
        frames_all[q, 0:2] = jnp.zeros((2,) + frames_ref.shape[1:], BF16)

    @pl.when(me < n - 1)
    def _():
        halos[1].wait_recv()
        halos[2].wait_recv()

    @pl.when(me == n - 1)
    def _():
        frames_all[q, count + 2 : count + 3] = jnp.zeros((1,) + frames_ref.shape[1:], BF16)
        cot_all[q, times : times + 3] = jnp.zeros((3,) + cot_ref.shape[1:], BF16)

    edges = (
        frames_all.at[q, 0:2], frames_all.at[q, count + 2 : count + 3],
        cot_all.at[q, times : times + 3],
    )
    crossing = [
        remote(ref, ref, col_send.at[4 + i], col_recv.at[4 + i], me, across)
        for i, ref in enumerate(edges)
    ]
    beside = [
        remote(ref, ref, col_send.at[7 + i], col_recv.at[7 + i], me, sibling)
        for i, ref in enumerate(edges)
    ]
    for copy in crossing + beside:
        copy.start()
    ring_pass(0, 1)
    ring_pass(1, 0)
    ring_pass(0, 2)
    for copy in own[:2] + crossing:
        copy.wait_recv()
    passed = [
        remote(ref.at[across], ref.at[across], col_send.at[10 + i], col_recv.at[10 + i], me, sibling)
        for i, ref in enumerate((frames_all, cot_all))
    ]
    for copy in passed:
        copy.start()
    ring_pass(1, 1)
    for copy in own[2:] + beside + passed:
        copy.wait_recv()

    @pl.loop(0, count + 3)
    def _(t):
        at = pl.ds(pl.multiple_of(t * width, width), width)
        for r in range(2):
            line = jnp.concatenate([frames_all[c, t, r].astype(F32) for c in range(4)], axis=0)
            for kw in range(3):
                inputs[kw, at, r * in_channels : (r + 1) * in_channels] = shifted(
                    line, kw - 1
                ).astype(BF16)

    @pl.loop(0, times + 3)
    def _(t):
        at = pl.ds(pl.multiple_of(t * width, width), width)
        for r in range(2):
            line = jnp.concatenate([cot_all[c, t, r].astype(F32) for c in range(4)], axis=0)
            cots[at, r * channels : (r + 1) * channels] = line.astype(BF16)

    pair = 2 * small
    for step, kw in enumerate(TAPS_W):
        ring_got(0, kw, 3)
        for kt in range(3):
            for kh in range(3):
                part = up_all[
                    kw, :, kt * 8 : kt * 8 + 8, kh * in_channels : (kh + 1) * in_channels
                ].astype(F32)
                part = part.reshape(small, in_channels).astype(BF16)
                for r in range(2):
                    r_in = r + kh - 1
                    if 0 <= r_in < 2:
                        up_taps[
                            kw, kt * pair + r * small : kt * pair + (r + 1) * small,
                            r_in * in_channels : (r_in + 1) * in_channels,
                        ] = part
        term = lax.dot_general(
            inputs[kw], up_taps[kw], (((1,), (1,)), ((), ())), preferred_element_type=F32
        )
        raw[...] = term if step == 0 else raw[...] + term
        if step == 0:
            ring_pass(1, 2)

    def frame(t):
        return slice(t * width, (t + 1) * width)

    for t in range(times + 3):
        if t % 2 == 0:
            value = raw[frame(t // 2 + 1), 0:pair] + raw[frame(t // 2), 2 * pair : 3 * pair]
        else:
            value = raw[frame((t + 1) // 2), pair : 2 * pair]
        before[frame(t)] = value
        active = (value / (1.0 + jnp.exp(-value))).astype(BF16)
        for kw in range(3):
            moved = shifted(active.astype(F32), kw - 1).astype(BF16)
            for kt in range(3):
                if 0 <= t - kt < times:
                    patches[kw, frame(t - kt), kt * pair : (kt + 1) * pair] = moved

    def exchange(i, part, got):
        return [
            remote(part.at[target], got.at[j], out_send.at[i + j], out_recv.at[i + j], me, sibling)
            for j, target in enumerate((sibling, diagonal))
        ]

    out_d = exchange(0, part_d, got_d)
    lane = lax.broadcasted_iota(jnp.int32, (channels, pair), 1)
    for step, kw in enumerate(TAPS_W):
        ring_got(1, kw, 3)
        last = mix_all[kw, :, 3 * pair : 4 * pair].astype(F32)
        tails = [last, pltpu.roll(last, small, 1), mix_all[kw, :, 4 * pair : 5 * pair].astype(F32)]
        for kt in range(3):
            block = mix_all[kw, :, kt * pair : (kt + 1) * pair]
            turned = pltpu.roll(block.astype(F32), small, 1)
            mix_taps[kw, channels : 2 * channels, kt * pair : (kt + 1) * pair] = block
            mix_taps[kw, 0:channels, kt * pair : (kt + 1) * pair] = jnp.where(
                lane < small, turned, tails[kt]
            ).astype(BF16)
        term = lax.dot_general(
            patches[kw], mix_taps[kw], (((1,), (1,)), ((), ())), preferred_element_type=F32
        )
        if step < 2:
            decoding[...] = term if step == 0 else decoding[...] + term
        else:
            term = term + decoding[...]
            for r in range(2):
                for t in range(times):
                    for c in range(4):
                        low = t * width + c * cols
                        part_d[c, t, r] = term[
                            low : low + cols, r * channels : (r + 1) * channels
                        ].astype(BF16)
            for copy in out_d:
                copy.start()
        spread[...] = jnp.dot(cots[...], mix_taps[kw], preferred_element_type=F32)
        for t in range(times + 1):
            part = None
            for kt in range(3):
                piece = spread[frame(t + 2 - kt), kt * pair : (kt + 1) * pair]
                part = piece if part is None else part + piece
            part = shifted(part, 1 - kw)
            gradient[frame(t)] = part if step == 0 else gradient[frame(t)] + part

    def add_and_cross(i, part, got, summed, last, first_copies):
        for copy in first_copies:
            copy.wait_recv()
        summed[...] = (part[across].astype(F32) + got[1].astype(F32)).astype(BF16)
        copy = remote(summed, last, out_send.at[i + 2], out_recv.at[i + 2], me, across)
        copy.start()
        return copy

    def finish(part, got, last, copy, out):
        copy.wait_recv()
        out[...] = (part[q].astype(F32) + got[0].astype(F32) + last[...].astype(F32)).astype(BF16)

    cross_d = add_and_cross(0, part_d, got_d, sum_d, last_d, out_d)

    for t in range(times + 1):
        value = before[frame(t + 2)]
        sigma = 1.0 / (1.0 + jnp.exp(-value))
        line = gradient[frame(t)] * sigma * (1.0 + value * (1.0 - sigma))
        line = line.astype(BF16).astype(F32)
        for kw in range(3):
            moved = shifted(line, 1 - kw).astype(BF16)
            for kt in range(3):
                if (t - kt) % 2 == 0 and 0 <= t - kt < 2 * count:
                    grads[kw, frame((t - kt) // 2), kt * pair : (kt + 1) * pair] = moved

    out_g = []
    for r in range(2):
        total = None
        for kw in range(3):
            term = jnp.dot(
                grads[kw], up_taps[kw, :, r * in_channels : (r + 1) * in_channels],
                preferred_element_type=F32,
            )
            total = term if total is None else total + term
        for i in range(count):
            for c in range(4):
                low = i * width + c * cols
                part_g[r, c, i] = total[low : low + cols].astype(BF16)
        out_g.append(exchange(3 + 3 * r, part_g.at[r], got_g.at[r]))
        for copy in out_g[r]:
            copy.start()
    finish(part_d, got_d, last_d, cross_d, decoded_ref)
    cross_g = [
        add_and_cross(
            3 + 3 * r, part_g.at[r], got_g.at[r], sum_g.at[r], last_g.at[r], out_g[r]
        )
        for r in range(2)
    ]
    for r in range(2):
        finish(part_g.at[r], got_g.at[r], last_g.at[r], cross_g[r], grad_ref.at[:, r])

    @pl.when(me < n - 1)
    def _():
        halos[0].wait_send()

    @pl.when(me > 0)
    def _():
        halos[1].wait_send()
        halos[2].wait_send()

    for copy in list(copies.values()) + own + crossing + beside + passed:
        copy.wait_send()
    for copy in out_d + out_g[0] + out_g[1] + [cross_d] + cross_g:
        copy.wait_send()


def fused(frames, up_kernel, mix_kernel, cotangent):
    n = lax.axis_size("tm")
    count, height, cols, in_channels = frames.shape
    times, channels = cotangent.shape[0], cotangent.shape[3]
    width, small = 4 * cols, channels // 4
    up_rows, mix_rows = up_kernel.T, mix_kernel.T
    whole = pl.BlockSpec(memory_space=pltpu.VMEM)
    d_block, g_block = (times, height, cols, channels), (count, height, cols, in_channels)
    g_half = (count, cols, in_channels)
    dma = pltpu.SemaphoreType.DMA
    return pl.pallas_call(
        functools.partial(fused_kernel, n),
        out_shape=(
            jax.ShapeDtypeStruct(d_block, BF16),
            jax.ShapeDtypeStruct(g_block, BF16),
        ),
        in_specs=[whole] * 4,
        out_specs=(whole, whole),
        scratch_shapes=[
            pltpu.VMEM((3, n, 24, 3 * in_channels), BF16),
            pltpu.VMEM((3, channels, 10 * small), BF16),
            pltpu.VMEM((4, count + 3, height, cols, in_channels), BF16),
            pltpu.VMEM((4, times + 3, height, cols, channels), BF16),
            pltpu.VMEM((3, 6 * small, 2 * in_channels), BF16),
            pltpu.VMEM((3, (count + 3) * width, 2 * in_channels), BF16),
            pltpu.VMEM((3, 2 * channels, 6 * small), BF16),
            pltpu.VMEM(((count + 3) * width, 6 * small), F32),
            pltpu.VMEM(((times + 3) * width, 2 * small), F32),
            pltpu.VMEM((3, times * width, 6 * small), BF16),
            pltpu.VMEM((times * width, 2 * channels), F32),
            pltpu.VMEM(((times + 3) * width, 2 * channels), BF16),
            pltpu.VMEM(((times + 3) * width, 6 * small), F32),
            pltpu.VMEM(((times + 1) * width, 2 * small), F32),
            pltpu.VMEM((3, count * width, 6 * small), BF16),
            pltpu.VMEM((4,) + d_block, BF16),
            pltpu.VMEM((2, 4) + g_half, BF16),
            pltpu.VMEM((2,) + d_block, BF16),
            pltpu.VMEM((2, 2) + g_half, BF16),
            pltpu.VMEM(d_block, BF16),
            pltpu.VMEM((2,) + g_half, BF16),
            pltpu.VMEM(d_block, BF16),
            pltpu.VMEM((2,) + g_half, BF16),
            dma((2, 2, 3, n // 2)),
            dma((2, 2, 3, n // 2)),
            dma((3,)),
            dma((3,)),
            dma((12,)),
            dma((12,)),
            dma((9,)),
            dma((9,)),
        ],
        compiler_params=pltpu.CompilerParams(
            collective_id=0, has_side_effects=True, vmem_limit_bytes=56 * 1024 * 1024
        ),
    )(up_rows, mix_rows, frames, cotangent)


def solution(mesh):
    placed = (P("tm", None, "col", None), P(None, "tm"), P(None, "tm"), P("tm", None, "col", None))
    small = mesh.shape["tm"] == 8 and mesh.shape["col"] == 4
    return jax.shard_map(
        fused if small else shards,
        mesh=mesh,
        in_specs=placed,
        out_specs=(P("tm", None, "col", None), P("tm", None, "col", None)),
        check_vma=False,
    )
```

```python
import functools

import jax
import jax.numpy as jnp
from jax import lax
from jax.experimental import pallas as pl
from jax.experimental.pallas import tpu as pltpu
from jax.sharding import PartitionSpec as P


def with_halo(block, sides, width):
    for axis, dim in sides:
        count = lax.axis_size(axis)
        forward = [(i, i + 1) for i in range(count - 1)]
        backward = [(target, source) for source, target in forward]
        low = lax.ppermute(
            lax.slice_in_dim(block, block.shape[dim] - width, None, axis=dim), axis, forward
        )
        high = lax.ppermute(lax.slice_in_dim(block, 0, width, axis=dim), axis, backward)
        block = jnp.concatenate([low, block, high], axis=dim)
    return block


def from_behind(array, axis, by):
    devices = lax.axis_size(axis)
    pairs = [(i, i + by) for i in range(devices) if 0 <= i + by < devices]
    return lax.ppermute(array, axis, pairs)


def widen(field):
    return with_halo(field, (("col", 2),), 1)


def from_previous(field):
    return from_behind(field, "tm", 1)


def from_next(field):
    return from_behind(field, "tm", -1)


def forward_pass(kernel, produce):
    return produce(lax.all_gather(kernel, "tm", axis=1, tiled=True), jnp.int32(0))


def backward_pass(kernel, combine, initial):
    return combine(initial, lax.all_gather(kernel, "tm", axis=1, tiled=True), jnp.int32(0))


def pad_rows(field):
    return jnp.pad(field, ((0, 0), (1, 1), (0, 0), (0, 0)))


def window(padded, first, count, row_low, col_low, height, width):
    part = padded[first : first + count, row_low : row_low + height, col_low : col_low + width]
    return part.reshape(-1, part.shape[-1])


def transposed(rows, matrix):
    return lax.dot_general(
        rows, matrix, (((1,), (1,)), ((), ())), preferred_element_type=jnp.float32
    )


def shards(frames, up_kernel, mix_kernel, cotangent):
    frame_count, height, width, in_channels = frames.shape
    out_channels = mix_kernel.shape[0] // 27
    count = 2 * frame_count
    block = count * height * width
    widened = widen(frames)
    earlier = from_previous(widened[-1:])
    extended = pad_rows(jnp.concatenate((earlier, widened), axis=0))
    rows_in = extended.shape[0] - 1

    def up_columns(piece, start):
        taps = piece.reshape(3, 3, 3, in_channels, piece.shape[1])
        even = jnp.zeros((rows_in * height * width, piece.shape[1]), jnp.float32)
        odd = even
        for tap_h in range(3):
            for tap_w in range(3):
                current = window(extended, 1, rows_in, tap_h, tap_w, height, width)
                prior = window(extended, 0, rows_in, tap_h, tap_w, height, width)
                even = even + jnp.dot(
                    current, taps[0, tap_h, tap_w], preferred_element_type=jnp.float32
                )
                even = even + jnp.dot(
                    prior, taps[2, tap_h, tap_w], preferred_element_type=jnp.float32
                )
                odd = odd + jnp.dot(
                    current, taps[1, tap_h, tap_w], preferred_element_type=jnp.float32
                )
        stacked = jnp.stack(
            (even.reshape(rows_in, height * width, -1), odd.reshape(rows_in, height * width, -1)),
            axis=1,
        )
        return stacked.reshape(-1, piece.shape[1])

    before_all = forward_pass(up_kernel, up_columns).reshape(
        2 * rows_in, height, width, out_channels
    )
    hidden = jax.nn.silu(before_all).astype(jnp.bfloat16)
    earlier_hidden = from_previous(hidden[-2:])
    hidden_pad = pad_rows(widen(jnp.concatenate((earlier_hidden, hidden), axis=0)))
    cot_pad = pad_rows(widen(jnp.concatenate((cotangent, from_next(cotangent[:2])), axis=0)))

    def mix_forward(piece, start):
        taps = piece.reshape(3, 3, 3, out_channels, piece.shape[1])
        total = jnp.zeros((block, piece.shape[1]), jnp.float32)
        for tap_t in range(3):
            for tap_h in range(3):
                for tap_w in range(3):
                    total = total + jnp.dot(
                        window(hidden_pad, tap_t, count, tap_h, tap_w, height, width),
                        taps[tap_t, tap_h, tap_w],
                        preferred_element_type=jnp.float32,
                    )
        return total

    def mix_backward(piece):
        taps = piece.reshape(3, 3, 3, out_channels, piece.shape[1])
        total = jnp.zeros((block, out_channels), jnp.float32)
        for tap_t in range(3):
            for tap_h in range(3):
                for tap_w in range(3):
                    total = total + transposed(
                        window(cot_pad, 2 - tap_t, count, 2 - tap_h, 2 - tap_w, height, width),
                        taps[tap_t, tap_h, tap_w],
                    )
        return total

    empty = jnp.zeros((block, out_channels), jnp.float32)
    decoded_flat = forward_pass(mix_kernel, mix_forward)

    def accumulate(total, piece, start):
        return mix_backward(piece)

    hidden_grad = backward_pass(mix_kernel, accumulate, empty)
    flat_before = before_all.reshape(block, out_channels)
    sigma = jax.nn.sigmoid(flat_before)
    before_grad = (hidden_grad * sigma * (1.0 + flat_before * (1.0 - sigma))).astype(jnp.bfloat16)
    before_grad = before_grad.reshape(count, height, width, out_channels)
    grad_pad = pad_rows(widen(jnp.concatenate((before_grad, from_next(before_grad[:1])), axis=0)))
    evens = grad_pad[0::2]
    odds = grad_pad[1::2]

    def up_backward(total, piece, start):
        taps = piece.reshape(3, 3, 3, in_channels, piece.shape[1])
        for tap_h in range(3):
            for tap_w in range(3):
                total = total + transposed(
                    window(evens, 0, frame_count, 2 - tap_h, 2 - tap_w, height, width),
                    taps[0, tap_h, tap_w],
                )
                total = total + transposed(
                    window(odds, 0, frame_count, 2 - tap_h, 2 - tap_w, height, width),
                    taps[1, tap_h, tap_w],
                )
                total = total + transposed(
                    window(evens, 1, frame_count, 2 - tap_h, 2 - tap_w, height, width),
                    taps[2, tap_h, tap_w],
                )
        return total

    grad_start = jnp.zeros((frame_count * height * width, in_channels), jnp.float32)
    grad_total = backward_pass(up_kernel, up_backward, grad_start)
    decoded = decoded_flat.astype(jnp.bfloat16).reshape(count, height, width, out_channels)
    frames_grad = grad_total.astype(jnp.bfloat16).reshape(frame_count, height, width, in_channels)
    return (decoded, frames_grad)


MESH_ID = pl.DeviceIdType.MESH
BF16 = jnp.bfloat16
F32 = jnp.float32
TAPS_W = (1, 0, 2)


def shifted(rows, by):
    if by == 0:
        return rows
    count = rows.shape[0]
    place = lax.broadcasted_iota(jnp.int32, rows.shape, 0)
    if by < 0:
        return jnp.where(place == 0, 0.0, pltpu.roll(rows, 1, 0))
    return jnp.where(place == count - 1, 0.0, pltpu.roll(rows, count - 1, 0))


def ring_tm(place, n):
    half = place // (n // 2)
    level = place + half * (n - 1 - 2 * place)
    return 2 * level + half


def fused_kernel(
    n, up_ref, mix_ref, frames_ref, cot_ref, decoded_ref, grad_ref,
    up_all, mix_all, frames_all, cot_all, up_taps, inputs, mix_taps, raw, before, patches, decoding,
    cots, spread, gradient, grads, part_d, part_g, got_d, got_g, sum_d, sum_g, last_d, last_g,
    ring_send, ring_recv, halo_send, halo_recv, col_send, col_recv, out_send, out_recv,
):
    me, q = lax.axis_index("tm"), lax.axis_index("col")
    sibling = q + 1 - 2 * (q % 2)
    across = (q + 2) % 4
    diagonal = (sibling + 2) % 4
    level, side = me // 2, me % 2
    place = level + side * (n - 1 - 2 * level)
    right, left = ring_tm((place + 1) % n, n), ring_tm((place + n - 1) % n, n)
    after, ahead = (me + 1) % n, (me + n - 1) % n
    count, in_channels = frames_ref.shape[0], frames_ref.shape[3]
    times, channels = cot_ref.shape[0], cot_ref.shape[3]
    cols = frames_ref.shape[2]
    width = 4 * cols
    small = channels // 4
    rows = mix_ref.shape[0]

    def remote(src, dst, send, recv, tm, col):
        return pltpu.make_async_remote_copy(
            src_ref=src, dst_ref=dst, send_sem=send, recv_sem=recv,
            device_id=(tm, col), device_id_type=MESH_ID,
        )

    barrier = pltpu.get_barrier_semaphore()
    for tm, col in ((left, q), (right, q), (after, q), (ahead, q), (me, sibling), (me, across)):
        pl.semaphore_signal(barrier, inc=1, device_id=(tm, col), device_id_type=MESH_ID)

    row = lax.broadcasted_iota(jnp.int32, (24, rows), 0)
    column = lax.broadcasted_iota(jnp.int32, (24, rows), 1)
    picked = None
    for kt in range(3):
        pick = jnp.where((row // 8 == kt) & (column == 8 * q + row % 8), 1.0, 0.0).astype(BF16)
        term = jnp.dot(
            pick, up_ref[:, kt * 9 * in_channels : (kt + 1) * 9 * in_channels],
            preferred_element_type=F32,
        )
        picked = term if picked is None else picked + term
    for kw in range(3):
        for kh in range(3):
            low = (kh * 3 + kw) * in_channels
            up_all[kw, me, :, kh * in_channels : (kh + 1) * in_channels] = picked[
                :, low : low + in_channels
            ].astype(BF16)
    pl.semaphore_wait(barrier, 6)

    def ring(direction, kind, tap_w, step):
        owner = ring_tm((place + (n - step if direction == 0 else step)) % n, n)
        target = right if direction == 0 else left
        ref = up_all.at[tap_w, owner] if kind == 0 else mix_all.at[
            tap_w, pl.ds(pl.multiple_of(owner * rows, rows), rows),
            0 : (8 if tap_w == 0 else 10) * small,
        ]
        index = (direction, kind, tap_w, step)
        return remote(ref, ref, ring_send.at[index], ring_recv.at[index], target, q)

    def steps_of(direction, kind):
        return n // 2 if direction == kind else n // 2 - 1

    copies = {}

    def ring_start(kind, tap_w, step):
        for direction in range(2):
            if step < steps_of(direction, kind):
                copy = ring(direction, kind, tap_w, step)
                copies[direction, kind, tap_w, step] = copy
                copy.start()

    def ring_got(kind, tap_w, step):
        for direction in range(2):
            if step < steps_of(direction, kind):
                copies[direction, kind, tap_w, step].wait_recv()

    def ring_pass(kind, step):
        for tap_w in TAPS_W:
            ring_got(kind, tap_w, step)
            ring_start(kind, tap_w, step + 1)

    own = [
        remote(src, dst, col_send.at[i], col_recv.at[i], me, col)
        for i, (src, dst, col) in enumerate((
            (frames_ref, frames_all.at[q, 2 : 2 + count], across),
            (cot_ref, cot_all.at[q, 0:times], across),
            (frames_ref, frames_all.at[q, 2 : 2 + count], sibling),
            (cot_ref, cot_all.at[q, 0:times], sibling),
        ))
    ]
    halos = [
        remote(frames_ref.at[count - 2 : count], frames_all.at[q, 0:2],
               halo_send.at[0], halo_recv.at[0], after, q),
        remote(frames_ref.at[0:1], frames_all.at[q, count + 2 : count + 3],
               halo_send.at[1], halo_recv.at[1], ahead, q),
        remote(cot_ref.at[0:3], cot_all.at[q, times : times + 3],
               halo_send.at[2], halo_recv.at[2], ahead, q),
    ]

    @pl.when(me < n - 1)
    def _():
        halos[0].start()

    @pl.when(me > 0)
    def _():
        halos[1].start()
        halos[2].start()

    for tap_w in TAPS_W:
        ring_start(0, tap_w, 0)
    for copy in own:
        copy.start()
    frames_all[q, 2 : 2 + count] = frames_ref[...]
    cot_all[q, 0:times] = cot_ref[...]

    source = lax.broadcasted_iota(jnp.int32, (channels, 2 * small), 0)
    lane = lax.broadcasted_iota(jnp.int32, (channels, 2 * small), 1)
    lane_low = lane % small
    wanted = rows * (lane_low // 8) + 8 * q + lane_low % 8
    first = jnp.where((source == wanted) & (lane < small), 1.0, 0.0).astype(BF16)
    second = jnp.where((source == wanted) & (lane >= small), 1.0, 0.0).astype(BF16)
    mine = pl.ds(pl.multiple_of(me * rows, rows), rows)
    def taken(order, pick):
        lines = [
            mix_ref[:, ((kt * 3 + kh) * 3 + kw) * channels : ((kt * 3 + kh) * 3 + kw + 1) * channels]
            for kt, kh, kw in order
        ]
        return jnp.dot(jnp.concatenate(lines, axis=0), pick, preferred_element_type=F32)

    for kw in TAPS_W:
        lows = [(0, 0, kw), (1, 0, kw), (2, 0, kw), (1, 2, kw)]
        highs = [(0, 1, kw), (1, 1, kw), (2, 1, kw), (0, 2, kw)]
        if kw > 0:
            lows, highs = lows + [(2, 2, 0)], highs + [(2, 2, kw)]
        low, high = taken(lows, first), taken(highs, second)
        for i in range(len(lows)):
            part = low[i * rows : (i + 1) * rows] + high[i * rows : (i + 1) * rows]
            mix_all[kw, mine, i * 2 * small : (i + 1) * 2 * small] = part.astype(BF16)
    ring_pass(0, 0)
    for tap_w in TAPS_W:
        ring_start(1, tap_w, 0)

    @pl.when(me > 0)
    def _():
        halos[0].wait_recv()

    @pl.when(me == 0)
    def _():
        frames_all[q, 0:2] = jnp.zeros((2,) + frames_ref.shape[1:], BF16)

    @pl.when(me < n - 1)
    def _():
        halos[1].wait_recv()
        halos[2].wait_recv()

    @pl.when(me == n - 1)
    def _():
        frames_all[q, count + 2 : count + 3] = jnp.zeros((1,) + frames_ref.shape[1:], BF16)
        cot_all[q, times : times + 3] = jnp.zeros((3,) + cot_ref.shape[1:], BF16)

    edges = (
        frames_all.at[q, 0:2], frames_all.at[q, count + 2 : count + 3],
        cot_all.at[q, times : times + 3],
    )
    crossing = [
        remote(ref, ref, col_send.at[4 + i], col_recv.at[4 + i], me, across)
        for i, ref in enumerate(edges)
    ]
    beside = [
        remote(ref, ref, col_send.at[7 + i], col_recv.at[7 + i], me, sibling)
        for i, ref in enumerate(edges)
    ]
    for copy in crossing + beside:
        copy.start()
    ring_pass(0, 1)
    ring_pass(1, 0)
    ring_pass(0, 2)
    for copy in own[:2] + crossing:
        copy.wait_recv()
    passed = [
        remote(ref.at[across], ref.at[across], col_send.at[10 + i], col_recv.at[10 + i], me, sibling)
        for i, ref in enumerate((frames_all, cot_all))
    ]
    for copy in passed:
        copy.start()
    ring_pass(1, 1)
    for copy in own[2:] + beside + passed:
        copy.wait_recv()

    @pl.loop(0, count + 3)
    def _(t):
        at = pl.ds(pl.multiple_of(t * width, width), width)
        for r in range(2):
            line = jnp.concatenate([frames_all[c, t, r].astype(F32) for c in range(4)], axis=0)
            for kw in range(3):
                inputs[kw, at, r * in_channels : (r + 1) * in_channels] = shifted(
                    line, kw - 1
                ).astype(BF16)

    @pl.loop(0, times + 3)
    def _(t):
        at = pl.ds(pl.multiple_of(t * width, width), width)
        for r in range(2):
            line = jnp.concatenate([cot_all[c, t, r].astype(F32) for c in range(4)], axis=0)
            cots[at, r * channels : (r + 1) * channels] = line.astype(BF16)

    pair = 2 * small
    for step, kw in enumerate(TAPS_W):
        ring_got(0, kw, 3)
        for kt in range(3):
            for kh in range(3):
                part = up_all[
                    kw, :, kt * 8 : kt * 8 + 8, kh * in_channels : (kh + 1) * in_channels
                ].astype(F32)
                part = part.reshape(small, in_channels).astype(BF16)
                for r in range(2):
                    r_in = r + kh - 1
                    if 0 <= r_in < 2:
                        up_taps[
                            kw, kt * pair + r * small : kt * pair + (r + 1) * small,
                            r_in * in_channels : (r_in + 1) * in_channels,
                        ] = part
        term = lax.dot_general(
            inputs[kw], up_taps[kw], (((1,), (1,)), ((), ())), preferred_element_type=F32
        )
        raw[...] = term if step == 0 else raw[...] + term
        if step == 0:
            ring_pass(1, 2)

    def frame(t):
        return slice(t * width, (t + 1) * width)

    for t in range(times + 3):
        if t % 2 == 0:
            value = raw[frame(t // 2 + 1), 0:pair] + raw[frame(t // 2), 2 * pair : 3 * pair]
        else:
            value = raw[frame((t + 1) // 2), pair : 2 * pair]
        before[frame(t)] = value
        active = (value / (1.0 + jnp.exp(-value))).astype(BF16)
        for kw in range(3):
            moved = shifted(active.astype(F32), kw - 1).astype(BF16)
            for kt in range(3):
                if 0 <= t - kt < times:
                    patches[kw, frame(t - kt), kt * pair : (kt + 1) * pair] = moved

    def exchange(i, part, got):
        return [
            remote(part.at[target], got.at[j], out_send.at[i + j], out_recv.at[i + j], me, sibling)
            for j, target in enumerate((sibling, diagonal))
        ]

    out_d = exchange(0, part_d, got_d)
    lane = lax.broadcasted_iota(jnp.int32, (channels, pair), 1)
    for step, kw in enumerate(TAPS_W):
        ring_got(1, kw, 3)
        last = mix_all[kw, :, 3 * pair : 4 * pair].astype(F32)
        final = mix_all[max(kw, 1), :, 4 * pair : 5 * pair].astype(F32)
        if kw == 0:
            final = pltpu.roll(final, small, 1)
        tails = [last, pltpu.roll(last, small, 1), final]
        for kt in range(3):
            block = mix_all[kw, :, kt * pair : (kt + 1) * pair]
            turned = pltpu.roll(block.astype(F32), small, 1)
            mix_taps[kw, channels : 2 * channels, kt * pair : (kt + 1) * pair] = block
            mix_taps[kw, 0:channels, kt * pair : (kt + 1) * pair] = jnp.where(
                lane < small, turned, tails[kt]
            ).astype(BF16)
        term = lax.dot_general(
            patches[kw], mix_taps[kw], (((1,), (1,)), ((), ())), preferred_element_type=F32
        )
        if step < 2:
            decoding[...] = term if step == 0 else decoding[...] + term
        else:
            term = term + decoding[...]
            for r in range(2):
                for t in range(times):
                    for c in range(4):
                        low = t * width + c * cols
                        part_d[c, t, r] = term[
                            low : low + cols, r * channels : (r + 1) * channels
                        ].astype(BF16)
            for copy in out_d:
                copy.start()
        spread[...] = jnp.dot(cots[...], mix_taps[kw], preferred_element_type=F32)
        for t in range(times + 1):
            part = None
            for kt in range(3):
                piece = spread[frame(t + 2 - kt), kt * pair : (kt + 1) * pair]
                part = piece if part is None else part + piece
            part = shifted(part, 1 - kw)
            gradient[frame(t)] = part if step == 0 else gradient[frame(t)] + part

    def add_and_cross(i, part, got, summed, last, first_copies):
        for copy in first_copies:
            copy.wait_recv()
        summed[...] = (part[across].astype(F32) + got[1].astype(F32)).astype(BF16)
        copy = remote(summed, last, out_send.at[i + 2], out_recv.at[i + 2], me, across)
        copy.start()
        return copy

    def finish(part, got, last, copy, out):
        copy.wait_recv()
        out[...] = (part[q].astype(F32) + got[0].astype(F32) + last[...].astype(F32)).astype(BF16)

    for t in range(times + 1):
        value = before[frame(t + 2)]
        sigma = 1.0 / (1.0 + jnp.exp(-value))
        line = gradient[frame(t)] * sigma * (1.0 + value * (1.0 - sigma))
        line = line.astype(BF16).astype(F32)
        for kw in range(3):
            moved = shifted(line, 1 - kw).astype(BF16)
            for kt in range(3):
                if (t - kt) % 2 == 0 and 0 <= t - kt < 2 * count:
                    grads[kw, frame((t - kt) // 2), kt * pair : (kt + 1) * pair] = moved

    cross_d = add_and_cross(0, part_d, got_d, sum_d, last_d, out_d)

    out_g = []
    for r in range(2):
        total = None
        for kw in range(3):
            term = jnp.dot(
                grads[kw], up_taps[kw, :, r * in_channels : (r + 1) * in_channels],
                preferred_element_type=F32,
            )
            total = term if total is None else total + term
        for i in range(count):
            for c in range(4):
                low = i * width + c * cols
                part_g[r, c, i] = total[low : low + cols].astype(BF16)
        out_g.append(exchange(3 + 3 * r, part_g.at[r], got_g.at[r]))
        for copy in out_g[r]:
            copy.start()
    finish(part_d, got_d, last_d, cross_d, decoded_ref)
    cross_g = [
        add_and_cross(
            3 + 3 * r, part_g.at[r], got_g.at[r], sum_g.at[r], last_g.at[r], out_g[r]
        )
        for r in range(2)
    ]
    for r in range(2):
        finish(part_g.at[r], got_g.at[r], last_g.at[r], cross_g[r], grad_ref.at[:, r])

    @pl.when(me < n - 1)
    def _():
        halos[0].wait_send()

    @pl.when(me > 0)
    def _():
        halos[1].wait_send()
        halos[2].wait_send()

    for copy in list(copies.values()) + own + crossing + beside + passed:
        copy.wait_send()
    for copy in out_d + out_g[0] + out_g[1] + [cross_d] + cross_g:
        copy.wait_send()


def place(made_d, made_g, decoded_ref, grad_ref, sems):
    copies = [
        pltpu.make_async_copy(made_d, decoded_ref, sems.at[0]),
        pltpu.make_async_copy(made_g, grad_ref, sems.at[1]),
    ]
    for copy in copies:
        copy.start()
    for copy in copies:
        copy.wait()


def fused(frames, up_kernel, mix_kernel, cotangent):
    n = lax.axis_size("tm")
    count, height, cols, in_channels = frames.shape
    times, channels = cotangent.shape[0], cotangent.shape[3]
    width, small = 4 * cols, channels // 4
    up_rows, mix_rows = up_kernel.T, mix_kernel.T
    whole = pl.BlockSpec(memory_space=pltpu.VMEM)
    d_block, g_block = (times, height, cols, channels), (count, height, cols, in_channels)
    g_half = (count, cols, in_channels)
    dma = pltpu.SemaphoreType.DMA
    made = pl.pallas_call(
        functools.partial(fused_kernel, n),
        out_shape=(
            jax.ShapeDtypeStruct(d_block, BF16),
            jax.ShapeDtypeStruct(g_block, BF16),
        ),
        in_specs=[whole] * 4,
        out_specs=(whole, whole),
        scratch_shapes=[
            pltpu.VMEM((3, n, 24, 3 * in_channels), BF16),
            pltpu.VMEM((3, channels, 10 * small), BF16),
            pltpu.VMEM((4, count + 3, height, cols, in_channels), BF16),
            pltpu.VMEM((4, times + 3, height, cols, channels), BF16),
            pltpu.VMEM((3, 6 * small, 2 * in_channels), BF16),
            pltpu.VMEM((3, (count + 3) * width, 2 * in_channels), BF16),
            pltpu.VMEM((3, 2 * channels, 6 * small), BF16),
            pltpu.VMEM(((count + 3) * width, 6 * small), F32),
            pltpu.VMEM(((times + 3) * width, 2 * small), F32),
            pltpu.VMEM((3, times * width, 6 * small), BF16),
            pltpu.VMEM((times * width, 2 * channels), F32),
            pltpu.VMEM(((times + 3) * width, 2 * channels), BF16),
            pltpu.VMEM(((times + 3) * width, 6 * small), F32),
            pltpu.VMEM(((times + 1) * width, 2 * small), F32),
            pltpu.VMEM((3, count * width, 6 * small), BF16),
            pltpu.VMEM((4,) + d_block, BF16),
            pltpu.VMEM((2, 4) + g_half, BF16),
            pltpu.VMEM((2,) + d_block, BF16),
            pltpu.VMEM((2, 2) + g_half, BF16),
            pltpu.VMEM(d_block, BF16),
            pltpu.VMEM((2,) + g_half, BF16),
            pltpu.VMEM(d_block, BF16),
            pltpu.VMEM((2,) + g_half, BF16),
            dma((2, 2, 3, n // 2)),
            dma((2, 2, 3, n // 2)),
            dma((3,)),
            dma((3,)),
            dma((12,)),
            dma((12,)),
            dma((9,)),
            dma((9,)),
        ],
        compiler_params=pltpu.CompilerParams(
            collective_id=0, has_side_effects=True, vmem_limit_bytes=56 * 1024 * 1024
        ),
    )(up_rows, mix_rows, frames, cotangent)
    anywhere = pl.BlockSpec(memory_space=pltpu.HBM)
    return pl.pallas_call(
        place,
        out_shape=tuple(jax.ShapeDtypeStruct(array.shape, array.dtype) for array in made),
        in_specs=[anywhere] * 2,
        out_specs=(anywhere, anywhere),
        scratch_shapes=[dma((2,))],
    )(*made)


def solution(mesh):
    placed = (P("tm", None, "col", None), P(None, "tm"), P(None, "tm"), P("tm", None, "col", None))
    small = mesh.shape["tm"] == 8 and mesh.shape["col"] == 4
    return jax.shard_map(
        fused if small else shards,
        mesh=mesh,
        in_specs=placed,
        out_specs=(P("tm", None, "col", None), P("tm", None, "col", None)),
        check_vma=False,
    )
```

```python
import functools

import jax
import jax.numpy as jnp
from jax import lax
from jax.experimental import pallas as pl
from jax.experimental.pallas import tpu as pltpu
from jax.sharding import PartitionSpec as P


def with_halo(block, sides, width):
    for axis, dim in sides:
        count = lax.axis_size(axis)
        forward = [(i, i + 1) for i in range(count - 1)]
        backward = [(target, source) for source, target in forward]
        low = lax.ppermute(
            lax.slice_in_dim(block, block.shape[dim] - width, None, axis=dim), axis, forward
        )
        high = lax.ppermute(lax.slice_in_dim(block, 0, width, axis=dim), axis, backward)
        block = jnp.concatenate([low, block, high], axis=dim)
    return block


def from_behind(array, axis, by):
    devices = lax.axis_size(axis)
    pairs = [(i, i + by) for i in range(devices) if 0 <= i + by < devices]
    return lax.ppermute(array, axis, pairs)


def widen(field):
    return with_halo(field, (("col", 2),), 1)


def from_previous(field):
    return from_behind(field, "tm", 1)


def from_next(field):
    return from_behind(field, "tm", -1)


def forward_pass(kernel, produce):
    return produce(lax.all_gather(kernel, "tm", axis=1, tiled=True), jnp.int32(0))


def backward_pass(kernel, combine, initial):
    return combine(initial, lax.all_gather(kernel, "tm", axis=1, tiled=True), jnp.int32(0))


def pad_rows(field):
    return jnp.pad(field, ((0, 0), (1, 1), (0, 0), (0, 0)))


def window(padded, first, count, row_low, col_low, height, width):
    part = padded[first : first + count, row_low : row_low + height, col_low : col_low + width]
    return part.reshape(-1, part.shape[-1])


def transposed(rows, matrix):
    return lax.dot_general(
        rows, matrix, (((1,), (1,)), ((), ())), preferred_element_type=jnp.float32
    )


def shards(frames, up_kernel, mix_kernel, cotangent):
    frame_count, height, width, in_channels = frames.shape
    out_channels = mix_kernel.shape[0] // 27
    count = 2 * frame_count
    block = count * height * width
    widened = widen(frames)
    earlier = from_previous(widened[-1:])
    extended = pad_rows(jnp.concatenate((earlier, widened), axis=0))
    rows_in = extended.shape[0] - 1

    def up_columns(piece, start):
        taps = piece.reshape(3, 3, 3, in_channels, piece.shape[1])
        even = jnp.zeros((rows_in * height * width, piece.shape[1]), jnp.float32)
        odd = even
        for tap_h in range(3):
            for tap_w in range(3):
                current = window(extended, 1, rows_in, tap_h, tap_w, height, width)
                prior = window(extended, 0, rows_in, tap_h, tap_w, height, width)
                even = even + jnp.dot(
                    current, taps[0, tap_h, tap_w], preferred_element_type=jnp.float32
                )
                even = even + jnp.dot(
                    prior, taps[2, tap_h, tap_w], preferred_element_type=jnp.float32
                )
                odd = odd + jnp.dot(
                    current, taps[1, tap_h, tap_w], preferred_element_type=jnp.float32
                )
        stacked = jnp.stack(
            (even.reshape(rows_in, height * width, -1), odd.reshape(rows_in, height * width, -1)),
            axis=1,
        )
        return stacked.reshape(-1, piece.shape[1])

    before_all = forward_pass(up_kernel, up_columns).reshape(
        2 * rows_in, height, width, out_channels
    )
    hidden = jax.nn.silu(before_all).astype(jnp.bfloat16)
    earlier_hidden = from_previous(hidden[-2:])
    hidden_pad = pad_rows(widen(jnp.concatenate((earlier_hidden, hidden), axis=0)))
    cot_pad = pad_rows(widen(jnp.concatenate((cotangent, from_next(cotangent[:2])), axis=0)))

    def mix_forward(piece, start):
        taps = piece.reshape(3, 3, 3, out_channels, piece.shape[1])
        total = jnp.zeros((block, piece.shape[1]), jnp.float32)
        for tap_t in range(3):
            for tap_h in range(3):
                for tap_w in range(3):
                    total = total + jnp.dot(
                        window(hidden_pad, tap_t, count, tap_h, tap_w, height, width),
                        taps[tap_t, tap_h, tap_w],
                        preferred_element_type=jnp.float32,
                    )
        return total

    def mix_backward(piece):
        taps = piece.reshape(3, 3, 3, out_channels, piece.shape[1])
        total = jnp.zeros((block, out_channels), jnp.float32)
        for tap_t in range(3):
            for tap_h in range(3):
                for tap_w in range(3):
                    total = total + transposed(
                        window(cot_pad, 2 - tap_t, count, 2 - tap_h, 2 - tap_w, height, width),
                        taps[tap_t, tap_h, tap_w],
                    )
        return total

    empty = jnp.zeros((block, out_channels), jnp.float32)
    decoded_flat = forward_pass(mix_kernel, mix_forward)

    def accumulate(total, piece, start):
        return mix_backward(piece)

    hidden_grad = backward_pass(mix_kernel, accumulate, empty)
    flat_before = before_all.reshape(block, out_channels)
    sigma = jax.nn.sigmoid(flat_before)
    before_grad = (hidden_grad * sigma * (1.0 + flat_before * (1.0 - sigma))).astype(jnp.bfloat16)
    before_grad = before_grad.reshape(count, height, width, out_channels)
    grad_pad = pad_rows(widen(jnp.concatenate((before_grad, from_next(before_grad[:1])), axis=0)))
    evens = grad_pad[0::2]
    odds = grad_pad[1::2]

    def up_backward(total, piece, start):
        taps = piece.reshape(3, 3, 3, in_channels, piece.shape[1])
        for tap_h in range(3):
            for tap_w in range(3):
                total = total + transposed(
                    window(evens, 0, frame_count, 2 - tap_h, 2 - tap_w, height, width),
                    taps[0, tap_h, tap_w],
                )
                total = total + transposed(
                    window(odds, 0, frame_count, 2 - tap_h, 2 - tap_w, height, width),
                    taps[1, tap_h, tap_w],
                )
                total = total + transposed(
                    window(evens, 1, frame_count, 2 - tap_h, 2 - tap_w, height, width),
                    taps[2, tap_h, tap_w],
                )
        return total

    grad_start = jnp.zeros((frame_count * height * width, in_channels), jnp.float32)
    grad_total = backward_pass(up_kernel, up_backward, grad_start)
    decoded = decoded_flat.astype(jnp.bfloat16).reshape(count, height, width, out_channels)
    frames_grad = grad_total.astype(jnp.bfloat16).reshape(frame_count, height, width, in_channels)
    return (decoded, frames_grad)


MESH_ID = pl.DeviceIdType.MESH
BF16 = jnp.bfloat16
F32 = jnp.float32


def shifted(rows, by):
    if by == 0:
        return rows
    count = rows.shape[0]
    place = lax.broadcasted_iota(jnp.int32, rows.shape, 0)
    if by < 0:
        return jnp.where(place == 0, 0.0, pltpu.roll(rows, 1, 0))
    return jnp.where(place == count - 1, 0.0, pltpu.roll(rows, count - 1, 0))


def ring_tm(place, n):
    half = place // (n // 2)
    level = place + half * (n - 1 - 2 * place)
    return 2 * level + half


def fused_kernel(
    n, up_ref, mix_ref, frames_ref, cot_ref, decoded_ref, grad_ref,
    up_all, mix_all, frames_all, cot_all, up_taps, inputs, mix_taps, raw, before, patches, decoding,
    cots, spread, gradient, grads, summed, part_d, part_g, got_d, got_g, sum_d, sum_g, last_d, last_g,
    ring_send, ring_recv, halo_send, halo_recv, col_send, col_recv, out_send, out_recv,
):
    me, q = lax.axis_index("tm"), lax.axis_index("col")
    sibling = q + 1 - 2 * (q % 2)
    across = (q + 2) % 4
    diagonal = (sibling + 2) % 4
    level, side = me // 2, me % 2
    place = level + side * (n - 1 - 2 * level)
    right, left = ring_tm((place + 1) % n, n), ring_tm((place + n - 1) % n, n)
    after, ahead = (me + 1) % n, (me + n - 1) % n
    count, in_channels = frames_ref.shape[0], frames_ref.shape[3]
    times, channels = cot_ref.shape[0], cot_ref.shape[3]
    cols = frames_ref.shape[2]
    width = 4 * cols
    small = channels // 4
    rows = mix_ref.shape[0]

    def remote(src, dst, send, recv, tm, col):
        return pltpu.make_async_remote_copy(
            src_ref=src, dst_ref=dst, send_sem=send, recv_sem=recv,
            device_id=(tm, col), device_id_type=MESH_ID,
        )

    barrier = pltpu.get_barrier_semaphore()
    for tm, col in ((left, q), (right, q), (after, q), (ahead, q), (me, sibling), (me, across)):
        pl.semaphore_signal(barrier, inc=1, device_id=(tm, col), device_id_type=MESH_ID)

    row = lax.broadcasted_iota(jnp.int32, (24, rows), 0)
    column = lax.broadcasted_iota(jnp.int32, (24, rows), 1)
    picked = None
    for kt in range(3):
        pick = jnp.where((row // 8 == kt) & (column == 8 * q + row % 8), 1.0, 0.0).astype(BF16)
        term = jnp.dot(
            pick, up_ref[:, kt * 9 * in_channels : (kt + 1) * 9 * in_channels],
            preferred_element_type=F32,
        )
        picked = term if picked is None else picked + term
    for kw in range(3):
        for kh in range(3):
            low = (kh * 3 + kw) * in_channels
            up_all[kw, me, :, kh * in_channels : (kh + 1) * in_channels] = picked[
                :, low : low + in_channels
            ].astype(BF16)
    pl.semaphore_wait(barrier, 6)

    def ring(direction, kind, tap_w, step, short):
        owner = ring_tm((place + (n - step if direction == 0 else step)) % n, n)
        target = right if direction == 0 else left
        ref = up_all.at[tap_w, owner] if kind == 0 else mix_all.at[
            tap_w, pl.ds(pl.multiple_of(owner * rows, rows), rows),
            0 : (8 if short else 10) * small,
        ]
        index = (direction, kind, tap_w, step)
        return remote(ref, ref, ring_send.at[index], ring_recv.at[index], target, q)

    def steps_of(direction, kind):
        return n // 2 if direction == kind else n // 2 - 1

    copies = {}

    def ring_start(kind, tap_w, step):
        for direction in range(2):
            if step < steps_of(direction, kind):
                copy = ring(direction, kind, tap_w, step, tap_w == 1)
                copies[direction, kind, tap_w, step] = copy
                copy.start()

    def ring_got(kind, tap_w, step):
        for direction in range(2):
            if step < steps_of(direction, kind):
                copies[direction, kind, tap_w, step].wait_recv()

    def ring_pass(kind, step):
        for tap_w in range(3):
            ring_got(kind, tap_w, step)
            ring_start(kind, tap_w, step + 1)

    own = [
        remote(src, dst, col_send.at[i], col_recv.at[i], me, col)
        for i, (src, dst, col) in enumerate((
            (frames_ref, frames_all.at[q, 2 : 2 + count], across),
            (cot_ref, cot_all.at[q, 0:times], across),
            (frames_ref, frames_all.at[q, 2 : 2 + count], sibling),
            (cot_ref, cot_all.at[q, 0:times], sibling),
        ))
    ]
    halos = [
        remote(frames_ref.at[count - 2 : count], frames_all.at[q, 0:2],
               halo_send.at[0], halo_recv.at[0], after, q),
        remote(frames_ref.at[0:1], frames_all.at[q, count + 2 : count + 3],
               halo_send.at[1], halo_recv.at[1], ahead, q),
        remote(cot_ref.at[0:3], cot_all.at[q, times : times + 3],
               halo_send.at[2], halo_recv.at[2], ahead, q),
    ]

    @pl.when(me < n - 1)
    def _():
        halos[0].start()

    @pl.when(me > 0)
    def _():
        halos[1].start()
        halos[2].start()

    for tap_w in range(3):
        ring_start(0, tap_w, 0)
    for copy in own:
        copy.start()
    frames_all[q, 2 : 2 + count] = frames_ref[...]
    cot_all[q, 0:times] = cot_ref[...]

    source = lax.broadcasted_iota(jnp.int32, (channels, 2 * small), 0)
    lane = lax.broadcasted_iota(jnp.int32, (channels, 2 * small), 1)
    lane_low = lane % small
    wanted = rows * (lane_low // 8) + 8 * q + lane_low % 8
    first = jnp.where((source == wanted) & (lane < small), 1.0, 0.0).astype(BF16)
    second = jnp.where((source == wanted) & (lane >= small), 1.0, 0.0).astype(BF16)
    mine = pl.ds(pl.multiple_of(me * rows, rows), rows)
    def taken(order, pick):
        lines = [
            mix_ref[:, ((kt * 3 + kh) * 3 + kw) * channels : ((kt * 3 + kh) * 3 + kw + 1) * channels]
            for kt, kh, kw in order
        ]
        return jnp.dot(jnp.concatenate(lines, axis=0), pick, preferred_element_type=F32)

    for kw in range(3):
        lows = [(0, 0, kw), (1, 0, kw), (2, 0, kw), (1, 2, kw)]
        highs = [(0, 1, kw), (1, 1, kw), (2, 1, kw), (0, 2, kw)]
        if kw != 1:
            lows, highs = lows + [(2, 2, 1)], highs + [(2, 2, kw)]
        low, high = taken(lows, first), taken(highs, second)
        for i in range(len(lows)):
            part = low[i * rows : (i + 1) * rows] + high[i * rows : (i + 1) * rows]
            mix_all[kw, mine, i * 2 * small : (i + 1) * 2 * small] = part.astype(BF16)
    ring_pass(0, 0)
    for tap_w in range(3):
        ring_start(1, tap_w, 0)

    @pl.when(me > 0)
    def _():
        halos[0].wait_recv()

    @pl.when(me == 0)
    def _():
        frames_all[q, 0:2] = jnp.zeros((2,) + frames_ref.shape[1:], BF16)

    @pl.when(me < n - 1)
    def _():
        halos[1].wait_recv()
        halos[2].wait_recv()

    @pl.when(me == n - 1)
    def _():
        frames_all[q, count + 2 : count + 3] = jnp.zeros((1,) + frames_ref.shape[1:], BF16)
        cot_all[q, times : times + 3] = jnp.zeros((3,) + cot_ref.shape[1:], BF16)

    edges = (
        frames_all.at[q, 0:2], frames_all.at[q, count + 2 : count + 3],
        cot_all.at[q, times : times + 3],
    )
    crossing = [
        remote(ref, ref, col_send.at[4 + i], col_recv.at[4 + i], me, across)
        for i, ref in enumerate(edges)
    ]
    beside = [
        remote(ref, ref, col_send.at[7 + i], col_recv.at[7 + i], me, sibling)
        for i, ref in enumerate(edges)
    ]
    for copy in crossing + beside:
        copy.start()
    ring_pass(0, 1)
    ring_pass(1, 0)
    ring_pass(0, 2)
    for copy in own[:2] + crossing:
        copy.wait_recv()
    passed = [
        remote(ref.at[across], ref.at[across], col_send.at[10 + i], col_recv.at[10 + i], me, sibling)
        for i, ref in enumerate((frames_all, cot_all))
    ]
    for copy in passed:
        copy.start()
    ring_pass(1, 1)
    for copy in own[2:] + beside + passed:
        copy.wait_recv()

    @pl.loop(0, count + 3)
    def _(t):
        at = pl.ds(pl.multiple_of(t * width, width), width)
        for r in range(2):
            line = jnp.concatenate([frames_all[c, t, r].astype(F32) for c in range(4)], axis=0)
            for kw in range(3):
                inputs[kw, at, r * in_channels : (r + 1) * in_channels] = shifted(
                    line, kw - 1
                ).astype(BF16)

    @pl.loop(0, times + 3)
    def _(t):
        at = pl.ds(pl.multiple_of(t * width, width), width)
        for r in range(2):
            line = jnp.concatenate([cot_all[c, t, r].astype(F32) for c in range(4)], axis=0)
            cots[at, r * channels : (r + 1) * channels] = line.astype(BF16)

    pair = 2 * small
    for kw in range(3):
        ring_got(0, kw, 3)
    ring_pass(1, 2)

    def frame(t):
        return pl.ds(pl.multiple_of(t * width, width), width)

    raw[...] = jnp.zeros_like(raw)

    @pl.loop(0, 3)
    def _(kw):
        for kt in range(3):
            for kh in range(3):
                part = up_all[
                    kw, :, kt * 8 : kt * 8 + 8, kh * in_channels : (kh + 1) * in_channels
                ].astype(F32)
                part = part.reshape(small, in_channels).astype(BF16)
                for r in range(2):
                    r_in = r + kh - 1
                    if 0 <= r_in < 2:
                        up_taps[
                            kw, kt * pair + r * small : kt * pair + (r + 1) * small,
                            r_in * in_channels : (r_in + 1) * in_channels,
                        ] = part
        raw[...] += lax.dot_general(
            inputs[kw], up_taps[kw], (((1,), (1,)), ((), ())), preferred_element_type=F32
        )

    def keep(t, value):
        before[frame(t)] = value
        active = (value / (1.0 + jnp.exp(-value))).astype(BF16).astype(F32)
        for kw in range(3):
            moved = shifted(active, kw - 1).astype(BF16)
            for kt in range(3):
                patches[kw, frame(t - kt + 2), kt * pair : (kt + 1) * pair] = moved

    @pl.loop(0, count + 2)
    def _(i):
        keep(2 * i, raw[frame(i + 1), 0:pair] + raw[frame(i), 2 * pair : 3 * pair])

    @pl.loop(0, count + 1)
    def _(i):
        keep(2 * i + 1, raw[frame(i + 1), pair : 2 * pair])

    def exchange(i, part, got):
        return [
            remote(part.at[target], got.at[j], out_send.at[i + j], out_recv.at[i + j], me, sibling)
            for j, target in enumerate((sibling, diagonal))
        ]

    out_d = exchange(0, part_d, got_d)
    lane = lax.broadcasted_iota(jnp.int32, (channels, pair), 1)
    decoding[...] = jnp.zeros_like(decoding)
    gradient[...] = jnp.zeros_like(gradient)

    @pl.loop(0, 3)
    def _(kw):
        @pl.when(kw == 1)
        def _():
            ring(1, 1, kw, 3, True).wait_recv()

        @pl.when(kw != 1)
        def _():
            ring(1, 1, kw, 3, False).wait_recv()

        last = mix_all[kw, :, 3 * pair : 4 * pair].astype(F32)
        final = mix_all[kw - kw % 2, :, 4 * pair : 5 * pair].astype(F32)
        final = jnp.where(kw == 1, pltpu.roll(final, small, 1), final)
        tails = [last, pltpu.roll(last, small, 1), final]
        for kt in range(3):
            block = mix_all[kw, :, kt * pair : (kt + 1) * pair]
            turned = pltpu.roll(block.astype(F32), small, 1)
            mix_taps[channels : 2 * channels, kt * pair : (kt + 1) * pair] = block
            mix_taps[0:channels, kt * pair : (kt + 1) * pair] = jnp.where(
                lane < small, turned, tails[kt]
            ).astype(BF16)
        decoding[...] += lax.dot_general(
            patches[kw, 2 * width : (times + 2) * width], mix_taps[...],
            (((1,), (1,)), ((), ())), preferred_element_type=F32,
        )
        spread[...] = jnp.dot(cots[...], mix_taps[...], preferred_element_type=F32)

        @pl.loop(0, times + 1)
        def _(t):
            part = None
            for kt in range(3):
                piece = spread[frame(t + 2 - kt), kt * pair : (kt + 1) * pair]
                part = piece if part is None else part + piece
            part = jnp.where(
                kw == 0, shifted(part, 1), jnp.where(kw == 1, part, shifted(part, -1))
            )
            gradient[frame(t)] += part

    @pl.loop(0, times)
    def _(t):
        for r in range(2):
            for c in range(4):
                at = pl.ds(pl.multiple_of(t * width + c * cols, cols), cols)
                part_d[c, t, r] = decoding[at, r * channels : (r + 1) * channels].astype(BF16)

    for copy in out_d:
        copy.start()

    def add_and_cross(i, part, got, sums, last, first_copies):
        for copy in first_copies:
            copy.wait_recv()
        sums[...] = (part[across].astype(F32) + got[1].astype(F32)).astype(BF16)
        copy = remote(sums, last, out_send.at[i + 2], out_recv.at[i + 2], me, across)
        copy.start()
        return copy

    def finish(part, got, last, copy, out):
        copy.wait_recv()
        out[...] = (part[q].astype(F32) + got[0].astype(F32) + last[...].astype(F32)).astype(BF16)

    @pl.loop(0, times + 1)
    def _(t):
        value = before[frame(t + 2)]
        sigma = 1.0 / (1.0 + jnp.exp(-value))
        line = gradient[frame(t)] * sigma * (1.0 + value * (1.0 - sigma))
        gradient[frame(t)] = line.astype(BF16).astype(F32)

    @pl.loop(0, count)
    def _(i):
        for kt in range(3):
            line = gradient[frame(2 * i + kt)]
            for kw in range(3):
                grads[kw, frame(i), kt * pair : (kt + 1) * pair] = shifted(line, 1 - kw).astype(BF16)

    cross_d = add_and_cross(0, part_d, got_d, sum_d, last_d, out_d)

    out_g = []
    for r in range(2):
        summed[...] = jnp.zeros_like(summed)

        @pl.loop(0, 3)
        def _(kw):
            summed[...] += jnp.dot(
                grads[kw], up_taps[kw, :, r * in_channels : (r + 1) * in_channels],
                preferred_element_type=F32,
            )

        @pl.loop(0, count)
        def _(i):
            for c in range(4):
                at = pl.ds(pl.multiple_of(i * width + c * cols, cols), cols)
                part_g[r, c, i] = summed[at].astype(BF16)

        out_g.append(exchange(3 + 3 * r, part_g.at[r], got_g.at[r]))
        for copy in out_g[r]:
            copy.start()
    finish(part_d, got_d, last_d, cross_d, decoded_ref)
    cross_g = [
        add_and_cross(
            3 + 3 * r, part_g.at[r], got_g.at[r], sum_g.at[r], last_g.at[r], out_g[r]
        )
        for r in range(2)
    ]
    for r in range(2):
        finish(part_g.at[r], got_g.at[r], last_g.at[r], cross_g[r], grad_ref.at[:, r])

    @pl.when(me < n - 1)
    def _():
        halos[0].wait_send()

    @pl.when(me > 0)
    def _():
        halos[1].wait_send()
        halos[2].wait_send()

    for copy in list(copies.values()) + own + crossing + beside + passed:
        copy.wait_send()
    for copy in out_d + out_g[0] + out_g[1] + [cross_d] + cross_g:
        copy.wait_send()


def place(made_d, made_g, decoded_ref, grad_ref):
    decoded_ref[...] = made_d[...]
    grad_ref[...] = made_g[...]


def fused(frames, up_kernel, mix_kernel, cotangent):
    n = lax.axis_size("tm")
    count, height, cols, in_channels = frames.shape
    times, channels = cotangent.shape[0], cotangent.shape[3]
    width, small = 4 * cols, channels // 4
    up_rows, mix_rows = up_kernel.T, mix_kernel.T
    whole = pl.BlockSpec(memory_space=pltpu.VMEM)
    d_block, g_block = (times, height, cols, channels), (count, height, cols, in_channels)
    g_half = (count, cols, in_channels)
    dma = pltpu.SemaphoreType.DMA
    made = pl.pallas_call(
        functools.partial(fused_kernel, n),
        out_shape=(
            jax.ShapeDtypeStruct(d_block, BF16),
            jax.ShapeDtypeStruct(g_block, BF16),
        ),
        in_specs=[whole] * 4,
        out_specs=(whole, whole),
        scratch_shapes=[
            pltpu.VMEM((3, n, 24, 3 * in_channels), BF16),
            pltpu.VMEM((3, channels, 10 * small), BF16),
            pltpu.VMEM((4, count + 3, height, cols, in_channels), BF16),
            pltpu.VMEM((4, times + 3, height, cols, channels), BF16),
            pltpu.VMEM((3, 6 * small, 2 * in_channels), BF16),
            pltpu.VMEM((3, (count + 3) * width, 2 * in_channels), BF16),
            pltpu.VMEM((2 * channels, 6 * small), BF16),
            pltpu.VMEM(((count + 3) * width, 6 * small), F32),
            pltpu.VMEM(((times + 3) * width, 2 * small), F32),
            pltpu.VMEM((3, (times + 5) * width, 6 * small), BF16),
            pltpu.VMEM((times * width, 2 * channels), F32),
            pltpu.VMEM(((times + 3) * width, 2 * channels), BF16),
            pltpu.VMEM(((times + 3) * width, 6 * small), F32),
            pltpu.VMEM(((times + 1) * width, 2 * small), F32),
            pltpu.VMEM((3, count * width, 6 * small), BF16),
            pltpu.VMEM((count * width, in_channels), F32),
            pltpu.VMEM((4,) + d_block, BF16),
            pltpu.VMEM((2, 4) + g_half, BF16),
            pltpu.VMEM((2,) + d_block, BF16),
            pltpu.VMEM((2, 2) + g_half, BF16),
            pltpu.VMEM(d_block, BF16),
            pltpu.VMEM((2,) + g_half, BF16),
            pltpu.VMEM(d_block, BF16),
            pltpu.VMEM((2,) + g_half, BF16),
            dma((2, 2, 3, n // 2)),
            dma((2, 2, 3, n // 2)),
            dma((3,)),
            dma((3,)),
            dma((12,)),
            dma((12,)),
            dma((9,)),
            dma((9,)),
        ],
        compiler_params=pltpu.CompilerParams(
            collective_id=0, has_side_effects=True, vmem_limit_bytes=56 * 1024 * 1024
        ),
    )(up_rows, mix_rows, frames, cotangent)
    return pl.pallas_call(
        place,
        out_shape=tuple(jax.ShapeDtypeStruct(array.shape, array.dtype) for array in made),
        in_specs=[whole] * 2,
        out_specs=(whole, whole),
    )(*made)


def solution(mesh):
    placed = (P("tm", None, "col", None), P(None, "tm"), P(None, "tm"), P("tm", None, "col", None))
    small = mesh.shape["tm"] == 8 and mesh.shape["col"] == 4
    return jax.shard_map(
        fused if small else shards,
        mesh=mesh,
        in_specs=placed,
        out_specs=(P("tm", None, "col", None), P("tm", None, "col", None)),
        check_vma=False,
    )
```

```python
import functools

import jax
import jax.numpy as jnp
from jax import lax
from jax.experimental import pallas as pl
from jax.experimental.pallas import tpu as pltpu
from jax.sharding import PartitionSpec as P


def with_halo(block, sides, width):
    for axis, dim in sides:
        count = lax.axis_size(axis)
        forward = [(i, i + 1) for i in range(count - 1)]
        backward = [(target, source) for source, target in forward]
        low = lax.ppermute(
            lax.slice_in_dim(block, block.shape[dim] - width, None, axis=dim), axis, forward
        )
        high = lax.ppermute(lax.slice_in_dim(block, 0, width, axis=dim), axis, backward)
        block = jnp.concatenate([low, block, high], axis=dim)
    return block


def from_behind(array, axis, by):
    devices = lax.axis_size(axis)
    pairs = [(i, i + by) for i in range(devices) if 0 <= i + by < devices]
    return lax.ppermute(array, axis, pairs)


def widen(field):
    return with_halo(field, (("col", 2),), 1)


def from_previous(field):
    return from_behind(field, "tm", 1)


def from_next(field):
    return from_behind(field, "tm", -1)


def forward_pass(kernel, produce):
    return produce(lax.all_gather(kernel, "tm", axis=1, tiled=True), jnp.int32(0))


def backward_pass(kernel, combine, initial):
    return combine(initial, lax.all_gather(kernel, "tm", axis=1, tiled=True), jnp.int32(0))


def pad_rows(field):
    return jnp.pad(field, ((0, 0), (1, 1), (0, 0), (0, 0)))


def window(padded, first, count, row_low, col_low, height, width):
    part = padded[first : first + count, row_low : row_low + height, col_low : col_low + width]
    return part.reshape(-1, part.shape[-1])


def transposed(rows, matrix):
    return lax.dot_general(
        rows, matrix, (((1,), (1,)), ((), ())), preferred_element_type=jnp.float32
    )


def shards(frames, up_kernel, mix_kernel, cotangent):
    frame_count, height, width, in_channels = frames.shape
    out_channels = mix_kernel.shape[0] // 27
    count = 2 * frame_count
    block = count * height * width
    widened = widen(frames)
    earlier = from_previous(widened[-1:])
    extended = pad_rows(jnp.concatenate((earlier, widened), axis=0))
    rows_in = extended.shape[0] - 1

    def up_columns(piece, start):
        taps = piece.reshape(3, 3, 3, in_channels, piece.shape[1])
        even = jnp.zeros((rows_in * height * width, piece.shape[1]), jnp.float32)
        odd = even
        for tap_h in range(3):
            for tap_w in range(3):
                current = window(extended, 1, rows_in, tap_h, tap_w, height, width)
                prior = window(extended, 0, rows_in, tap_h, tap_w, height, width)
                even = even + jnp.dot(
                    current, taps[0, tap_h, tap_w], preferred_element_type=jnp.float32
                )
                even = even + jnp.dot(
                    prior, taps[2, tap_h, tap_w], preferred_element_type=jnp.float32
                )
                odd = odd + jnp.dot(
                    current, taps[1, tap_h, tap_w], preferred_element_type=jnp.float32
                )
        stacked = jnp.stack(
            (even.reshape(rows_in, height * width, -1), odd.reshape(rows_in, height * width, -1)),
            axis=1,
        )
        return stacked.reshape(-1, piece.shape[1])

    before_all = forward_pass(up_kernel, up_columns).reshape(
        2 * rows_in, height, width, out_channels
    )
    hidden = jax.nn.silu(before_all).astype(jnp.bfloat16)
    earlier_hidden = from_previous(hidden[-2:])
    hidden_pad = pad_rows(widen(jnp.concatenate((earlier_hidden, hidden), axis=0)))
    cot_pad = pad_rows(widen(jnp.concatenate((cotangent, from_next(cotangent[:2])), axis=0)))

    def mix_forward(piece, start):
        taps = piece.reshape(3, 3, 3, out_channels, piece.shape[1])
        total = jnp.zeros((block, piece.shape[1]), jnp.float32)
        for tap_t in range(3):
            for tap_h in range(3):
                for tap_w in range(3):
                    total = total + jnp.dot(
                        window(hidden_pad, tap_t, count, tap_h, tap_w, height, width),
                        taps[tap_t, tap_h, tap_w],
                        preferred_element_type=jnp.float32,
                    )
        return total

    def mix_backward(piece):
        taps = piece.reshape(3, 3, 3, out_channels, piece.shape[1])
        total = jnp.zeros((block, out_channels), jnp.float32)
        for tap_t in range(3):
            for tap_h in range(3):
                for tap_w in range(3):
                    total = total + transposed(
                        window(cot_pad, 2 - tap_t, count, 2 - tap_h, 2 - tap_w, height, width),
                        taps[tap_t, tap_h, tap_w],
                    )
        return total

    empty = jnp.zeros((block, out_channels), jnp.float32)
    decoded_flat = forward_pass(mix_kernel, mix_forward)

    def accumulate(total, piece, start):
        return mix_backward(piece)

    hidden_grad = backward_pass(mix_kernel, accumulate, empty)
    flat_before = before_all.reshape(block, out_channels)
    sigma = jax.nn.sigmoid(flat_before)
    before_grad = (hidden_grad * sigma * (1.0 + flat_before * (1.0 - sigma))).astype(jnp.bfloat16)
    before_grad = before_grad.reshape(count, height, width, out_channels)
    grad_pad = pad_rows(widen(jnp.concatenate((before_grad, from_next(before_grad[:1])), axis=0)))
    evens = grad_pad[0::2]
    odds = grad_pad[1::2]

    def up_backward(total, piece, start):
        taps = piece.reshape(3, 3, 3, in_channels, piece.shape[1])
        for tap_h in range(3):
            for tap_w in range(3):
                total = total + transposed(
                    window(evens, 0, frame_count, 2 - tap_h, 2 - tap_w, height, width),
                    taps[0, tap_h, tap_w],
                )
                total = total + transposed(
                    window(odds, 0, frame_count, 2 - tap_h, 2 - tap_w, height, width),
                    taps[1, tap_h, tap_w],
                )
                total = total + transposed(
                    window(evens, 1, frame_count, 2 - tap_h, 2 - tap_w, height, width),
                    taps[2, tap_h, tap_w],
                )
        return total

    grad_start = jnp.zeros((frame_count * height * width, in_channels), jnp.float32)
    grad_total = backward_pass(up_kernel, up_backward, grad_start)
    decoded = decoded_flat.astype(jnp.bfloat16).reshape(count, height, width, out_channels)
    frames_grad = grad_total.astype(jnp.bfloat16).reshape(frame_count, height, width, in_channels)
    return (decoded, frames_grad)


MESH_ID = pl.DeviceIdType.MESH
BF16 = jnp.bfloat16
F32 = jnp.float32


def shifted(rows, by):
    if by == 0:
        return rows
    count = rows.shape[0]
    place = lax.broadcasted_iota(jnp.int32, rows.shape, 0)
    if by < 0:
        return jnp.where(place == 0, 0.0, pltpu.roll(rows, 1, 0))
    return jnp.where(place == count - 1, 0.0, pltpu.roll(rows, count - 1, 0))


def ring_tm(place, n):
    half = place // (n // 2)
    level = place + half * (n - 1 - 2 * place)
    return 2 * level + half


def fused_kernel(
    n, up_ref, mix_ref, frames_ref, cot_ref, decoded_ref, grad_ref,
    up_all, mix_all, frames_all, cot_all, up_taps, inputs, mix_taps, raw, before, patches, decoding,
    cots, spread, gradient, grads, summed, part_d, part_g, got_d, got_g, sum_d, sum_g, last_d, last_g,
    ring_send, ring_recv, halo_send, halo_recv, col_send, col_recv, out_send, out_recv,
):
    me, q = lax.axis_index("tm"), lax.axis_index("col")
    sibling = q + 1 - 2 * (q % 2)
    across = (q + 2) % 4
    diagonal = (sibling + 2) % 4
    level, side = me // 2, me % 2
    place = level + side * (n - 1 - 2 * level)
    right, left = ring_tm((place + 1) % n, n), ring_tm((place + n - 1) % n, n)
    after, ahead = (me + 1) % n, (me + n - 1) % n
    count, in_channels = frames_ref.shape[0], frames_ref.shape[3]
    times, channels = cot_ref.shape[0], cot_ref.shape[3]
    cols = frames_ref.shape[2]
    width = 4 * cols
    small = channels // 4
    rows = mix_ref.shape[0]

    def remote(src, dst, send, recv, tm, col):
        return pltpu.make_async_remote_copy(
            src_ref=src, dst_ref=dst, send_sem=send, recv_sem=recv,
            device_id=(tm, col), device_id_type=MESH_ID,
        )

    barrier = pltpu.get_barrier_semaphore()
    for tm, col in ((left, q), (right, q), (after, q), (ahead, q), (me, sibling), (me, across)):
        pl.semaphore_signal(barrier, inc=1, device_id=(tm, col), device_id_type=MESH_ID)

    row = lax.broadcasted_iota(jnp.int32, (24, rows), 0)
    column = lax.broadcasted_iota(jnp.int32, (24, rows), 1)
    picked = None
    for kt in range(3):
        pick = jnp.where((row // 8 == kt) & (column == 8 * q + row % 8), 1.0, 0.0).astype(BF16)
        term = jnp.dot(
            pick, up_ref[:, kt * 9 * in_channels : (kt + 1) * 9 * in_channels],
            preferred_element_type=F32,
        )
        picked = term if picked is None else picked + term
    for kw in range(3):
        for kh in range(3):
            low = (kh * 3 + kw) * in_channels
            up_all[kw, me, :, kh * in_channels : (kh + 1) * in_channels] = picked[
                :, low : low + in_channels
            ].astype(BF16)
    pl.semaphore_wait(barrier, 6)

    def ring(direction, kind, tap_w, step):
        owner = ring_tm((place + (n - step if direction == 0 else step)) % n, n)
        target = right if direction == 0 else left
        ref = up_all.at[tap_w, owner] if kind == 0 else mix_all.at[
            tap_w, pl.ds(pl.multiple_of(owner * rows, rows), rows),
            0 : (8 if tap_w == 1 else 10) * small,
        ]
        index = (direction, kind, tap_w, step)
        return remote(ref, ref, ring_send.at[index], ring_recv.at[index], target, q)

    def steps_of(direction, kind):
        return n // 2 if direction != kind else n // 2 - 1

    copies = {}

    def ring_start(kind, tap_w, step):
        for direction in range(2):
            if step < steps_of(direction, kind):
                copy = ring(direction, kind, tap_w, step)
                copies[direction, kind, tap_w, step] = copy
                copy.start()

    def ring_got(kind, tap_w, step):
        for direction in range(2):
            if step < steps_of(direction, kind):
                copies[direction, kind, tap_w, step].wait_recv()

    def ring_pass(kind, step):
        for tap_w in range(3):
            ring_got(kind, tap_w, step)
            ring_start(kind, tap_w, step + 1)

    own = [
        remote(src, dst, col_send.at[i], col_recv.at[i], me, col)
        for i, (src, dst, col) in enumerate((
            (frames_ref, frames_all.at[q, 2 : 2 + count], across),
            (cot_ref, cot_all.at[q, 0:times], across),
            (frames_ref, frames_all.at[q, 2 : 2 + count], sibling),
            (cot_ref, cot_all.at[q, 0:times], sibling),
        ))
    ]
    halos = [
        remote(frames_ref.at[count - 2 : count], frames_all.at[q, 0:2],
               halo_send.at[0], halo_recv.at[0], after, q),
        remote(frames_ref.at[0:1], frames_all.at[q, count + 2 : count + 3],
               halo_send.at[1], halo_recv.at[1], ahead, q),
        remote(cot_ref.at[0:3], cot_all.at[q, times : times + 3],
               halo_send.at[2], halo_recv.at[2], ahead, q),
    ]

    @pl.when(me < n - 1)
    def _():
        halos[0].start()

    @pl.when(me > 0)
    def _():
        halos[1].start()
        halos[2].start()

    for tap_w in range(3):
        ring_start(0, tap_w, 0)
    for copy in own:
        copy.start()
    frames_all[q, 2 : 2 + count] = frames_ref[...]
    cot_all[q, 0:times] = cot_ref[...]

    source = lax.broadcasted_iota(jnp.int32, (channels, 2 * small), 0)
    lane = lax.broadcasted_iota(jnp.int32, (channels, 2 * small), 1)
    lane_low = lane % small
    wanted = rows * (lane_low // 8) + 8 * q + lane_low % 8
    first = jnp.where((source == wanted) & (lane < small), 1.0, 0.0).astype(BF16)
    second = jnp.where((source == wanted) & (lane >= small), 1.0, 0.0).astype(BF16)
    mine = pl.ds(pl.multiple_of(me * rows, rows), rows)
    def taken(order, pick):
        lines = [
            mix_ref[:, ((kt * 3 + kh) * 3 + kw) * channels : ((kt * 3 + kh) * 3 + kw + 1) * channels]
            for kt, kh, kw in order
        ]
        return jnp.dot(jnp.concatenate(lines, axis=0), pick, preferred_element_type=F32)

    for kw in range(3):
        lows = [(0, 0, kw), (1, 0, kw), (2, 0, kw), (1, 2, kw)]
        highs = [(0, 1, kw), (1, 1, kw), (2, 1, kw), (0, 2, kw)]
        if kw != 1:
            lows, highs = lows + [(2, 2, 1)], highs + [(2, 2, kw)]
        low, high = taken(lows, first), taken(highs, second)
        for i in range(len(lows)):
            part = low[i * rows : (i + 1) * rows] + high[i * rows : (i + 1) * rows]
            mix_all[kw, mine, i * 2 * small : (i + 1) * 2 * small] = part.astype(BF16)
    ring_pass(0, 0)
    for tap_w in range(3):
        ring_start(1, tap_w, 0)

    @pl.when(me > 0)
    def _():
        halos[0].wait_recv()

    @pl.when(me == 0)
    def _():
        frames_all[q, 0:2] = jnp.zeros((2,) + frames_ref.shape[1:], BF16)

    @pl.when(me < n - 1)
    def _():
        halos[1].wait_recv()
        halos[2].wait_recv()

    @pl.when(me == n - 1)
    def _():
        frames_all[q, count + 2 : count + 3] = jnp.zeros((1,) + frames_ref.shape[1:], BF16)
        cot_all[q, times : times + 3] = jnp.zeros((3,) + cot_ref.shape[1:], BF16)

    edges = (
        frames_all.at[q, 0:2], frames_all.at[q, count + 2 : count + 3],
        cot_all.at[q, times : times + 3],
    )
    crossing = [
        remote(ref, ref, col_send.at[4 + i], col_recv.at[4 + i], me, across)
        for i, ref in enumerate(edges)
    ]
    beside = [
        remote(ref, ref, col_send.at[7 + i], col_recv.at[7 + i], me, sibling)
        for i, ref in enumerate(edges)
    ]
    for copy in crossing + beside:
        copy.start()
    ring_pass(0, 1)
    ring_pass(1, 0)
    ring_pass(0, 2)
    for copy in own[:2] + crossing:
        copy.wait_recv()
    passed = [
        remote(ref.at[across], ref.at[across], col_send.at[10 + i], col_recv.at[10 + i], me, sibling)
        for i, ref in enumerate((frames_all, cot_all))
    ]
    for copy in passed:
        copy.start()
    ring_pass(1, 1)
    for copy in own[2:] + beside + passed:
        copy.wait_recv()

    @pl.loop(0, count + 3)
    def _(t):
        at = pl.ds(pl.multiple_of(t * width, width), width)
        for r in range(2):
            line = jnp.concatenate([frames_all[c, t, r].astype(F32) for c in range(4)], axis=0)
            for kw in range(3):
                inputs[kw, at, r * in_channels : (r + 1) * in_channels] = shifted(
                    line, kw - 1
                ).astype(BF16)

    @pl.loop(0, times + 3)
    def _(t):
        at = pl.ds(pl.multiple_of(t * width, width), width)
        for r in range(2):
            line = jnp.concatenate([cot_all[c, t, r].astype(F32) for c in range(4)], axis=0)
            cots[at, r * channels : (r + 1) * channels] = line.astype(BF16)

    pair = 2 * small
    for kw in range(3):
        ring_got(0, kw, 3)
    ring_pass(1, 2)

    def frame(t):
        return pl.ds(pl.multiple_of(t * width, width), width)

    raw[...] = jnp.zeros_like(raw)

    @pl.loop(0, 3)
    def _(kw):
        for kt in range(3):
            for kh in range(3):
                part = up_all[
                    kw, :, kt * 8 : kt * 8 + 8, kh * in_channels : (kh + 1) * in_channels
                ].astype(F32)
                part = part.reshape(small, in_channels).astype(BF16)
                for r in range(2):
                    r_in = r + kh - 1
                    if 0 <= r_in < 2:
                        up_taps[
                            kw, kt * pair + r * small : kt * pair + (r + 1) * small,
                            r_in * in_channels : (r_in + 1) * in_channels,
                        ] = part
        raw[...] += lax.dot_general(
            inputs[kw], up_taps[kw], (((1,), (1,)), ((), ())), preferred_element_type=F32
        )

    def keep(t, value):
        before[frame(t)] = value
        active = (value / (1.0 + jnp.exp(-value))).astype(BF16).astype(F32)
        for kw in range(3):
            moved = shifted(active, kw - 1).astype(BF16)
            for kt in range(3):
                patches[kw, frame(t - kt + 2), kt * pair : (kt + 1) * pair] = moved

    @pl.loop(0, count + 2)
    def _(i):
        keep(2 * i, raw[frame(i + 1), 0:pair] + raw[frame(i), 2 * pair : 3 * pair])

    @pl.loop(0, count + 1)
    def _(i):
        keep(2 * i + 1, raw[frame(i + 1), pair : 2 * pair])

    def exchange(i, part, got):
        return [
            remote(part.at[target], got.at[j], out_send.at[i + j], out_recv.at[i + j], me, sibling)
            for j, target in enumerate((sibling, diagonal))
        ]

    out_d = exchange(0, part_d, got_d)
    lane = lax.broadcasted_iota(jnp.int32, (channels, pair), 1)
    def add_and_cross(i, part, got, sums, last, first_copies):
        for copy in first_copies:
            copy.wait_recv()
        sums[...] = (part[across].astype(F32) + got[1].astype(F32)).astype(BF16)
        copy = remote(sums, last, out_send.at[i + 2], out_recv.at[i + 2], me, across)
        copy.start()
        return copy

    def finish(part, got, last, copy, out):
        copy.wait_recv()
        out[...] = (part[q].astype(F32) + got[0].astype(F32) + last[...].astype(F32)).astype(BF16)

    def decode(kw):
        ring_got(1, kw, 3)
        last = mix_all[kw, :, 3 * pair : 4 * pair].astype(F32)
        final = mix_all[kw - kw % 2, :, 4 * pair : 5 * pair].astype(F32)
        if kw == 1:
            final = pltpu.roll(final, small, 1)
        tails = [last, pltpu.roll(last, small, 1), final]
        for kt in range(3):
            block = mix_all[kw, :, kt * pair : (kt + 1) * pair]
            turned = pltpu.roll(block.astype(F32), small, 1)
            mix_taps[kw, channels : 2 * channels, kt * pair : (kt + 1) * pair] = block
            mix_taps[kw, 0:channels, kt * pair : (kt + 1) * pair] = jnp.where(
                lane < small, turned, tails[kt]
            ).astype(BF16)
        term = lax.dot_general(
            patches[kw, 2 * width : (times + 2) * width], mix_taps[kw],
            (((1,), (1,)), ((), ())), preferred_element_type=F32,
        )
        decoding[...] = term if kw == 0 else decoding[...] + term

    def back(kw):
        spread[...] = jnp.dot(cots[...], mix_taps[kw], preferred_element_type=F32)

        @pl.loop(0, times + 1)
        def _(t):
            part = None
            for kt in range(3):
                piece = spread[frame(t + 2 - kt), kt * pair : (kt + 1) * pair]
                part = piece if part is None else part + piece
            part = shifted(part, 1 - kw)
            gradient[frame(t)] = part if kw == 0 else gradient[frame(t)] + part

    decode(0)
    back(0)
    decode(1)
    decode(2)

    @pl.loop(0, times)
    def _(t):
        for r in range(2):
            for c in range(4):
                at = pl.ds(pl.multiple_of(t * width + c * cols, cols), cols)
                part_d[c, t, r] = decoding[at, r * channels : (r + 1) * channels].astype(BF16)

    for copy in out_d:
        copy.start()
    back(1)
    cross_d = add_and_cross(0, part_d, got_d, sum_d, last_d, out_d)
    back(2)

    @pl.loop(0, times + 1)
    def _(t):
        value = before[frame(t + 2)]
        sigma = 1.0 / (1.0 + jnp.exp(-value))
        line = gradient[frame(t)] * sigma * (1.0 + value * (1.0 - sigma))
        gradient[frame(t)] = line.astype(BF16).astype(F32)

    @pl.loop(0, count)
    def _(i):
        for kt in range(3):
            line = gradient[frame(2 * i + kt)]
            for kw in range(3):
                grads[kw, frame(i), kt * pair : (kt + 1) * pair] = shifted(line, 1 - kw).astype(BF16)

    out_g = []
    for r in range(2):
        summed[...] = jnp.zeros_like(summed)

        @pl.loop(0, 3)
        def _(kw):
            summed[...] += jnp.dot(
                grads[kw], up_taps[kw, :, r * in_channels : (r + 1) * in_channels],
                preferred_element_type=F32,
            )

        @pl.loop(0, count)
        def _(i):
            for c in range(4):
                at = pl.ds(pl.multiple_of(i * width + c * cols, cols), cols)
                part_g[r, c, i] = summed[at].astype(BF16)

        out_g.append(exchange(3 + 3 * r, part_g.at[r], got_g.at[r]))
        for copy in out_g[r]:
            copy.start()
    finish(part_d, got_d, last_d, cross_d, decoded_ref)
    cross_g = [
        add_and_cross(
            3 + 3 * r, part_g.at[r], got_g.at[r], sum_g.at[r], last_g.at[r], out_g[r]
        )
        for r in range(2)
    ]
    for r in range(2):
        finish(part_g.at[r], got_g.at[r], last_g.at[r], cross_g[r], grad_ref.at[:, r])

    @pl.when(me < n - 1)
    def _():
        halos[0].wait_send()

    @pl.when(me > 0)
    def _():
        halos[1].wait_send()
        halos[2].wait_send()

    for copy in list(copies.values()) + own + crossing + beside + passed:
        copy.wait_send()
    for copy in out_d + out_g[0] + out_g[1] + [cross_d] + cross_g:
        copy.wait_send()


def place(made_d, made_g, decoded_ref, grad_ref):
    decoded_ref[...] = made_d[...]
    grad_ref[...] = made_g[...]


def fused(frames, up_kernel, mix_kernel, cotangent):
    n = lax.axis_size("tm")
    count, height, cols, in_channels = frames.shape
    times, channels = cotangent.shape[0], cotangent.shape[3]
    width, small = 4 * cols, channels // 4
    up_rows, mix_rows = up_kernel.T, mix_kernel.T
    whole = pl.BlockSpec(memory_space=pltpu.VMEM)
    d_block, g_block = (times, height, cols, channels), (count, height, cols, in_channels)
    g_half = (count, cols, in_channels)
    dma = pltpu.SemaphoreType.DMA
    made = pl.pallas_call(
        functools.partial(fused_kernel, n),
        out_shape=(
            jax.ShapeDtypeStruct(d_block, BF16),
            jax.ShapeDtypeStruct(g_block, BF16),
        ),
        in_specs=[whole] * 4,
        out_specs=(whole, whole),
        scratch_shapes=[
            pltpu.VMEM((3, n, 24, 3 * in_channels), BF16),
            pltpu.VMEM((3, channels, 10 * small), BF16),
            pltpu.VMEM((4, count + 3, height, cols, in_channels), BF16),
            pltpu.VMEM((4, times + 3, height, cols, channels), BF16),
            pltpu.VMEM((3, 6 * small, 2 * in_channels), BF16),
            pltpu.VMEM((3, (count + 3) * width, 2 * in_channels), BF16),
            pltpu.VMEM((3, 2 * channels, 6 * small), BF16),
            pltpu.VMEM(((count + 3) * width, 6 * small), F32),
            pltpu.VMEM(((times + 3) * width, 2 * small), F32),
            pltpu.VMEM((3, (times + 5) * width, 6 * small), BF16),
            pltpu.VMEM((times * width, 2 * channels), F32),
            pltpu.VMEM(((times + 3) * width, 2 * channels), BF16),
            pltpu.VMEM(((times + 3) * width, 6 * small), F32),
            pltpu.VMEM(((times + 1) * width, 2 * small), F32),
            pltpu.VMEM((3, count * width, 6 * small), BF16),
            pltpu.VMEM((count * width, in_channels), F32),
            pltpu.VMEM((4,) + d_block, BF16),
            pltpu.VMEM((2, 4) + g_half, BF16),
            pltpu.VMEM((2,) + d_block, BF16),
            pltpu.VMEM((2, 2) + g_half, BF16),
            pltpu.VMEM(d_block, BF16),
            pltpu.VMEM((2,) + g_half, BF16),
            pltpu.VMEM(d_block, BF16),
            pltpu.VMEM((2,) + g_half, BF16),
            dma((2, 2, 3, n // 2)),
            dma((2, 2, 3, n // 2)),
            dma((3,)),
            dma((3,)),
            dma((12,)),
            dma((12,)),
            dma((9,)),
            dma((9,)),
        ],
        compiler_params=pltpu.CompilerParams(
            collective_id=0, has_side_effects=True, vmem_limit_bytes=56 * 1024 * 1024
        ),
    )(up_rows, mix_rows, frames, cotangent)
    return pl.pallas_call(
        place,
        out_shape=tuple(jax.ShapeDtypeStruct(array.shape, array.dtype) for array in made),
        in_specs=[whole] * 2,
        out_specs=(whole, whole),
    )(*made)


def solution(mesh):
    placed = (P("tm", None, "col", None), P(None, "tm"), P(None, "tm"), P("tm", None, "col", None))
    small = mesh.shape["tm"] == 8 and mesh.shape["col"] == 4
    return jax.shard_map(
        fused if small else shards,
        mesh=mesh,
        in_specs=placed,
        out_specs=(P("tm", None, "col", None), P("tm", None, "col", None)),
        check_vma=False,
    )
```

```python
import functools

import jax
import jax.numpy as jnp
from jax import lax
from jax.experimental import pallas as pl
from jax.experimental.pallas import tpu as pltpu
from jax.sharding import PartitionSpec as P


def with_halo(block, sides, width):
    for axis, dim in sides:
        count = lax.axis_size(axis)
        forward = [(i, i + 1) for i in range(count - 1)]
        backward = [(target, source) for source, target in forward]
        low = lax.ppermute(
            lax.slice_in_dim(block, block.shape[dim] - width, None, axis=dim), axis, forward
        )
        high = lax.ppermute(lax.slice_in_dim(block, 0, width, axis=dim), axis, backward)
        block = jnp.concatenate([low, block, high], axis=dim)
    return block


def from_behind(array, axis, by):
    devices = lax.axis_size(axis)
    pairs = [(i, i + by) for i in range(devices) if 0 <= i + by < devices]
    return lax.ppermute(array, axis, pairs)


def widen(field):
    return with_halo(field, (("col", 2),), 1)


def from_previous(field):
    return from_behind(field, "tm", 1)


def from_next(field):
    return from_behind(field, "tm", -1)


def forward_pass(kernel, produce):
    return produce(lax.all_gather(kernel, "tm", axis=1, tiled=True), jnp.int32(0))


def backward_pass(kernel, combine, initial):
    return combine(initial, lax.all_gather(kernel, "tm", axis=1, tiled=True), jnp.int32(0))


def pad_rows(field):
    return jnp.pad(field, ((0, 0), (1, 1), (0, 0), (0, 0)))


def window(padded, first, count, row_low, col_low, height, width):
    part = padded[first : first + count, row_low : row_low + height, col_low : col_low + width]
    return part.reshape(-1, part.shape[-1])


def transposed(rows, matrix):
    return lax.dot_general(
        rows, matrix, (((1,), (1,)), ((), ())), preferred_element_type=jnp.float32
    )


def shards(frames, up_kernel, mix_kernel, cotangent):
    frame_count, height, width, in_channels = frames.shape
    out_channels = mix_kernel.shape[0] // 27
    count = 2 * frame_count
    block = count * height * width
    widened = widen(frames)
    earlier = from_previous(widened[-1:])
    extended = pad_rows(jnp.concatenate((earlier, widened), axis=0))
    rows_in = extended.shape[0] - 1

    def up_columns(piece, start):
        taps = piece.reshape(3, 3, 3, in_channels, piece.shape[1])
        even = jnp.zeros((rows_in * height * width, piece.shape[1]), jnp.float32)
        odd = even
        for tap_h in range(3):
            for tap_w in range(3):
                current = window(extended, 1, rows_in, tap_h, tap_w, height, width)
                prior = window(extended, 0, rows_in, tap_h, tap_w, height, width)
                even = even + jnp.dot(
                    current, taps[0, tap_h, tap_w], preferred_element_type=jnp.float32
                )
                even = even + jnp.dot(
                    prior, taps[2, tap_h, tap_w], preferred_element_type=jnp.float32
                )
                odd = odd + jnp.dot(
                    current, taps[1, tap_h, tap_w], preferred_element_type=jnp.float32
                )
        stacked = jnp.stack(
            (even.reshape(rows_in, height * width, -1), odd.reshape(rows_in, height * width, -1)),
            axis=1,
        )
        return stacked.reshape(-1, piece.shape[1])

    before_all = forward_pass(up_kernel, up_columns).reshape(
        2 * rows_in, height, width, out_channels
    )
    hidden = jax.nn.silu(before_all).astype(jnp.bfloat16)
    earlier_hidden = from_previous(hidden[-2:])
    hidden_pad = pad_rows(widen(jnp.concatenate((earlier_hidden, hidden), axis=0)))
    cot_pad = pad_rows(widen(jnp.concatenate((cotangent, from_next(cotangent[:2])), axis=0)))

    def mix_forward(piece, start):
        taps = piece.reshape(3, 3, 3, out_channels, piece.shape[1])
        total = jnp.zeros((block, piece.shape[1]), jnp.float32)
        for tap_t in range(3):
            for tap_h in range(3):
                for tap_w in range(3):
                    total = total + jnp.dot(
                        window(hidden_pad, tap_t, count, tap_h, tap_w, height, width),
                        taps[tap_t, tap_h, tap_w],
                        preferred_element_type=jnp.float32,
                    )
        return total

    def mix_backward(piece):
        taps = piece.reshape(3, 3, 3, out_channels, piece.shape[1])
        total = jnp.zeros((block, out_channels), jnp.float32)
        for tap_t in range(3):
            for tap_h in range(3):
                for tap_w in range(3):
                    total = total + transposed(
                        window(cot_pad, 2 - tap_t, count, 2 - tap_h, 2 - tap_w, height, width),
                        taps[tap_t, tap_h, tap_w],
                    )
        return total

    empty = jnp.zeros((block, out_channels), jnp.float32)
    decoded_flat = forward_pass(mix_kernel, mix_forward)

    def accumulate(total, piece, start):
        return mix_backward(piece)

    hidden_grad = backward_pass(mix_kernel, accumulate, empty)
    flat_before = before_all.reshape(block, out_channels)
    sigma = jax.nn.sigmoid(flat_before)
    before_grad = (hidden_grad * sigma * (1.0 + flat_before * (1.0 - sigma))).astype(jnp.bfloat16)
    before_grad = before_grad.reshape(count, height, width, out_channels)
    grad_pad = pad_rows(widen(jnp.concatenate((before_grad, from_next(before_grad[:1])), axis=0)))
    evens = grad_pad[0::2]
    odds = grad_pad[1::2]

    def up_backward(total, piece, start):
        taps = piece.reshape(3, 3, 3, in_channels, piece.shape[1])
        for tap_h in range(3):
            for tap_w in range(3):
                total = total + transposed(
                    window(evens, 0, frame_count, 2 - tap_h, 2 - tap_w, height, width),
                    taps[0, tap_h, tap_w],
                )
                total = total + transposed(
                    window(odds, 0, frame_count, 2 - tap_h, 2 - tap_w, height, width),
                    taps[1, tap_h, tap_w],
                )
                total = total + transposed(
                    window(evens, 1, frame_count, 2 - tap_h, 2 - tap_w, height, width),
                    taps[2, tap_h, tap_w],
                )
        return total

    grad_start = jnp.zeros((frame_count * height * width, in_channels), jnp.float32)
    grad_total = backward_pass(up_kernel, up_backward, grad_start)
    decoded = decoded_flat.astype(jnp.bfloat16).reshape(count, height, width, out_channels)
    frames_grad = grad_total.astype(jnp.bfloat16).reshape(frame_count, height, width, in_channels)
    return (decoded, frames_grad)


MESH_ID = pl.DeviceIdType.MESH
BF16 = jnp.bfloat16
F32 = jnp.float32


def shifted(rows, by):
    if by == 0:
        return rows
    count = rows.shape[0]
    place = lax.broadcasted_iota(jnp.int32, rows.shape, 0)
    if by < 0:
        return jnp.where(place == 0, 0.0, pltpu.roll(rows, 1, 0))
    return jnp.where(place == count - 1, 0.0, pltpu.roll(rows, count - 1, 0))


def ring_tm(place, n):
    half = place // (n // 2)
    level = place + half * (n - 1 - 2 * place)
    return 2 * level + half


def fused_kernel(
    n, up_ref, mix_ref, frames_ref, cot_ref, decoded_ref, grad_ref,
    up_all, mix_all, frames_all, cot_all, up_taps, inputs, mix_taps, raw, before, patches, decoding,
    cots, spread, gradient, grads, summed, part_d, part_g, got_d, got_g, sum_d, sum_g, last_d, last_g,
    ring_send, ring_recv, halo_send, halo_recv, col_send, col_recv, out_send, out_recv,
):
    me, q = lax.axis_index("tm"), lax.axis_index("col")
    sibling = q + 1 - 2 * (q % 2)
    across = (q + 2) % 4
    diagonal = (sibling + 2) % 4
    level, side = me // 2, me % 2
    place = level + side * (n - 1 - 2 * level)
    right, left = ring_tm((place + 1) % n, n), ring_tm((place + n - 1) % n, n)
    after, ahead = (me + 1) % n, (me + n - 1) % n
    count, in_channels = frames_ref.shape[0], frames_ref.shape[3]
    times, channels = cot_ref.shape[0], cot_ref.shape[3]
    cols = frames_ref.shape[2]
    width = 4 * cols
    small = channels // 4
    rows = mix_ref.shape[0]

    def remote(src, dst, send, recv, tm, col):
        return pltpu.make_async_remote_copy(
            src_ref=src, dst_ref=dst, send_sem=send, recv_sem=recv,
            device_id=(tm, col), device_id_type=MESH_ID,
        )

    barrier = pltpu.get_barrier_semaphore()
    for tm, col in ((left, q), (right, q), (after, q), (ahead, q), (me, sibling), (me, across)):
        pl.semaphore_signal(barrier, inc=1, device_id=(tm, col), device_id_type=MESH_ID)

    row = lax.broadcasted_iota(jnp.int32, (24, rows), 0)
    column = lax.broadcasted_iota(jnp.int32, (24, rows), 1)
    picked = None
    for kt in range(3):
        pick = jnp.where((row // 8 == kt) & (column == 8 * q + row % 8), 1.0, 0.0).astype(BF16)
        term = jnp.dot(
            pick, up_ref[:, kt * 9 * in_channels : (kt + 1) * 9 * in_channels],
            preferred_element_type=F32,
        )
        picked = term if picked is None else picked + term
    for kw in range(3):
        for kh in range(3):
            low = (kh * 3 + kw) * in_channels
            up_all[kw, me, :, kh * in_channels : (kh + 1) * in_channels] = picked[
                :, low : low + in_channels
            ].astype(BF16)
    pl.semaphore_wait(barrier, 6)

    def ring(direction, kind, tap_w, step):
        owner = ring_tm((place + (n - step if direction == 0 else step)) % n, n)
        target = right if direction == 0 else left
        ref = up_all.at[tap_w, owner] if kind == 0 else mix_all.at[
            tap_w, pl.ds(pl.multiple_of(owner * rows, rows), rows),
            0 : (8 if tap_w == 1 else 10) * small,
        ]
        index = (direction, kind, tap_w, step)
        return remote(ref, ref, ring_send.at[index], ring_recv.at[index], target, q)

    def steps_of(direction, kind):
        return n // 2 if direction != kind else n // 2 - 1

    copies = {}

    def ring_start(kind, tap_w, step, directions=(0, 1)):
        for direction in directions:
            if step < steps_of(direction, kind):
                copy = ring(direction, kind, tap_w, step)
                copies[direction, kind, tap_w, step] = copy
                copy.start()

    def ring_got(kind, tap_w, step, directions=(0, 1)):
        for direction in directions:
            if step < steps_of(direction, kind):
                copies[direction, kind, tap_w, step].wait_recv()

    def ring_pass(kind, step):
        for tap_w in range(3):
            for direction in range(2):
                ring_got(kind, tap_w, step, (direction,))
                ring_start(kind, tap_w, step + 1, (direction,))

    own = [
        remote(src, dst, col_send.at[i], col_recv.at[i], me, col)
        for i, (src, dst, col) in enumerate((
            (frames_ref, frames_all.at[q, 2 : 2 + count], across),
            (cot_ref, cot_all.at[q, 0:times], across),
            (frames_ref, frames_all.at[q, 2 : 2 + count], sibling),
            (cot_ref, cot_all.at[q, 0:times], sibling),
        ))
    ]
    halos = [
        remote(frames_ref.at[count - 2 : count], frames_all.at[q, 0:2],
               halo_send.at[0], halo_recv.at[0], after, q),
        remote(frames_ref.at[0:1], frames_all.at[q, count + 2 : count + 3],
               halo_send.at[1], halo_recv.at[1], ahead, q),
        remote(cot_ref.at[0:3], cot_all.at[q, times : times + 3],
               halo_send.at[2], halo_recv.at[2], ahead, q),
    ]

    @pl.when(me < n - 1)
    def _():
        halos[0].start()

    @pl.when(me > 0)
    def _():
        halos[1].start()
        halos[2].start()

    for tap_w in range(3):
        ring_start(0, tap_w, 0)
    for copy in own:
        copy.start()
    frames_all[q, 2 : 2 + count] = frames_ref[...]
    cot_all[q, 0:times] = cot_ref[...]

    source = lax.broadcasted_iota(jnp.int32, (channels, 2 * small), 0)
    lane = lax.broadcasted_iota(jnp.int32, (channels, 2 * small), 1)
    lane_low = lane % small
    wanted = rows * (lane_low // 8) + 8 * q + lane_low % 8
    first = jnp.where((source == wanted) & (lane < small), 1.0, 0.0).astype(BF16)
    second = jnp.where((source == wanted) & (lane >= small), 1.0, 0.0).astype(BF16)
    mine = pl.ds(pl.multiple_of(me * rows, rows), rows)
    def taken(order, pick):
        lines = [
            mix_ref[:, ((kt * 3 + kh) * 3 + kw) * channels : ((kt * 3 + kh) * 3 + kw + 1) * channels]
            for kt, kh, kw in order
        ]
        return jnp.dot(jnp.concatenate(lines, axis=0), pick, preferred_element_type=F32)

    for kw in range(3):
        lows = [(0, 0, kw), (1, 0, kw), (2, 0, kw), (1, 2, kw)]
        highs = [(0, 1, kw), (1, 1, kw), (2, 1, kw), (0, 2, kw)]
        if kw != 1:
            lows, highs = lows + [(2, 2, 1)], highs + [(2, 2, kw)]
        low, high = taken(lows, first), taken(highs, second)
        for i in range(len(lows)):
            part = low[i * rows : (i + 1) * rows] + high[i * rows : (i + 1) * rows]
            mix_all[kw, mine, i * 2 * small : (i + 1) * 2 * small] = part.astype(BF16)
    ring_pass(0, 0)
    for tap_w in range(3):
        ring_start(1, tap_w, 0)

    @pl.when(me > 0)
    def _():
        halos[0].wait_recv()

    @pl.when(me == 0)
    def _():
        frames_all[q, 0:2] = jnp.zeros((2,) + frames_ref.shape[1:], BF16)

    @pl.when(me < n - 1)
    def _():
        halos[1].wait_recv()
        halos[2].wait_recv()

    @pl.when(me == n - 1)
    def _():
        frames_all[q, count + 2 : count + 3] = jnp.zeros((1,) + frames_ref.shape[1:], BF16)
        cot_all[q, times : times + 3] = jnp.zeros((3,) + cot_ref.shape[1:], BF16)

    edges = (
        frames_all.at[q, 0:2], frames_all.at[q, count + 2 : count + 3],
        cot_all.at[q, times : times + 3],
    )
    crossing = [
        remote(ref, ref, col_send.at[4 + i], col_recv.at[4 + i], me, across)
        for i, ref in enumerate(edges)
    ]
    beside = [
        remote(ref, ref, col_send.at[7 + i], col_recv.at[7 + i], me, sibling)
        for i, ref in enumerate(edges)
    ]
    for copy in crossing + beside:
        copy.start()
    ring_pass(0, 1)
    ring_pass(1, 0)
    ring_pass(0, 2)
    for copy in own[:2] + crossing:
        copy.wait_recv()
    passed = [
        remote(ref.at[across], ref.at[across], col_send.at[10 + i], col_recv.at[10 + i], me, sibling)
        for i, ref in enumerate((frames_all, cot_all))
    ]
    for copy in passed:
        copy.start()
    ring_pass(1, 1)
    for copy in own[2:] + beside + passed:
        copy.wait_recv()

    @pl.loop(0, count + 3)
    def _(t):
        at = pl.ds(pl.multiple_of(t * width, width), width)
        for r in range(2):
            line = jnp.concatenate([frames_all[c, t, r].astype(F32) for c in range(4)], axis=0)
            for kw in range(3):
                inputs[kw, at, r * in_channels : (r + 1) * in_channels] = shifted(
                    line, kw - 1
                ).astype(BF16)

    @pl.loop(0, times + 3)
    def _(t):
        at = pl.ds(pl.multiple_of(t * width, width), width)
        for r in range(2):
            line = jnp.concatenate([cot_all[c, t, r].astype(F32) for c in range(4)], axis=0)
            cots[at, r * channels : (r + 1) * channels] = line.astype(BF16)

    pair = 2 * small
    for kw in range(3):
        ring_got(0, kw, 3)
    ring_pass(1, 2)

    def frame(t):
        return pl.ds(pl.multiple_of(t * width, width), width)

    raw[...] = jnp.zeros_like(raw)

    @pl.loop(0, 3)
    def _(kw):
        for kt in range(3):
            for kh in range(3):
                part = up_all[
                    kw, :, kt * 8 : kt * 8 + 8, kh * in_channels : (kh + 1) * in_channels
                ].astype(F32)
                part = part.reshape(small, in_channels).astype(BF16)
                for r in range(2):
                    r_in = r + kh - 1
                    if 0 <= r_in < 2:
                        up_taps[
                            kw, kt * pair + r * small : kt * pair + (r + 1) * small,
                            r_in * in_channels : (r_in + 1) * in_channels,
                        ] = part
        raw[...] += lax.dot_general(
            inputs[kw], up_taps[kw], (((1,), (1,)), ((), ())), preferred_element_type=F32
        )

    def keep(t, value):
        before[frame(t)] = value
        active = (value / (1.0 + jnp.exp(-value))).astype(BF16).astype(F32)
        for kw in range(3):
            moved = shifted(active, kw - 1).astype(BF16)
            for kt in range(3):
                patches[kw, frame(t - kt + 2), kt * pair : (kt + 1) * pair] = moved

    @pl.loop(0, count + 2)
    def _(i):
        keep(2 * i, raw[frame(i + 1), 0:pair] + raw[frame(i), 2 * pair : 3 * pair])

    @pl.loop(0, count + 1)
    def _(i):
        keep(2 * i + 1, raw[frame(i + 1), pair : 2 * pair])

    def exchange(i, part, got):
        return [
            remote(part.at[target], got.at[j], out_send.at[i + j], out_recv.at[i + j], me, sibling)
            for j, target in enumerate((sibling, diagonal))
        ]

    out_d = exchange(0, part_d, got_d)
    lane = lax.broadcasted_iota(jnp.int32, (channels, pair), 1)
    def add_and_cross(i, part, got, sums, last, first_copies):
        for copy in first_copies:
            copy.wait_recv()
        sums[...] = (part[across].astype(F32) + got[1].astype(F32)).astype(BF16)
        copy = remote(sums, last, out_send.at[i + 2], out_recv.at[i + 2], me, across)
        copy.start()
        return copy

    def finish(part, got, last, copy, out):
        copy.wait_recv()
        out[...] = (part[q].astype(F32) + got[0].astype(F32) + last[...].astype(F32)).astype(BF16)

    def decode(kw):
        ring_got(1, kw, 3)
        last = mix_all[kw, :, 3 * pair : 4 * pair].astype(F32)
        final = mix_all[kw - kw % 2, :, 4 * pair : 5 * pair].astype(F32)
        if kw == 1:
            final = pltpu.roll(final, small, 1)
        tails = [last, pltpu.roll(last, small, 1), final]
        for kt in range(3):
            block = mix_all[kw, :, kt * pair : (kt + 1) * pair]
            turned = pltpu.roll(block.astype(F32), small, 1)
            mix_taps[kw, channels : 2 * channels, kt * pair : (kt + 1) * pair] = block
            mix_taps[kw, 0:channels, kt * pair : (kt + 1) * pair] = jnp.where(
                lane < small, turned, tails[kt]
            ).astype(BF16)
        term = lax.dot_general(
            patches[kw, 2 * width : (times + 2) * width], mix_taps[kw],
            (((1,), (1,)), ((), ())), preferred_element_type=F32,
        )
        decoding[...] = term if kw == 0 else decoding[...] + term

    def back(kw):
        spread[...] = jnp.dot(cots[...], mix_taps[kw], preferred_element_type=F32)

        @pl.loop(0, times + 1)
        def _(t):
            part = None
            for kt in range(3):
                piece = spread[frame(t + 2 - kt), kt * pair : (kt + 1) * pair]
                part = piece if part is None else part + piece
            part = shifted(part, 1 - kw)
            gradient[frame(t)] = part if kw == 0 else gradient[frame(t)] + part

    decode(0)
    back(0)
    decode(1)
    decode(2)

    @pl.loop(0, times)
    def _(t):
        for r in range(2):
            for c in range(4):
                at = pl.ds(pl.multiple_of(t * width + c * cols, cols), cols)
                part_d[c, t, r] = decoding[at, r * channels : (r + 1) * channels].astype(BF16)

    for copy in out_d:
        copy.start()
    back(1)
    cross_d = add_and_cross(0, part_d, got_d, sum_d, last_d, out_d)
    back(2)

    @pl.loop(0, times + 1)
    def _(t):
        value = before[frame(t + 2)]
        sigma = 1.0 / (1.0 + jnp.exp(-value))
        line = gradient[frame(t)] * sigma * (1.0 + value * (1.0 - sigma))
        gradient[frame(t)] = line.astype(BF16).astype(F32)

    @pl.loop(0, count)
    def _(i):
        for kt in range(3):
            line = gradient[frame(2 * i + kt)]
            for kw in range(3):
                grads[kw, frame(i), kt * pair : (kt + 1) * pair] = shifted(line, 1 - kw).astype(BF16)

    out_g = []
    for r in range(2):
        summed[...] = jnp.zeros_like(summed)

        @pl.loop(0, 3)
        def _(kw):
            summed[...] += jnp.dot(
                grads[kw], up_taps[kw, :, r * in_channels : (r + 1) * in_channels],
                preferred_element_type=F32,
            )

        @pl.loop(0, count)
        def _(i):
            for c in range(4):
                at = pl.ds(pl.multiple_of(i * width + c * cols, cols), cols)
                part_g[r, c, i] = summed[at].astype(BF16)

        out_g.append(exchange(3 + 3 * r, part_g.at[r], got_g.at[r]))
        for copy in out_g[r]:
            copy.start()
    cross_g = [
        add_and_cross(
            3 + 3 * r, part_g.at[r], got_g.at[r], sum_g.at[r], last_g.at[r], out_g[r]
        )
        for r in range(2)
    ]
    finish(part_d, got_d, last_d, cross_d, decoded_ref)
    for r in range(2):
        finish(part_g.at[r], got_g.at[r], last_g.at[r], cross_g[r], grad_ref.at[:, r])

    @pl.when(me < n - 1)
    def _():
        halos[0].wait_send()

    @pl.when(me > 0)
    def _():
        halos[1].wait_send()
        halos[2].wait_send()

    for copy in list(copies.values()) + own + crossing + beside + passed:
        copy.wait_send()
    for copy in out_d + out_g[0] + out_g[1] + [cross_d] + cross_g:
        copy.wait_send()


def place(made_d, made_g, decoded_ref, grad_ref):
    decoded_ref[...] = made_d[...]
    grad_ref[...] = made_g[...]


def fused(frames, up_kernel, mix_kernel, cotangent):
    n = lax.axis_size("tm")
    count, height, cols, in_channels = frames.shape
    times, channels = cotangent.shape[0], cotangent.shape[3]
    width, small = 4 * cols, channels // 4
    up_rows, mix_rows = up_kernel.T, mix_kernel.T
    whole = pl.BlockSpec(memory_space=pltpu.VMEM)
    d_block, g_block = (times, height, cols, channels), (count, height, cols, in_channels)
    g_half = (count, cols, in_channels)
    dma = pltpu.SemaphoreType.DMA
    made = pl.pallas_call(
        functools.partial(fused_kernel, n),
        out_shape=(
            jax.ShapeDtypeStruct(d_block, BF16),
            jax.ShapeDtypeStruct(g_block, BF16),
        ),
        in_specs=[whole] * 4,
        out_specs=(whole, whole),
        scratch_shapes=[
            pltpu.VMEM((3, n, 24, 3 * in_channels), BF16),
            pltpu.VMEM((3, channels, 10 * small), BF16),
            pltpu.VMEM((4, count + 3, height, cols, in_channels), BF16),
            pltpu.VMEM((4, times + 3, height, cols, channels), BF16),
            pltpu.VMEM((3, 6 * small, 2 * in_channels), BF16),
            pltpu.VMEM((3, (count + 3) * width, 2 * in_channels), BF16),
            pltpu.VMEM((3, 2 * channels, 6 * small), BF16),
            pltpu.VMEM(((count + 3) * width, 6 * small), F32),
            pltpu.VMEM(((times + 3) * width, 2 * small), F32),
            pltpu.VMEM((3, (times + 5) * width, 6 * small), BF16),
            pltpu.VMEM((times * width, 2 * channels), F32),
            pltpu.VMEM(((times + 3) * width, 2 * channels), BF16),
            pltpu.VMEM(((times + 3) * width, 6 * small), F32),
            pltpu.VMEM(((times + 1) * width, 2 * small), F32),
            pltpu.VMEM((3, count * width, 6 * small), BF16),
            pltpu.VMEM((count * width, in_channels), F32),
            pltpu.VMEM((4,) + d_block, BF16),
            pltpu.VMEM((2, 4) + g_half, BF16),
            pltpu.VMEM((2,) + d_block, BF16),
            pltpu.VMEM((2, 2) + g_half, BF16),
            pltpu.VMEM(d_block, BF16),
            pltpu.VMEM((2,) + g_half, BF16),
            pltpu.VMEM(d_block, BF16),
            pltpu.VMEM((2,) + g_half, BF16),
            dma((2, 2, 3, n // 2)),
            dma((2, 2, 3, n // 2)),
            dma((3,)),
            dma((3,)),
            dma((12,)),
            dma((12,)),
            dma((9,)),
            dma((9,)),
        ],
        compiler_params=pltpu.CompilerParams(
            collective_id=0, has_side_effects=True, vmem_limit_bytes=56 * 1024 * 1024
        ),
    )(up_rows, mix_rows, frames, cotangent)
    return pl.pallas_call(
        place,
        out_shape=tuple(jax.ShapeDtypeStruct(array.shape, array.dtype) for array in made),
        in_specs=[whole] * 2,
        out_specs=(whole, whole),
    )(*made)


def solution(mesh):
    placed = (P("tm", None, "col", None), P(None, "tm"), P(None, "tm"), P("tm", None, "col", None))
    small = mesh.shape["tm"] == 8 and mesh.shape["col"] == 4
    return jax.shard_map(
        fused if small else shards,
        mesh=mesh,
        in_specs=placed,
        out_specs=(P("tm", None, "col", None), P("tm", None, "col", None)),
        check_vma=False,
    )
```

```python
import functools

import jax
import jax.numpy as jnp
from jax import lax
from jax.experimental import pallas as pl
from jax.experimental.pallas import tpu as pltpu
from jax.sharding import PartitionSpec as P


def with_halo(block, sides, width):
    for axis, dim in sides:
        count = lax.axis_size(axis)
        forward = [(i, i + 1) for i in range(count - 1)]
        backward = [(target, source) for source, target in forward]
        low = lax.ppermute(
            lax.slice_in_dim(block, block.shape[dim] - width, None, axis=dim), axis, forward
        )
        high = lax.ppermute(lax.slice_in_dim(block, 0, width, axis=dim), axis, backward)
        block = jnp.concatenate([low, block, high], axis=dim)
    return block


def from_behind(array, axis, by):
    devices = lax.axis_size(axis)
    pairs = [(i, i + by) for i in range(devices) if 0 <= i + by < devices]
    return lax.ppermute(array, axis, pairs)


def widen(field):
    return with_halo(field, (("col", 2),), 1)


def from_previous(field):
    return from_behind(field, "tm", 1)


def from_next(field):
    return from_behind(field, "tm", -1)


def forward_pass(kernel, produce):
    return produce(lax.all_gather(kernel, "tm", axis=1, tiled=True), jnp.int32(0))


def backward_pass(kernel, combine, initial):
    return combine(initial, lax.all_gather(kernel, "tm", axis=1, tiled=True), jnp.int32(0))


def pad_rows(field):
    return jnp.pad(field, ((0, 0), (1, 1), (0, 0), (0, 0)))


def window(padded, first, count, row_low, col_low, height, width):
    part = padded[first : first + count, row_low : row_low + height, col_low : col_low + width]
    return part.reshape(-1, part.shape[-1])


def transposed(rows, matrix):
    return lax.dot_general(
        rows, matrix, (((1,), (1,)), ((), ())), preferred_element_type=jnp.float32
    )


def shards(frames, up_kernel, mix_kernel, cotangent):
    frame_count, height, width, in_channels = frames.shape
    out_channels = mix_kernel.shape[0] // 27
    count = 2 * frame_count
    block = count * height * width
    widened = widen(frames)
    earlier = from_previous(widened[-1:])
    extended = pad_rows(jnp.concatenate((earlier, widened), axis=0))
    rows_in = extended.shape[0] - 1

    def up_columns(piece, start):
        taps = piece.reshape(3, 3, 3, in_channels, piece.shape[1])
        even = jnp.zeros((rows_in * height * width, piece.shape[1]), jnp.float32)
        odd = even
        for tap_h in range(3):
            for tap_w in range(3):
                current = window(extended, 1, rows_in, tap_h, tap_w, height, width)
                prior = window(extended, 0, rows_in, tap_h, tap_w, height, width)
                even = even + jnp.dot(
                    current, taps[0, tap_h, tap_w], preferred_element_type=jnp.float32
                )
                even = even + jnp.dot(
                    prior, taps[2, tap_h, tap_w], preferred_element_type=jnp.float32
                )
                odd = odd + jnp.dot(
                    current, taps[1, tap_h, tap_w], preferred_element_type=jnp.float32
                )
        stacked = jnp.stack(
            (even.reshape(rows_in, height * width, -1), odd.reshape(rows_in, height * width, -1)),
            axis=1,
        )
        return stacked.reshape(-1, piece.shape[1])

    before_all = forward_pass(up_kernel, up_columns).reshape(
        2 * rows_in, height, width, out_channels
    )
    hidden = jax.nn.silu(before_all).astype(jnp.bfloat16)
    earlier_hidden = from_previous(hidden[-2:])
    hidden_pad = pad_rows(widen(jnp.concatenate((earlier_hidden, hidden), axis=0)))
    cot_pad = pad_rows(widen(jnp.concatenate((cotangent, from_next(cotangent[:2])), axis=0)))

    def mix_forward(piece, start):
        taps = piece.reshape(3, 3, 3, out_channels, piece.shape[1])
        total = jnp.zeros((block, piece.shape[1]), jnp.float32)
        for tap_t in range(3):
            for tap_h in range(3):
                for tap_w in range(3):
                    total = total + jnp.dot(
                        window(hidden_pad, tap_t, count, tap_h, tap_w, height, width),
                        taps[tap_t, tap_h, tap_w],
                        preferred_element_type=jnp.float32,
                    )
        return total

    def mix_backward(piece):
        taps = piece.reshape(3, 3, 3, out_channels, piece.shape[1])
        total = jnp.zeros((block, out_channels), jnp.float32)
        for tap_t in range(3):
            for tap_h in range(3):
                for tap_w in range(3):
                    total = total + transposed(
                        window(cot_pad, 2 - tap_t, count, 2 - tap_h, 2 - tap_w, height, width),
                        taps[tap_t, tap_h, tap_w],
                    )
        return total

    empty = jnp.zeros((block, out_channels), jnp.float32)
    decoded_flat = forward_pass(mix_kernel, mix_forward)

    def accumulate(total, piece, start):
        return mix_backward(piece)

    hidden_grad = backward_pass(mix_kernel, accumulate, empty)
    flat_before = before_all.reshape(block, out_channels)
    sigma = jax.nn.sigmoid(flat_before)
    before_grad = (hidden_grad * sigma * (1.0 + flat_before * (1.0 - sigma))).astype(jnp.bfloat16)
    before_grad = before_grad.reshape(count, height, width, out_channels)
    grad_pad = pad_rows(widen(jnp.concatenate((before_grad, from_next(before_grad[:1])), axis=0)))
    evens = grad_pad[0::2]
    odds = grad_pad[1::2]

    def up_backward(total, piece, start):
        taps = piece.reshape(3, 3, 3, in_channels, piece.shape[1])
        for tap_h in range(3):
            for tap_w in range(3):
                total = total + transposed(
                    window(evens, 0, frame_count, 2 - tap_h, 2 - tap_w, height, width),
                    taps[0, tap_h, tap_w],
                )
                total = total + transposed(
                    window(odds, 0, frame_count, 2 - tap_h, 2 - tap_w, height, width),
                    taps[1, tap_h, tap_w],
                )
                total = total + transposed(
                    window(evens, 1, frame_count, 2 - tap_h, 2 - tap_w, height, width),
                    taps[2, tap_h, tap_w],
                )
        return total

    grad_start = jnp.zeros((frame_count * height * width, in_channels), jnp.float32)
    grad_total = backward_pass(up_kernel, up_backward, grad_start)
    decoded = decoded_flat.astype(jnp.bfloat16).reshape(count, height, width, out_channels)
    frames_grad = grad_total.astype(jnp.bfloat16).reshape(frame_count, height, width, in_channels)
    return (decoded, frames_grad)


MESH_ID = pl.DeviceIdType.MESH
BF16 = jnp.bfloat16
F32 = jnp.float32


def shifted(rows, by):
    if by == 0:
        return rows
    count = rows.shape[0]
    place = lax.broadcasted_iota(jnp.int32, rows.shape, 0)
    if by < 0:
        return jnp.where(place == 0, 0.0, pltpu.roll(rows, 1, 0))
    return jnp.where(place == count - 1, 0.0, pltpu.roll(rows, count - 1, 0))


def ring_tm(place, n):
    half = place // (n // 2)
    level = place + half * (n - 1 - 2 * place)
    return 2 * level + half


def fused_kernel(
    n, up_ref, mix_ref, frames_ref, cot_ref, decoded_ref, grad_ref,
    up_all, mix_all, frames_all, cot_all, up_taps, inputs, mix_taps, raw, before, patches, decoding,
    cots, spread, gradient, grads, summed, part_d, part_g, got_d, got_g, sum_d, sum_g, last_d, last_g,
    ring_send, ring_recv, halo_send, halo_recv, col_send, col_recv, out_send, out_recv,
):
    me, q = lax.axis_index("tm"), lax.axis_index("col")
    sibling = q + 1 - 2 * (q % 2)
    across = (q + 2) % 4
    diagonal = (sibling + 2) % 4
    level, side = me // 2, me % 2
    place = level + side * (n - 1 - 2 * level)
    right, left = ring_tm((place + 1) % n, n), ring_tm((place + n - 1) % n, n)
    after, ahead = (me + 1) % n, (me + n - 1) % n
    count, in_channels = frames_ref.shape[0], frames_ref.shape[3]
    times, channels = cot_ref.shape[0], cot_ref.shape[3]
    cols = frames_ref.shape[2]
    width = 4 * cols
    small = channels // 4
    rows = mix_ref.shape[0]

    def remote(src, dst, send, recv, tm, col):
        return pltpu.make_async_remote_copy(
            src_ref=src, dst_ref=dst, send_sem=send, recv_sem=recv,
            device_id=(tm, col), device_id_type=MESH_ID,
        )

    barrier = pltpu.get_barrier_semaphore()
    for tm, col in ((left, q), (right, q), (after, q), (ahead, q), (me, sibling), (me, across)):
        pl.semaphore_signal(barrier, inc=1, device_id=(tm, col), device_id_type=MESH_ID)

    row = lax.broadcasted_iota(jnp.int32, (24, rows), 0)
    column = lax.broadcasted_iota(jnp.int32, (24, rows), 1)
    picked = None
    for kt in range(3):
        pick = jnp.where((row // 8 == kt) & (column == 8 * q + row % 8), 1.0, 0.0).astype(BF16)
        term = jnp.dot(
            pick, up_ref[:, kt * 9 * in_channels : (kt + 1) * 9 * in_channels],
            preferred_element_type=F32,
        )
        picked = term if picked is None else picked + term
    for kw in range(3):
        for kh in range(3):
            low = (kh * 3 + kw) * in_channels
            up_all[kw, me, :, kh * in_channels : (kh + 1) * in_channels] = picked[
                :, low : low + in_channels
            ].astype(BF16)
    pl.semaphore_wait(barrier, 6)

    def ring(direction, kind, tap_w, step):
        owner = ring_tm((place + (n - step if direction == 0 else step)) % n, n)
        target = right if direction == 0 else left
        ref = up_all.at[tap_w, owner] if kind == 0 else mix_all.at[
            tap_w, pl.ds(pl.multiple_of(owner * rows, rows), rows),
            0 : (8 if tap_w == 1 else 10) * small,
        ]
        index = (direction, kind, tap_w, step)
        return remote(ref, ref, ring_send.at[index], ring_recv.at[index], target, q)

    def steps_of(direction, kind):
        return n // 2 if direction != kind else n // 2 - 1

    copies = {}

    def ring_start(kind, tap_w, step, directions=(0, 1)):
        for direction in directions:
            if step < steps_of(direction, kind):
                copy = ring(direction, kind, tap_w, step)
                copies[direction, kind, tap_w, step] = copy
                copy.start()

    def ring_got(kind, tap_w, step, directions=(0, 1)):
        for direction in directions:
            if step < steps_of(direction, kind):
                copies[direction, kind, tap_w, step].wait_recv()

    def ring_pass(kind, step, directions=(0, 1)):
        for tap_w in range(3):
            for direction in directions:
                ring_got(kind, tap_w, step, (direction,))
                ring_start(kind, tap_w, step + 1, (direction,))

    own = [
        remote(src, dst, col_send.at[i], col_recv.at[i], me, col)
        for i, (src, dst, col) in enumerate((
            (frames_ref, frames_all.at[q, 2 : 2 + count], across),
            (cot_ref, cot_all.at[q, 0:times], across),
            (frames_ref, frames_all.at[q, 2 : 2 + count], sibling),
            (cot_ref, cot_all.at[q, 0:times], sibling),
        ))
    ]
    halos = [
        remote(frames_ref.at[count - 2 : count], frames_all.at[q, 0:2],
               halo_send.at[0], halo_recv.at[0], after, q),
        remote(frames_ref.at[0:1], frames_all.at[q, count + 2 : count + 3],
               halo_send.at[1], halo_recv.at[1], ahead, q),
        remote(cot_ref.at[0:3], cot_all.at[q, times : times + 3],
               halo_send.at[2], halo_recv.at[2], ahead, q),
    ]

    @pl.when(me < n - 1)
    def _():
        halos[0].start()

    @pl.when(me > 0)
    def _():
        halos[1].start()
        halos[2].start()

    for tap_w in range(3):
        ring_start(0, tap_w, 0)
    for copy in own:
        copy.start()
    frames_all[q, 2 : 2 + count] = frames_ref[...]
    cot_all[q, 0:times] = cot_ref[...]

    source = lax.broadcasted_iota(jnp.int32, (channels, 2 * small), 0)
    lane = lax.broadcasted_iota(jnp.int32, (channels, 2 * small), 1)
    lane_low = lane % small
    wanted = rows * (lane_low // 8) + 8 * q + lane_low % 8
    first = jnp.where((source == wanted) & (lane < small), 1.0, 0.0).astype(BF16)
    second = jnp.where((source == wanted) & (lane >= small), 1.0, 0.0).astype(BF16)
    mine = pl.ds(pl.multiple_of(me * rows, rows), rows)
    def taken(order, pick):
        lines = [
            mix_ref[:, ((kt * 3 + kh) * 3 + kw) * channels : ((kt * 3 + kh) * 3 + kw + 1) * channels]
            for kt, kh, kw in order
        ]
        return jnp.dot(jnp.concatenate(lines, axis=0), pick, preferred_element_type=F32)

    for kw in range(3):
        lows = [(0, 0, kw), (1, 0, kw), (2, 0, kw), (1, 2, kw)]
        highs = [(0, 1, kw), (1, 1, kw), (2, 1, kw), (0, 2, kw)]
        if kw != 1:
            lows, highs = lows + [(2, 2, 1)], highs + [(2, 2, kw)]
        low, high = taken(lows, first), taken(highs, second)
        for i in range(len(lows)):
            part = low[i * rows : (i + 1) * rows] + high[i * rows : (i + 1) * rows]
            mix_all[kw, mine, i * 2 * small : (i + 1) * 2 * small] = part.astype(BF16)
    ring_pass(0, 0)
    for tap_w in range(3):
        ring_start(1, tap_w, 0)

    @pl.when(me > 0)
    def _():
        halos[0].wait_recv()

    @pl.when(me == 0)
    def _():
        frames_all[q, 0:2] = jnp.zeros((2,) + frames_ref.shape[1:], BF16)

    @pl.when(me < n - 1)
    def _():
        halos[1].wait_recv()
        halos[2].wait_recv()

    @pl.when(me == n - 1)
    def _():
        frames_all[q, count + 2 : count + 3] = jnp.zeros((1,) + frames_ref.shape[1:], BF16)
        cot_all[q, times : times + 3] = jnp.zeros((3,) + cot_ref.shape[1:], BF16)

    edges = (
        frames_all.at[q, 0:2], frames_all.at[q, count + 2 : count + 3],
        cot_all.at[q, times : times + 3],
    )
    crossing = [
        remote(ref, ref, col_send.at[4 + i], col_recv.at[4 + i], me, across)
        for i, ref in enumerate(edges)
    ]
    beside = [
        remote(ref, ref, col_send.at[7 + i], col_recv.at[7 + i], me, sibling)
        for i, ref in enumerate(edges)
    ]
    for copy in crossing + beside:
        copy.start()
    ring_pass(0, 1)
    ring_pass(1, 0)
    ring_pass(0, 2)
    ring_pass(1, 1)
    for copy in own[:2] + crossing:
        copy.wait_recv()
    passed = [
        remote(ref.at[across], ref.at[across], col_send.at[10 + i], col_recv.at[10 + i], me, sibling)
        for i, ref in enumerate((frames_all, cot_all))
    ]
    for copy in passed:
        copy.start()
    for copy in own[2:] + beside + passed:
        copy.wait_recv()

    @pl.loop(0, count + 3)
    def _(t):
        at = pl.ds(pl.multiple_of(t * width, width), width)
        for r in range(2):
            line = jnp.concatenate([frames_all[c, t, r].astype(F32) for c in range(4)], axis=0)
            for kw in range(3):
                inputs[kw, at, r * in_channels : (r + 1) * in_channels] = shifted(
                    line, kw - 1
                ).astype(BF16)

    @pl.loop(0, times + 3)
    def _(t):
        at = pl.ds(pl.multiple_of(t * width, width), width)
        for r in range(2):
            line = jnp.concatenate([cot_all[c, t, r].astype(F32) for c in range(4)], axis=0)
            cots[at, r * channels : (r + 1) * channels] = line.astype(BF16)

    pair = 2 * small
    ring_pass(1, 2, (0,))
    for kw in range(3):
        ring_got(0, kw, 3)

    def frame(t):
        return pl.ds(pl.multiple_of(t * width, width), width)

    raw[...] = jnp.zeros_like(raw)

    @pl.loop(0, 3)
    def _(kw):
        for kt in range(3):
            for kh in range(3):
                part = up_all[
                    kw, :, kt * 8 : kt * 8 + 8, kh * in_channels : (kh + 1) * in_channels
                ].astype(F32)
                part = part.reshape(small, in_channels).astype(BF16)
                for r in range(2):
                    r_in = r + kh - 1
                    if 0 <= r_in < 2:
                        up_taps[
                            kw, kt * pair + r * small : kt * pair + (r + 1) * small,
                            r_in * in_channels : (r_in + 1) * in_channels,
                        ] = part
        raw[...] += lax.dot_general(
            inputs[kw], up_taps[kw], (((1,), (1,)), ((), ())), preferred_element_type=F32
        )

    def keep(t, value):
        before[frame(t)] = value
        active = (value / (1.0 + jnp.exp(-value))).astype(BF16).astype(F32)
        for kw in range(3):
            moved = shifted(active, kw - 1).astype(BF16)
            for kt in range(3):
                patches[kw, frame(t - kt + 2), kt * pair : (kt + 1) * pair] = moved

    @pl.loop(0, count + 2)
    def _(i):
        keep(2 * i, raw[frame(i + 1), 0:pair] + raw[frame(i), 2 * pair : 3 * pair])

    @pl.loop(0, count + 1)
    def _(i):
        keep(2 * i + 1, raw[frame(i + 1), pair : 2 * pair])

    def exchange(i, part, got):
        return [
            remote(part.at[target], got.at[j], out_send.at[i + j], out_recv.at[i + j], me, sibling)
            for j, target in enumerate((sibling, diagonal))
        ]

    out_d = exchange(0, part_d, got_d)
    lane = lax.broadcasted_iota(jnp.int32, (channels, pair), 1)
    def add_and_cross(i, part, got, sums, last, first_copies):
        for copy in first_copies:
            copy.wait_recv()
        sums[...] = (part[across].astype(F32) + got[1].astype(F32)).astype(BF16)
        copy = remote(sums, last, out_send.at[i + 2], out_recv.at[i + 2], me, across)
        copy.start()
        return copy

    def finish(part, got, last, copy, out):
        copy.wait_recv()
        out[...] = (part[q].astype(F32) + got[0].astype(F32) + last[...].astype(F32)).astype(BF16)

    def decode(kw):
        ring_got(1, kw, 2, (1,))
        ring_got(1, kw, 3)
        last = mix_all[kw, :, 3 * pair : 4 * pair].astype(F32)
        final = mix_all[kw - kw % 2, :, 4 * pair : 5 * pair].astype(F32)
        if kw == 1:
            final = pltpu.roll(final, small, 1)
        tails = [last, pltpu.roll(last, small, 1), final]
        for kt in range(3):
            block = mix_all[kw, :, kt * pair : (kt + 1) * pair]
            turned = pltpu.roll(block.astype(F32), small, 1)
            mix_taps[kw, channels : 2 * channels, kt * pair : (kt + 1) * pair] = block
            mix_taps[kw, 0:channels, kt * pair : (kt + 1) * pair] = jnp.where(
                lane < small, turned, tails[kt]
            ).astype(BF16)
        term = lax.dot_general(
            patches[kw, 2 * width : (times + 2) * width], mix_taps[kw],
            (((1,), (1,)), ((), ())), preferred_element_type=F32,
        )
        decoding[...] = term if kw == 0 else decoding[...] + term

    def back(kw):
        spread[...] = jnp.dot(cots[...], mix_taps[kw], preferred_element_type=F32)

        @pl.loop(0, times + 1)
        def _(t):
            part = None
            for kt in range(3):
                piece = spread[frame(t + 2 - kt), kt * pair : (kt + 1) * pair]
                part = piece if part is None else part + piece
            part = shifted(part, 1 - kw)
            gradient[frame(t)] = part if kw == 0 else gradient[frame(t)] + part

    decode(0)
    back(0)
    decode(1)
    decode(2)

    @pl.loop(0, times)
    def _(t):
        for r in range(2):
            for c in range(4):
                at = pl.ds(pl.multiple_of(t * width + c * cols, cols), cols)
                part_d[c, t, r] = decoding[at, r * channels : (r + 1) * channels].astype(BF16)

    for copy in out_d:
        copy.start()
    back(1)
    cross_d = add_and_cross(0, part_d, got_d, sum_d, last_d, out_d)
    back(2)

    @pl.loop(0, times + 1)
    def _(t):
        value = before[frame(t + 2)]
        sigma = 1.0 / (1.0 + jnp.exp(-value))
        line = gradient[frame(t)] * sigma * (1.0 + value * (1.0 - sigma))
        gradient[frame(t)] = line.astype(BF16).astype(F32)

    @pl.loop(0, count)
    def _(i):
        for kt in range(3):
            line = gradient[frame(2 * i + kt)]
            for kw in range(3):
                grads[kw, frame(i), kt * pair : (kt + 1) * pair] = shifted(line, 1 - kw).astype(BF16)

    out_g = []
    for r in range(2):
        summed[...] = jnp.zeros_like(summed)

        @pl.loop(0, 3)
        def _(kw):
            summed[...] += jnp.dot(
                grads[kw], up_taps[kw, :, r * in_channels : (r + 1) * in_channels],
                preferred_element_type=F32,
            )

        @pl.loop(0, count)
        def _(i):
            for c in range(4):
                at = pl.ds(pl.multiple_of(i * width + c * cols, cols), cols)
                part_g[r, c, i] = summed[at].astype(BF16)

        out_g.append(exchange(3 + 3 * r, part_g.at[r], got_g.at[r]))
        for copy in out_g[r]:
            copy.start()
    cross_g = [
        add_and_cross(
            3 + 3 * r, part_g.at[r], got_g.at[r], sum_g.at[r], last_g.at[r], out_g[r]
        )
        for r in range(2)
    ]
    finish(part_d, got_d, last_d, cross_d, decoded_ref)
    for r in range(2):
        finish(part_g.at[r], got_g.at[r], last_g.at[r], cross_g[r], grad_ref.at[:, r])

    @pl.when(me < n - 1)
    def _():
        halos[0].wait_send()

    @pl.when(me > 0)
    def _():
        halos[1].wait_send()
        halos[2].wait_send()

    for copy in list(copies.values()) + own + crossing + beside + passed:
        copy.wait_send()
    for copy in out_d + out_g[0] + out_g[1] + [cross_d] + cross_g:
        copy.wait_send()


def place(made_d, made_g, decoded_ref, grad_ref):
    decoded_ref[...] = made_d[...]
    grad_ref[...] = made_g[...]


def fused(frames, up_kernel, mix_kernel, cotangent):
    n = lax.axis_size("tm")
    count, height, cols, in_channels = frames.shape
    times, channels = cotangent.shape[0], cotangent.shape[3]
    width, small = 4 * cols, channels // 4
    up_rows, mix_rows = up_kernel.T, mix_kernel.T
    whole = pl.BlockSpec(memory_space=pltpu.VMEM)
    d_block, g_block = (times, height, cols, channels), (count, height, cols, in_channels)
    g_half = (count, cols, in_channels)
    dma = pltpu.SemaphoreType.DMA
    made = pl.pallas_call(
        functools.partial(fused_kernel, n),
        out_shape=(
            jax.ShapeDtypeStruct(d_block, BF16),
            jax.ShapeDtypeStruct(g_block, BF16),
        ),
        in_specs=[whole] * 4,
        out_specs=(whole, whole),
        scratch_shapes=[
            pltpu.VMEM((3, n, 24, 3 * in_channels), BF16),
            pltpu.VMEM((3, channels, 10 * small), BF16),
            pltpu.VMEM((4, count + 3, height, cols, in_channels), BF16),
            pltpu.VMEM((4, times + 3, height, cols, channels), BF16),
            pltpu.VMEM((3, 6 * small, 2 * in_channels), BF16),
            pltpu.VMEM((3, (count + 3) * width, 2 * in_channels), BF16),
            pltpu.VMEM((3, 2 * channels, 6 * small), BF16),
            pltpu.VMEM(((count + 3) * width, 6 * small), F32),
            pltpu.VMEM(((times + 3) * width, 2 * small), F32),
            pltpu.VMEM((3, (times + 5) * width, 6 * small), BF16),
            pltpu.VMEM((times * width, 2 * channels), F32),
            pltpu.VMEM(((times + 3) * width, 2 * channels), BF16),
            pltpu.VMEM(((times + 3) * width, 6 * small), F32),
            pltpu.VMEM(((times + 1) * width, 2 * small), F32),
            pltpu.VMEM((3, count * width, 6 * small), BF16),
            pltpu.VMEM((count * width, in_channels), F32),
            pltpu.VMEM((4,) + d_block, BF16),
            pltpu.VMEM((2, 4) + g_half, BF16),
            pltpu.VMEM((2,) + d_block, BF16),
            pltpu.VMEM((2, 2) + g_half, BF16),
            pltpu.VMEM(d_block, BF16),
            pltpu.VMEM((2,) + g_half, BF16),
            pltpu.VMEM(d_block, BF16),
            pltpu.VMEM((2,) + g_half, BF16),
            dma((2, 2, 3, n // 2)),
            dma((2, 2, 3, n // 2)),
            dma((3,)),
            dma((3,)),
            dma((12,)),
            dma((12,)),
            dma((9,)),
            dma((9,)),
        ],
        compiler_params=pltpu.CompilerParams(
            collective_id=0, has_side_effects=True, vmem_limit_bytes=56 * 1024 * 1024
        ),
    )(up_rows, mix_rows, frames, cotangent)
    return pl.pallas_call(
        place,
        out_shape=tuple(jax.ShapeDtypeStruct(array.shape, array.dtype) for array in made),
        in_specs=[whole] * 2,
        out_specs=(whole, whole),
    )(*made)


def solution(mesh):
    placed = (P("tm", None, "col", None), P(None, "tm"), P(None, "tm"), P("tm", None, "col", None))
    small = mesh.shape["tm"] == 8 and mesh.shape["col"] == 4
    return jax.shard_map(
        fused if small else shards,
        mesh=mesh,
        in_specs=placed,
        out_specs=(P("tm", None, "col", None), P("tm", None, "col", None)),
        check_vma=False,
    )
```
